32 devices in a mesh: dp: 16 (over z, y, x), tp: 2 (over core).
Axes of the slice: x: 2, y: 2, z: 4, core: 2. Of those that a mesh axis runs over, the one named last changes fastest.
Arguments:
- images: float32 [192, 197, 384], P('dp'), may hold values from -6 to 6
- image_count: int32 [16], P('dp'), may hold values from 3 to 12, as said below
- cotangent: float32 [192, 197, 384], P('dp'), may hold values from -6 to 6
- w_query: float32 [384, 384], P('dp', 'tp'), may hold values from -0.3125 to 0.3125
- w_key: float32 [384, 384], P('dp', 'tp'), may hold values from -0.3125 to 0.3125
- w_value: float32 [384, 384], P('dp', 'tp'), may hold values from -0.3125 to 0.3125
- w_out: float32 [384, 384], P('tp', 'dp'), may hold values from -2 to 2
- w_up: float32 [384, 1536], P('dp', 'tp'), may hold values from -0.3125 to 0.3125
- w_down: float32 [1536, 384], P('tp', 'dp'), may hold values from -0.15625 to 0.15625
- vectors: float32 [4608], P(('dp', 'tp')), may hold values from -0.9 to 1.4
- mom_query: float32 [384, 384], P('dp', 'tp'), may hold values from -320 to 320
- mom_key: float32 [384, 384], P('dp', 'tp'), may hold values from -320 to 320
- mom_value: float32 [384, 384], P('dp', 'tp'), may hold values from -320 to 320
- mom_out: float32 [384, 384], P('tp', 'dp'), may hold values from -320 to 320
- mom_up: float32 [384, 1536], P('dp', 'tp'), may hold values from -320 to 320
- mom_down: float32 [1536, 384], P('tp', 'dp'), may hold values from -320 to 320
- adam_first: float32 [4608], P(('dp', 'tp')), may hold values from -96 to 96
- adam_second: float32 [4608], P(('dp', 'tp')), may hold values from 7.5648 to 75.648
Outputs:
- block_out: float32 [192, 197, 384], P('dp')
- input_grad: float32 [192, 197, 384], P('dp')
- grad_query: float32 [384, 384], P('dp', 'tp')
- grad_key: float32 [384, 384], P('dp', 'tp')
- grad_value: float32 [384, 384], P('dp', 'tp')
- grad_out: float32 [384, 384], P('tp', 'dp')
- grad_up: float32 [384, 1536], P('dp', 'tp')
- grad_down: float32 [1536, 384], P('tp', 'dp')
- grad_vectors: float32 [4608], P(('dp', 'tp'))
- new_mom_query: float32 [384, 384], P('dp', 'tp')
- new_mom_key: float32 [384, 384], P('dp', 'tp')
- new_mom_value: float32 [384, 384], P('dp', 'tp')
- new_mom_out: float32 [384, 384], P('tp', 'dp')
- new_mom_up: float32 [384, 1536], P('dp', 'tp')
- new_mom_down: float32 [1536, 384], P('tp', 'dp')
- step_query: float32 [384, 384], P('dp', 'tp')
- step_key: float32 [384, 384], P('dp', 'tp')
- step_value: float32 [384, 384], P('dp', 'tp')
- step_out: float32 [384, 384], P('tp', 'dp')
- step_up: float32 [384, 1536], P('dp', 'tp')
- step_down: float32 [1536, 384], P('tp', 'dp')
- first_new: float32 [4608], P(('dp', 'tp'))
- second_new: float32 [4608], P(('dp', 'tp'))
- vector_update: float32 [4608], P(('dp', 'tp'))
The draws below stay inside these ranges and needn't reach their ends.
Inputs may be any that keep to these rules, and one draw needn't show every extreme that they name: `image_count`: each index of dp holds between max(1, 12 div 4) and 12 live images; some index holds 12 and some the least.
All inputs are finite; a program needn't handle non-finite values.
Results may differ from the reference program's by a relative error of at most 0.0003.
Values sent between devices are 32-bit elements; how exact they have to be, the bound alone decides.
No kernel may reach another device: no remote copies, remote signals or barrier semaphores. Data moves between devices by JAX's collectives and lax.ppermute only.
A program may use at most 256 MiB of HBM per device.

```python
import math
import jax
import jax.numpy as jnp
from jax import lax

D = 384
HEADS = 6
HEAD_DIM = 64
FF = 1536
SEQ = 197
CAP = 12
NS_STEPS = 5
STEP = 10
IMAGES = 192
VEC = 4608
N_DP = 16


def draw_image_count(key, part):
    first_key, second_key, third_key = jax.random.split(jax.random.fold_in(key, 11), 3)
    least = max(1, CAP // 4)
    spread = CAP - least + 1
    first_draw = jax.random.randint(first_key, (N_DP,), 0, spread)
    second_draw = jax.random.randint(second_key, (N_DP,), 0, spread)
    counts = least + jnp.minimum(first_draw, second_draw)
    order = jax.random.permutation(third_key, N_DP)
    counts = counts.at[order[0]].set(CAP).at[order[1]].set(least)
    return counts.astype(jnp.int32)


def draw_vectors(key, part):
    gain_key, shift_key = jax.random.split(jax.random.fold_in(key, 23))
    position = jnp.arange(VEC)
    gains = jax.random.uniform(gain_key, (VEC,), jnp.float32, 0.6, 1.4)
    shifts = 0.3 * jnp.clip(jax.random.normal(shift_key, (VEC,), jnp.float32), -3.0, 3.0)
    return jnp.where(position < 2 * D, gains, shifts).astype(jnp.float32)


def levels(stream_key, shape, cuts, smallest, high):
    loudness = 1.0
    for dim, parts in cuts:
        heights = jax.random.uniform(jax.random.fold_in(jax.random.fold_in(stream_key, 6), dim), (parts,), jnp.float32, smallest / len(cuts), high / len(cuts))
        loudness = loudness * jnp.repeat(jnp.exp(heights), shape[dim] // parts).reshape((-1,) + (1,) * (len(shape) - 1 - dim))
    return loudness


def centred(own_key, dims, deviation, reach, cuts=(), kind=jnp.bfloat16):
    factor_of = levels(own_key, dims, cuts, -0.22, 0.18) if cuts else 1.0
    values = jax.random.normal(own_key, dims, jnp.float32) * deviation * factor_of
    return jnp.minimum(jnp.maximum(values, -reach), reach).astype(kind)


def setup_inputs(seed: int = 0) -> dict:
    key_list = jax.random.split(jax.random.key(seed), 19)
    images = centred(key_list[0], (IMAGES, SEQ, D), 1.0, 6.0, ((0, 16),), jnp.float32)
    image_count = draw_image_count(jax.random.fold_in(key_list[18], 71), 0)
    cotangent = centred(key_list[2], (IMAGES, SEQ, D), 1.0, 6.0, ((0, 16),), jnp.float32)
    w_query = centred(key_list[3], (D, D), D ** -0.5, 0.3125, ((0, 16), (1, 2)), jnp.float32)
    w_key = centred(key_list[4], (D, D), D ** -0.5, 0.3125, ((0, 16), (1, 2)), jnp.float32)
    w_value = centred(key_list[5], (D, D), D ** -0.5, 0.3125, ((0, 16), (1, 2)), jnp.float32)
    w_out = centred(key_list[6], (D, D), (max(1, D // 48)) ** -0.5, 2.0, ((0, 2), (1, 16)), jnp.float32)
    w_up = centred(key_list[7], (D, FF), D ** -0.5, 0.3125, ((0, 16), (1, 2)), jnp.float32)
    w_down = centred(key_list[8], (FF, D), FF ** -0.5, 0.15625, ((0, 2), (1, 16)), jnp.float32)
    vectors = draw_vectors(jax.random.fold_in(key_list[18], 71), 0)
    mom_query = centred(key_list[10], (D, D), (0.3 * (IMAGES * SEQ) ** 0.5), 320.0, ((0, 16), (1, 2)), jnp.float32)
    mom_key = centred(key_list[11], (D, D), (0.3 * (IMAGES * SEQ) ** 0.5), 320.0, ((0, 16), (1, 2)), jnp.float32)
    mom_value = centred(key_list[12], (D, D), (0.3 * (IMAGES * SEQ) ** 0.5), 320.0, ((0, 16), (1, 2)), jnp.float32)
    mom_out = centred(key_list[13], (D, D), (0.3 * (IMAGES * SEQ) ** 0.5), 320.0, ((0, 2), (1, 16)), jnp.float32)
    mom_up = centred(key_list[14], (D, FF), (0.3 * (IMAGES * SEQ) ** 0.5), 320.0, ((0, 16), (1, 2)), jnp.float32)
    mom_down = centred(key_list[15], (FF, D), (0.3 * (IMAGES * SEQ) ** 0.5), 320.0, ((0, 2), (1, 16)), jnp.float32)
    adam_first = centred(key_list[16], (VEC,), (0.08 * (IMAGES * SEQ) ** 0.5), 96.0, ((0, 32),), jnp.float32)
    adam_second = jnp.clip(jnp.exp(math.log(75.648) - 2.3025852 * jax.random.uniform(key_list[17], (VEC,), jnp.float32) ** levels(key_list[17], (VEC,), ((0, 32),), -0.2, 0.2)), 7.5648, 75.648)
    return {"images": images, "image_count": image_count, "cotangent": cotangent, "w_query": w_query, "w_key": w_key, "w_value": w_value, "w_out": w_out, "w_up": w_up, "w_down": w_down, "vectors": vectors, "mom_query": mom_query, "mom_key": mom_key, "mom_value": mom_value, "mom_out": mom_out, "mom_up": mom_up, "mom_down": mom_down, "adam_first": adam_first, "adam_second": adam_second}


highest = lax.Precision.HIGHEST
norm_eps = 1e-06
ns_first = 3.4445
ns_second = -4.775
ns_third = 2.0315
momentum_decay = 0.95
matrix_rate = 1.0
adam_beta_one = 0.9
adam_beta_two = 0.999
adam_rate = 0.05
adam_decay = 0.05
adam_eps = 1e-08

@jax.custom_vjp
def low(v):
    return lax.optimization_barrier(v.astype(jnp.bfloat16)).astype(jnp.float32)

@jax.custom_vjp
def low_back(v):
    return v

def low_keep(v):
    return (low(v), None)

def low_pass(kept, grad):
    return (grad,)

def back_keep(v):
    return (v, None)

def back_low(kept, grad):
    return (low(grad),)
low.defvjp(low_keep, low_pass)
low_back.defvjp(back_keep, back_low)

def layer_norm(inputs, gain, shift):
    centre = lax.optimization_barrier(jnp.mean(inputs, axis=-1, keepdims=True))
    offset = inputs - centre
    spread = lax.optimization_barrier(jnp.mean(offset * offset, axis=-1, keepdims=True))
    return offset * lax.rsqrt(spread + norm_eps) * gain + shift

def matmul(left, right):
    return jnp.dot(left, right, precision=highest, preferred_element_type=jnp.float32)

def unpack(vectors):
    pieces = [vectors[position * D:(position + 1) * D] for position in range(8)]
    return pieces + [vectors[8 * D:]]

def forward(weights, vectors, group_in):
    w_query, w_key, w_value, w_out, w_up, w_down = weights
    gain_one, gain_two, shift_one, shift_two, query_bias, value_bias, out_bias, down_bias, up_bias = unpack(vectors)
    image_here = group_in.shape[0]
    tokens = group_in.reshape(image_here * SEQ, D)
    normed = layer_norm(tokens, gain_one, shift_one)
    queries = (matmul(normed, w_query) + query_bias).reshape(image_here, SEQ, HEADS, HEAD_DIM)
    key_rows = matmul(normed, w_key).reshape(image_here, SEQ, HEADS, HEAD_DIM)
    values = (matmul(normed, w_value) + value_bias).reshape(image_here, SEQ, HEADS, HEAD_DIM)
    scores = jnp.einsum('bqhd,bkhd->bhqk', queries, key_rows, precision=highest) * HEAD_DIM ** (-0.5)
    attention_weights = jax.nn.softmax(scores, axis=-1)
    attended = jnp.einsum('bhqk,bkhd->bqhd', attention_weights, values, precision=highest).reshape(image_here * SEQ, D)
    hidden = tokens + matmul(attended, w_out) + out_bias
    second = layer_norm(hidden, gain_two, shift_two)
    activated = jax.nn.gelu(matmul(second, w_up) + up_bias, approximate=False)
    result = hidden + matmul(activated, w_down) + down_bias
    return result.reshape(image_here, SEQ, D)

def orthogonalize(matrix):
    row_count, col_count = matrix.shape
    current = matrix / (jnp.sqrt(jnp.sum(matrix * matrix)) + 1e-07)
    is_tall = row_count > col_count
    if is_tall:
        current = current.T
    for sweep_index in range(NS_STEPS):
        gram_matrix = matmul(current, current.T)
        mixing = ns_second * gram_matrix + ns_third * matmul(gram_matrix, gram_matrix)
        current = ns_first * current + matmul(mixing, current)
    if is_tall:
        current = current.T
    return current * math.sqrt(max(1.0, row_count / col_count))

def reference(images, image_count, cotangent, w_query, w_key, w_value, w_out, w_up, w_down, vectors, mom_query, mom_key, mom_value, mom_out, mom_up, mom_down, adam_first, adam_second):
    weights = (w_query, w_key, w_value, w_out, w_up, w_down)
    slot_ids = jnp.arange(IMAGES, dtype=jnp.int32)
    live_mask = (slot_ids % CAP < image_count[slot_ids // CAP]).astype(jnp.float32)
    groups = IMAGES // CAP
    block_in = images.reshape(groups, CAP, SEQ, D)
    block_cot = (cotangent * live_mask[:, None, None]).reshape(groups, CAP, SEQ, D)
    zero_grads = (jax.tree.map(jnp.zeros_like, weights), jnp.zeros_like(vectors))

    def one_group(grad_sum, inputs):
        group_in, group_cot = inputs
        result, pullback = jax.vjp(forward, weights, vectors, group_in)
        weight_part, vector_part, input_part = pullback(group_cot)
        grad_sum = (jax.tree.map(jnp.add, grad_sum[0], weight_part), grad_sum[1] + vector_part)
        return (grad_sum, (result, input_part))
    (weight_grads, grad_vectors), (outputs, input_parts) = lax.scan(one_group, zero_grads, (block_in, block_cot))
    live_block = live_mask.reshape(groups, CAP)[:, :, None, None]
    block_out = (outputs * live_block).reshape(IMAGES, SEQ, D)
    input_grad = input_parts.reshape(IMAGES, SEQ, D)
    momenta = (mom_query, mom_key, mom_value, mom_out, mom_up, mom_down)
    new_momenta = tuple((momentum_decay * previous + gradient for previous, gradient in zip(momenta, weight_grads)))
    updates = tuple((-matrix_rate * orthogonalize(moment) for moment in new_momenta))
    first_new = adam_beta_one * adam_first + (1.0 - adam_beta_one) * grad_vectors
    second_new = adam_beta_two * adam_second + (1.0 - adam_beta_two) * grad_vectors * grad_vectors
    first_hat = first_new / (1.0 - adam_beta_one ** STEP)
    second_hat = second_new / (1.0 - adam_beta_two ** STEP)
    vector_update = -adam_rate * (first_hat / (jnp.sqrt(second_hat) + adam_eps) + adam_decay * vectors)
    return (block_out, input_grad, weight_grads[0], weight_grads[1], weight_grads[2], weight_grads[3], weight_grads[4], weight_grads[5], grad_vectors, new_momenta[0], new_momenta[1], new_momenta[2], new_momenta[3], new_momenta[4], new_momenta[5], updates[0], updates[1], updates[2], updates[3], updates[4], updates[5], first_new, second_new, vector_update)
```

```python
import functools
import math

import jax
import jax.numpy as jnp
import numpy as np
from jax import lax
from jax.experimental import pallas as pl
from jax.experimental.pallas import tpu as pltpu
from jax.sharding import PartitionSpec as P

D = 384
HEADS = 6
HEAD_DIM = 64
FF = 1536
SEQ = 197
PAD = 208
GROUP = 2
NS_STEPS = 5
STEP = 10
HALF = D // 2
SLOTS = 4
VEC = 4608
UNITS = FF // 2

norm_eps = 1e-06
ns_first = 3.4445
ns_second = -4.775
ns_third = 2.0315
momentum_decay = 0.95
matrix_rate = 1.0
adam_beta_one = 0.9
adam_beta_two = 0.999
adam_rate = 0.05
adam_decay = 0.05
adam_eps = 1e-08
f32 = jnp.float32
bf16 = jnp.bfloat16
VMEM_BYTES = 60 * 2**20
ONCE = pl.Buffered(1)


def split(value):
    high = value.astype(bf16)
    return high, (value - high.astype(f32)).astype(bf16)


def dot_one(left, right, left_dim, right_dim):
    return lax.dot_general(
        left, right, (((left_dim,), (right_dim,)), ((), ())), preferred_element_type=f32
    )


def dot(left, right, left_dim, right_dim):
    left_high, left_low = left if isinstance(left, tuple) else split(left)
    right_high, right_low = right if isinstance(right, tuple) else split(right)
    return dot_one(left_high, right_high, left_dim, right_dim) + (
        dot_one(left_high, right_low, left_dim, right_dim)
        + dot_one(left_low, right_high, left_dim, right_dim)
    )


def nn(left, right):
    return dot(left, right, 1, 0)


def nt(left, right):
    return dot(left, right, 1, 1)


def tn(left, right):
    return dot(left, right, 0, 0)


def levels(dp_size):
    bits = dp_size.bit_length() - 1
    out = []
    shift = 0
    while bits:
        width = min(2, bits)
        out.append((shift, 1 << width))
        shift += width
        bits -= width
    return out[::-1]


def padded_rows(dp_size):
    return -(-(D // dp_size) // 8) * 8


def swap_dp(value, mask, dp_size):
    return lax.ppermute(value, "dp", [(i, i ^ mask) for i in range(dp_size)])


def swap_tp(value):
    return lax.ppermute(value, "tp", [(0, 1), (1, 0)])


def tie(first, second):
    return lax.optimization_barrier((first, second))


def exchange(block, level, dp_size):
    shift, size = level
    return [swap_dp(block, s << shift, dp_size) for s in range(1, size)]


def gather(block, groups, dp_size):
    for level in groups:
        block = jnp.concatenate([block] + exchange(block, level, dp_size), axis=0)
    return block


def place_of(value, groups):
    place = 0
    stride = 1
    for shift, size in groups:
        place = place + ((value >> shift) & (size - 1)) * stride
        stride *= size
    return place


def scatter_sum(value, groups, dp_size):
    for shift, size in groups[::-1]:
        value = value.reshape((size, -1) + value.shape[1:])
        total = value[0]
        for part in [swap_dp(value[s], s << shift, dp_size) for s in range(1, size)]:
            total = total + part
        value = total
    return value


def normalize(rows):
    centre = jnp.sum(rows, axis=-1, keepdims=True) * (1.0 / D)
    offset = rows - centre
    spread = jnp.sum(offset * offset, axis=-1, keepdims=True) * (1.0 / D)
    rate = lax.rsqrt(spread + norm_eps)
    return offset * rate, rate


def normalize_back(grad, unit, rate, gain):
    scaled = grad * gain
    mean_one = jnp.sum(scaled, axis=-1, keepdims=True) * (1.0 / D)
    mean_two = jnp.sum(scaled * unit, axis=-1, keepdims=True) * (1.0 / D)
    return rate * (scaled - mean_one - unit * mean_two)


def row_sum(value):
    return jnp.sum(value, axis=0, keepdims=True)


def head_lanes(head):
    base = (head // 3) * 3 * HALF + (head % 3) * HEAD_DIM
    return base, base + HALF, base + 2 * HALF


def relative(vec, is_first):
    half = vec.shape[1] // 2
    return jnp.where(is_first, vec, jnp.concatenate([vec[:, half:], vec[:, :half]], axis=1))


def attention_forward(dp_size, info, images, own, other, qkv_out, att_out, hid_out, wqkv_out, wo_out, vec_out, xs, wqkv, wo, att, vec):
    step = pl.program_id(0)
    rows = D // dp_size
    is_first = info[0] == 0

    @pl.when(step == 0)
    def _():
        xs[...] = jnp.zeros_like(xs)
        piece = VEC // (2 * dp_size)
        for j in range(dp_size):
            at = place_of(info[1] ^ j, levels(dp_size))
            mine = own[at]
            theirs = other[at]
            here = slice(j * rows, (j + 1) * rows)
            wqkv[here, : 3 * HALF] = mine[:, : 3 * HALF]
            wqkv[here, 3 * HALF :] = theirs[:, : 3 * HALF]
            wo[here, :HALF] = mine[:, 3 * HALF : 4 * HALF]
            wo[here, HALF:] = theirs[:, 3 * HALF : 4 * HALF]
            for line in range(-(-piece // 128)):
                size = min(128, piece - line * 128)
                one = mine[line : line + 1, 4 * HALF : 4 * HALF + size]
                two = theirs[line : line + 1, 4 * HALF : 4 * HALF + size]
                base = 2 * j * piece + line * 128
                vec[0:1, base : base + size] = jnp.where(is_first, one, two)
                vec[0:1, base + piece : base + piece + size] = jnp.where(is_first, two, one)

    xs[:, :SEQ, :] = images[...]
    tokens = xs[...].reshape(GROUP * PAD, D)
    unit, _ = normalize(tokens)
    normed = unit * vec[0:1, :D] + vec[0:1, 2 * D : 3 * D]
    bias_q = relative(vec[0:1, 4 * D : 5 * D], is_first)
    bias_v = relative(vec[0:1, 5 * D : 6 * D], is_first)
    zero = jnp.zeros((1, HALF), f32)
    bias = jnp.concatenate(
        [bias_q[:, :HALF], zero, bias_v[:, :HALF], bias_q[:, HALF:], zero, bias_v[:, HALF:]], axis=1
    )
    qkv = nn(normed, wqkv[...]) + bias
    qkv_out[...] = qkv.reshape(GROUP, PAD, 3 * D)
    column = lax.broadcasted_iota(jnp.int32, (PAD, PAD), 1)
    for image in range(GROUP):
        part = slice(image * PAD, (image + 1) * PAD)
        for head in range(HEADS):
            at_q, at_k, at_v = head_lanes(head)
            query = qkv_out[image, :, at_q : at_q + HEAD_DIM] * 0.125
            key = qkv_out[image, :, at_k : at_k + HEAD_DIM]
            value = qkv_out[image, :, at_v : at_v + HEAD_DIM]
            scores = jnp.where(column < SEQ, nt(query, key), -1e30)
            weights = jnp.exp(scores - jnp.max(scores, axis=-1, keepdims=True))
            total = jnp.sum(weights, axis=-1, keepdims=True)
            att[part, head * HEAD_DIM : (head + 1) * HEAD_DIM] = nn(weights, value) / total
    attended = att[...]
    att_out[...] = attended.reshape(GROUP, PAD, D)
    hidden = tokens + nt(attended, wo[...]) + vec[0:1, 6 * D : 7 * D]
    hid_out[...] = hidden.reshape(GROUP, PAD, D)

    @pl.when(step == pl.num_programs(0) - 1)
    def _():
        wqkv_out[...] = wqkv[...]
        wo_out[...] = wo[...]
        vec_out[...] = vec[...]


def mlp(dp_size, info, hid, att, cot, own, other, wo, vec, block_out, dh_out, datt_out, keep, send, gout_out, sums, wup, wdown, cs, gup, gdown, gout):
    step = pl.program_id(0)
    rows = D // dp_size

    @pl.when(step == 0)
    def _():
        cs[...] = jnp.zeros_like(cs)
        gup[...] = jnp.zeros_like(gup)
        gdown[...] = jnp.zeros_like(gdown)
        gout[...] = jnp.zeros_like(gout)
        sums[...] = jnp.zeros_like(sums)
        for j in range(dp_size):
            at = place_of(info[1] ^ j, levels(dp_size))
            here = slice(j * rows, (j + 1) * rows)
            wup[here, :UNITS] = own[at, :, :UNITS]
            wup[here, UNITS:] = other[at, :, :UNITS]
            wdown[here, :UNITS] = own[at, :, UNITS:]
            wdown[here, UNITS:] = other[at, :, UNITS:]

    first = (info[0] * pl.num_programs(0) + step) * GROUP
    lives = [jnp.where(first + image < info[2], 1.0, 0.0).astype(f32) for image in range(GROUP)]
    for image in range(GROUP):
        cs[image, :SEQ, :] = cot[image] * lives[image]
    hidden = hid[...].reshape(GROUP * PAD, D)
    unit, rate = normalize(hidden)
    gain = vec[0:1, D : 2 * D]
    second = unit * gain + vec[0:1, 3 * D : 4 * D]
    pre = nn(second, wup[...]) + relative(vec[0:1, 8 * D :], info[0] == 0)
    phi = 0.5 * (1.0 + lax.erf(pre * math.sqrt(0.5)))
    act = pre * phi
    slope = phi + pre * (jnp.exp(-0.5 * pre * pre) * (1.0 / math.sqrt(2.0 * math.pi)))
    result = hidden + nt(act, wdown[...]) + vec[0:1, 7 * D : 8 * D]
    for image in range(GROUP):
        block_out[image] = result[image * PAD : image * PAD + SEQ] * lives[image]
    dy = cs[...].reshape(GROUP * PAD, D)
    gdown[...] += tn(dy, act)
    dpre = nn(dy, wdown[...]) * slope
    gup[...] += tn(second, dpre)
    dsecond = nt(dpre, wup[...])
    dh = dy + normalize_back(dsecond, unit, rate, gain)
    dh_out[...] = dh.reshape(GROUP, PAD, D)
    attended = att[...].reshape(GROUP * PAD, D)
    gout[...] += tn(dh, attended)
    datt_out[...] = nn(dh, wo[...]).reshape(GROUP, PAD, D)
    sums[0:1, :] += row_sum(dpre)
    sums[1:2, :D] += row_sum(dsecond * unit)
    sums[2:3, :D] += row_sum(dsecond)
    sums[3:4, :D] += row_sum(dh)
    sums[4:5, :D] += row_sum(dy)

    @pl.when(step == pl.num_programs(0) - 1)
    def _():
        gout_out[...] = gout[...]
        pitch = padded_rows(dp_size)
        if pitch != rows:
            keep[...] = jnp.zeros_like(keep)
            send[...] = jnp.zeros_like(send)
        upper = levels(dp_size)[:-1]
        low_count = levels(dp_size)[-1][1]
        low = info[1] & (low_count - 1)
        for j in range(dp_size):
            at = place_of(info[1] ^ j, upper)
            here = slice(j * rows, (j + 1) * rows)
            block = j % low_count
            there = slice(block * pitch, block * pitch + rows)
            for slot in range(SLOTS):
                grad = gup if slot < 2 else gdown
                base = (slot % 2) * D
                keep[low ^ slot, at, there, :] = grad[here, base : base + D]
                send[low ^ slot, at, there, :] = grad[here, UNITS + base : UNITS + base + D]


def attention_backward(dp_size, last, groups, first, info, images, qkv, datt, dh, wqkv, vec, *rest):
    if last:
        sums_a, gout, grads_in, sums_in, grad_in, keep, send, xs, dqkv, grads, sums, flat = rest
    else:
        grad_in, grads_out, sums_out, xs, dqkv, grads, sums = rest
    step = pl.program_id(0)
    rows = D // dp_size

    @pl.when(step == 0)
    def _():
        xs[...] = jnp.zeros_like(xs)
        if last:
            grads[...] = grads_in[...]
            sums[...] = sums_in[...]
        else:
            grads[...] = jnp.zeros_like(grads)
            sums[...] = jnp.zeros_like(sums)

    xs[:, :SEQ, :] = images[...]
    tokens = xs[...].reshape(GROUP * PAD, D)
    unit, rate = normalize(tokens)
    gain = vec[0:1, :D]
    normed = unit * gain + vec[0:1, 2 * D : 3 * D]
    line = lax.broadcasted_iota(jnp.int32, (PAD, PAD), 0)
    for image in range(GROUP):
        part = slice(image * PAD, (image + 1) * PAD)
        for head in range(HEADS):
            at_q, at_k, at_v = head_lanes(head)
            query = qkv[image, :, at_q : at_q + HEAD_DIM] * 0.125
            key = qkv[image, :, at_k : at_k + HEAD_DIM]
            value = qkv[image, :, at_v : at_v + HEAD_DIM]
            grad_o = datt[image, :, head * HEAD_DIM : (head + 1) * HEAD_DIM]
            scores = jnp.where(line < SEQ, nt(key, query), -1e30)
            weights = jnp.exp(scores - jnp.max(scores, axis=0, keepdims=True))
            weights = weights / jnp.sum(weights, axis=0, keepdims=True)
            dweights = nt(value, grad_o)
            delta = jnp.sum(weights * dweights, axis=0, keepdims=True)
            dscores = weights * (dweights - delta)
            dqkv[part, at_v : at_v + HEAD_DIM] = nn(weights, grad_o)
            dqkv[part, at_k : at_k + HEAD_DIM] = nn(dscores, query)
            dqkv[part, at_q : at_q + HEAD_DIM] = tn(dscores, key) * 0.125
    dall = dqkv[...]
    grads[...] += tn(normed, dall)
    dnormed = nt(dall, wqkv[...])
    dx = dh[...].reshape(GROUP * PAD, D) + normalize_back(dnormed, unit, rate, gain)
    for image in range(GROUP):
        grad_in[image] = dx[image * PAD : image * PAD + SEQ]
    sums[0:1, :] += row_sum(dall)
    sums[1:2, :D] += row_sum(dnormed * unit)
    sums[2:3, :D] += row_sum(dnormed)

    @pl.when(step == pl.num_programs(0) - 1)
    def _():
        if not last:
            grads_out[...] = grads[...]
            sums_out[...] = sums[...]
            return
        is_first = info[0] == 0
        total = sums[0:1, :]
        query_sum = jnp.concatenate([total[:, :HALF], total[:, 3 * HALF : 4 * HALF]], axis=1)
        value_sum = jnp.concatenate([total[:, 2 * HALF : 3 * HALF], total[:, 5 * HALF :]], axis=1)
        flat[0:1, :D] = sums[1:2, :D]
        flat[0:1, D : 2 * D] = sums_a[1:2, :D]
        flat[0:1, 2 * D : 3 * D] = sums[2:3, :D]
        flat[0:1, 3 * D : 4 * D] = sums_a[2:3, :D]
        flat[0:1, 4 * D : 5 * D] = relative(query_sum, is_first)
        flat[0:1, 5 * D : 6 * D] = relative(value_sum, is_first)
        flat[0:1, 6 * D : 7 * D] = sums_a[3:4, :D]
        flat[0:1, 7 * D : 8 * D] = sums_a[4:5, :D]
        flat[0:1, 8 * D :] = relative(sums_a[0:1, :], is_first)
        pitch = padded_rows(dp_size)
        keep[...] = jnp.zeros_like(keep)
        send[...] = jnp.zeros_like(send)
        upper = levels(dp_size)[:-1]
        low_count = levels(dp_size)[-1][1]
        low = info[1] & (low_count - 1)
        piece = VEC // (2 * dp_size)
        for j in range(dp_size):
            at = place_of(info[1] ^ j, upper)
            here = slice(j * rows, (j + 1) * rows)
            block = j % low_count
            one = flat[0:1, 2 * j * piece : (2 * j + 1) * piece]
            two = flat[0:1, (2 * j + 1) * piece : (2 * j + 2) * piece]
            keep[low ^ block, at, 2 * pitch : 2 * pitch + 1, :piece] = jnp.where(is_first, one, two)
            send[low ^ block, at, 2 * pitch : 2 * pitch + 1, :piece] = jnp.where(is_first, two, one)
            for slot in range(SLOTS):
                place = block ^ slot
                there = slice((place % 2) * pitch, (place % 2) * pitch + rows)
                lanes = slice((place // 2) * HALF, (place // 2 + 1) * HALF)
                if slot < 3:
                    mine = grads[here, slot * HALF : (slot + 1) * HALF]
                    theirs = grads[here, (slot + 3) * HALF : (slot + 4) * HALF]
                else:
                    mine = gout[here, :HALF]
                    theirs = gout[here, HALF:]
                keep[low ^ slot, at, there, lanes] = mine
                send[low ^ slot, at, there, lanes] = theirs


def params():
    return pltpu.CompilerParams(vmem_limit_bytes=VMEM_BYTES, dimension_semantics=("arbitrary",))


def whole(shape):
    return pl.BlockSpec(shape, lambda g, info: (0,) * len(shape), pipeline_mode=ONCE)


def per_group(shape, first=0):
    return pl.BlockSpec((GROUP,) + shape, lambda g, info: (first + g,) + (0,) * len(shape))


def half_images(groups, first=0):
    return pl.BlockSpec((GROUP, SEQ, D), lambda g, info: (info[0] * groups + first + g, 0, 0))


def shaped(*shape):
    return jax.ShapeDtypeStruct(shape, f32)


def call(kernel, groups, in_specs, out_specs, out_shape, scratch, cost):
    return pl.pallas_call(
        kernel,
        grid_spec=pltpu.PrefetchScalarGridSpec(
            num_scalar_prefetch=1,
            grid=(groups,),
            in_specs=in_specs,
            out_specs=out_specs,
            scratch_shapes=[pltpu.VMEM(s, f32) for s in scratch],
        ),
        out_shape=out_shape,
        compiler_params=params(),
        cost_estimate=pl.CostEstimate(flops=cost, bytes_accessed=20 * 2**20, transcendentals=0),
    )


def polynomial(gram):
    pair = split(gram)
    return ns_second * gram + ns_third * nn(pair, pair)


def eye(size):
    line = lax.broadcasted_iota(jnp.int32, (size, size), 0)
    column = lax.broadcasted_iota(jnp.int32, (size, size), 1)
    return jnp.where(line == column, 1.0, 0.0).astype(f32)


def norm_scale(total):
    return 1.0 / (jnp.sqrt(jnp.full((1, 1), total, f32)) + 1e-07)


def gram_part(block, out):
    pair = split(block[...])
    out[...] = nt(pair, pair)


def newton(info, gram_ref, block, own, other, wide_out, small_out):
    gram = gram_ref[...]
    ident = eye(gram.shape[0])
    scale = norm_scale(jnp.sum(gram * ident))
    gram = gram * (scale * scale)
    total = None
    half = own.shape[0]
    mine = jnp.concatenate([own[:, :HALF], own[:, HALF:]], axis=0)
    theirs = jnp.concatenate([other[:, :HALF], other[:, HALF:]], axis=0)
    shrink = norm_scale(jnp.sum(mine * mine) + jnp.sum(theirs * theirs))
    mine = mine * shrink
    theirs = theirs * shrink
    for sweep in range(NS_STEPS):
        mine_pair = split(mine)
        theirs_pair = split(theirs)
        square = nt(mine_pair, mine_pair) + nt(theirs_pair, theirs_pair)
        mixing = polynomial(gram) + ns_first * ident
        square_mixing = split(polynomial(square))
        pair = split(mixing)
        total = mixing if total is None else nn(pair, total)
        mine = ns_first * mine + nn(square_mixing, mine_pair)
        if sweep < NS_STEPS - 1:
            theirs = ns_first * theirs + nn(square_mixing, theirs_pair)
            gram = nn(nn(gram, pair), pair)
    factor = jnp.where(info[3] >= 2, -2.0, -1.0).astype(f32) * matrix_rate
    wide_out[...] = nn(total[: wide_out.shape[0]], block[...]) * (scale * factor)
    rows = small_out.shape[0]
    small_out[:, :HALF] = mine[:rows] * (-matrix_rate)
    small_out[:, HALF:] = mine[half : half + rows] * (-matrix_rate)


def plain(kernel, operands, out_shape, cost):
    return pl.pallas_call(
        kernel,
        in_specs=[
            pl.BlockSpec(memory_space=pltpu.SMEM if x.ndim == 1 else pltpu.VMEM) for x in operands
        ],
        out_specs=jax.tree.map(lambda _: pl.BlockSpec(memory_space=pltpu.VMEM), out_shape),
        out_shape=out_shape,
        compiler_params=pltpu.CompilerParams(vmem_limit_bytes=VMEM_BYTES),
        cost_estimate=pl.CostEstimate(flops=cost, bytes_accessed=5 * 2**20, transcendentals=0),
    )(*operands)


def pick(stack, index):
    return lax.dynamic_index_in_dim(stack, index, 0, keepdims=False)


def body(
    images,
    image_count,
    cotangent,
    w_query,
    w_key,
    w_value,
    w_out,
    w_up,
    w_down,
    vectors,
    mom_query,
    mom_key,
    mom_value,
    mom_out,
    mom_up,
    mom_down,
    adam_first,
    adam_second,
):
    tp_index = lax.axis_index("tp")
    dp_index = lax.axis_index("dp")
    dp_size = lax.axis_size("dp")
    rows = D // dp_size
    pitch = padded_rows(dp_size)
    piece = vectors.shape[0]
    groups = images.shape[0] // (2 * GROUP)
    slots = groups * GROUP
    is_first = tp_index == 0
    every = levels(dp_size)
    upper, plane = every[:-1], every[-1]
    above = dp_size // plane[1]
    low = dp_index & (plane[1] - 1)
    info = jnp.stack([tp_index, dp_index, image_count[0], low]).astype(jnp.int32)

    vec_tail = jnp.pad(vectors, (0, rows * 128 - piece)).reshape(rows, 128)
    shard_one = jnp.concatenate([w_query, w_key, w_value, w_out.T, vec_tail], axis=1)
    shard_two = jnp.concatenate([w_up, w_down.T], axis=1)
    part_one = gather(shard_one[None], upper, dp_size)
    part_two = gather(shard_two[None], upper, dp_size)
    own_one = gather(part_one, [plane], dp_size)
    other_one = swap_tp(own_one)
    got_two = exchange(part_two, plane, dp_size)

    qkv, att, hid, wqkv, wo, vec = call(
        functools.partial(attention_forward, dp_size),
        groups,
        [
            half_images(groups),
            whole((dp_size, rows, 4 * HALF + 128)),
            whole((dp_size, rows, 4 * HALF + 128)),
        ],
        [
            per_group((PAD, 3 * D)),
            per_group((PAD, D)),
            per_group((PAD, D)),
            whole((D, 3 * D)),
            whole((D, D)),
            whole((1, VEC)),
        ],
        [
            shaped(slots, PAD, 3 * D),
            shaped(slots, PAD, D),
            shaped(slots, PAD, D),
            shaped(D, 3 * D),
            shaped(D, D),
            shaped(1, VEC),
        ],
        [(GROUP, PAD, D), (D, 3 * D), (D, D), (GROUP * PAD, D), (1, VEC)],
        16 * 10**9,
    )(info, images, own_one, other_one)

    got_two, hid = tie(got_two, hid)
    own_two = jnp.concatenate([part_two] + got_two, axis=0)
    other_two = swap_tp(own_two)

    block_own, dh, datt, keep_a, send_a, gout, sums_a = call(
        functools.partial(mlp, dp_size),
        groups,
        [
            per_group((PAD, D)),
            per_group((PAD, D)),
            half_images(groups),
            whole((dp_size, rows, 2 * UNITS)),
            whole((dp_size, rows, 2 * UNITS)),
            whole((D, D)),
            whole((1, VEC)),
        ],
        [
            per_group((SEQ, D)),
            per_group((PAD, D)),
            per_group((PAD, D)),
            whole((SLOTS, above, SLOTS * pitch, D)),
            whole((SLOTS, above, SLOTS * pitch, D)),
            whole((D, D)),
            whole((8, FF)),
        ],
        [
            shaped(slots, SEQ, D),
            shaped(slots, PAD, D),
            shaped(slots, PAD, D),
            shaped(SLOTS, above, SLOTS * pitch, D),
            shaped(SLOTS, above, SLOTS * pitch, D),
            shaped(D, D),
            shaped(8, FF),
        ],
        [(D, FF), (D, FF), (GROUP, PAD, D), (D, FF), (D, FF), (D, D)],
        48 * 10**9,
    )(info, hid, att, cotangent, own_two, other_two, wo, vec)

    got_a = swap_tp(send_a)

    def backward(last, first, count, operands, extra_in, extra_out_specs, extra_out, extra_scratch):
        return call(
            functools.partial(attention_backward, dp_size, last, groups, first),
            count,
            [
                half_images(groups, first),
                per_group((PAD, 3 * D), first),
                per_group((PAD, D), first),
                per_group((PAD, D), first),
                whole((D, 3 * D)),
                whole((1, VEC)),
            ]
            + [whole(x.shape) for x in extra_in],
            [per_group((SEQ, D))] + extra_out_specs,
            [shaped(count * GROUP, SEQ, D)] + extra_out,
            [(GROUP, PAD, D), (GROUP * PAD, 3 * D), (D, 3 * D), (8, 3 * D)] + extra_scratch,
            10 * 10**9 * count,
        )(*operands, *extra_in)

    grad_one, grads_one, sums_one = backward(
        False,
        0,
        1,
        (info, images, qkv, datt, dh, wqkv, vec),
        [],
        [whole((D, 3 * D)), whole((8, 3 * D))],
        [shaped(D, 3 * D), shaped(8, 3 * D)],
        [],
    )
    got_a, sums_one = tie(got_a, sums_one)

    mom_wide = jnp.concatenate([mom_up, mom_down.T], axis=1)
    mom_small = jnp.concatenate([mom_query, mom_key, mom_value, mom_out.T], axis=1)
    ahead = jnp.pad(mom_wide.reshape(rows, SLOTS, D), ((0, pitch - rows), (0, 0), (0, 0)))
    behind = jnp.pad(mom_small.reshape(rows, SLOTS, HALF), ((0, pitch - rows), (0, 0), (0, D - HALF)))
    mom_slots = jnp.concatenate([ahead, behind], axis=0).transpose(1, 0, 2)
    mom_slots = jnp.stack([pick(mom_slots, low ^ s) for s in range(SLOTS)])
    body_rows = above * SLOTS * pitch
    sum_a = jnp.concatenate([(keep_a + got_a).reshape(SLOTS, body_rows, D), mom_slots], axis=1)
    plane_a = [swap_dp(sum_a[s], s, dp_size) for s in range(1, plane[1])]
    sum_a, sums_one = tie(sum_a, sums_one)
    small = (SLOTS, above, 2 * pitch + 8, D)
    grad_two, keep_b, send_b = backward(
        True,
        1,
        groups - 1,
        (info, images, qkv, datt, dh, wqkv, vec),
        [sums_a, gout, grads_one, sums_one],
        [whole(small), whole(small)],
        [shaped(*small), shaped(*small)],
        [(1, VEC)],
    )
    plane_a, keep_b = tie(plane_a, keep_b)

    sum_b = keep_b + swap_tp(send_b)
    sum_b = scatter_sum(sum_b.reshape((-1,) + small[2:]), [plane], dp_size)
    parts_a = [sum_a[0]] + plane_a
    held_wide = jnp.stack([part[body_rows : body_rows + pitch] for part in parts_a])
    held_wide = jnp.concatenate([pick(held_wide, low ^ block) for block in range(SLOTS)], axis=0)
    held_small = [part[body_rows + pitch :, :HALF] for part in parts_a]
    held_small = jnp.concatenate(
        [
            jnp.concatenate([held_small[0], held_small[1]], axis=0),
            jnp.concatenate([held_small[2], held_small[3]], axis=0),
        ],
        axis=1,
    )
    total_a = parts_a[0][:body_rows]
    for part in plane_a:
        total_a = total_a + part[:body_rows]
    total_a = total_a.reshape(above, SLOTS * pitch, D)
    grads_a = scatter_sum(total_a, upper, dp_size)[0]
    grads_b = scatter_sum(sum_b, upper, dp_size)[0]
    grad_vectors = grads_b[2 * pitch, :piece]
    grads_b = grads_b[: 2 * pitch]

    new_b = momentum_decay * held_small + grads_b
    all_b = gather(new_b[None], upper, dp_size).reshape(-1, D)
    new_a = momentum_decay * held_wide + grads_a
    all_a = gather(new_a[None], upper, dp_size).reshape(-1, D)
    size = all_a.shape[0]
    gram = plain(gram_part, (all_a,), shaped(size, size), 10**9)
    gram = gram + swap_tp(gram)
    gram_half = lax.dynamic_slice_in_dim(gram, tp_index * (size // 2), size // 2, 0)
    gram_half = gram_half + swap_dp(gram_half, 1, dp_size)
    gram_other = swap_tp(gram_half)
    gram = jnp.concatenate(
        [jnp.where(is_first, gram_half, gram_other), jnp.where(is_first, gram_other, gram_half)]
    )
    steps_a, steps_b = plain(
        newton,
        (info, gram, all_a, all_b, swap_tp(all_b)),
        (shaped(SLOTS * pitch, D), shaped(2 * pitch, D)),
        24 * 10**9,
    )

    both_a = jnp.concatenate([grads_a, steps_a], axis=1).reshape(SLOTS, pitch, 2 * D)

    def outgoing(s):
        here = slice((s % 2) * pitch, (s % 2) * pitch + rows)
        lanes = slice((s // 2) * HALF, (s // 2 + 1) * HALF)
        return jnp.concatenate(
            [pick(both_a, low ^ s)[:rows], grads_b[here, lanes], steps_b[here, lanes]], axis=1
        )

    got = [outgoing(0)] + [swap_dp(outgoing(s), s, dp_size) for s in range(1, plane[1])]
    got = jnp.stack(got)
    by_slot = [pick(got, low ^ slot) for slot in range(SLOTS)]
    up_one, up_two, down_one, down_two = by_slot
    small_slots = [block[:, 2 * D :] for block in by_slot]
    grad_up = jnp.concatenate([up_one[:, :D], up_two[:, :D]], axis=1)
    step_up = jnp.concatenate([up_one[:, D : 2 * D], up_two[:, D : 2 * D]], axis=1)
    grad_down = jnp.concatenate([down_one[:, :D], down_two[:, :D]], axis=1).T
    step_down = jnp.concatenate([down_one[:, D : 2 * D], down_two[:, D : 2 * D]], axis=1).T
    grad_small = [block[:, :HALF] for block in small_slots]
    step_small = [block[:, HALF:] for block in small_slots]
    weight_grads = tuple(grad_small[:3]) + (grad_small[3].T, grad_up, grad_down)
    steps = tuple(step_small[:3]) + (step_small[3].T, step_up, step_down)
    momenta = (mom_query, mom_key, mom_value, mom_out, mom_up, mom_down)
    new_momenta = tuple(
        momentum_decay * previous + gradient for previous, gradient in zip(momenta, weight_grads)
    )

    def both_halves(mine):
        theirs = swap_tp(mine)
        return jnp.concatenate(
            [jnp.where(is_first, mine, theirs), jnp.where(is_first, theirs, mine)], axis=0
        )

    block_out = both_halves(block_own)
    input_grad = both_halves(jnp.concatenate([grad_one, grad_two], axis=0))

    first_new = adam_beta_one * adam_first + (1.0 - adam_beta_one) * grad_vectors
    second_new = adam_beta_two * adam_second + (1.0 - adam_beta_two) * grad_vectors * grad_vectors
    first_hat = first_new / (1.0 - adam_beta_one**STEP)
    second_hat = second_new / (1.0 - adam_beta_two**STEP)
    vector_update = -adam_rate * (
        first_hat / (jnp.sqrt(second_hat) + adam_eps) + adam_decay * vectors
    )
    return (
        (block_out, input_grad)
        + weight_grads
        + (grad_vectors,)
        + new_momenta
        + steps
        + (first_new, second_new, vector_update)
    )


def solution(mesh):
    image = P("dp", None, None)
    wide = P("dp", "tp")
    tall = P("tp", "dp")
    flat = P(("dp", "tp"))
    six = (wide, wide, wide, tall, wide, tall)
    in_specs = (image, P("dp"), image) + six + (flat,) + six + (flat, flat)
    out_specs = (image, image) + six + (flat,) + six + six + (flat, flat, flat)
    return jax.shard_map(body, mesh=mesh, in_specs=in_specs, out_specs=out_specs, check_vma=False)
```

```python
import functools
import math

import jax
import jax.numpy as jnp
import numpy as np
from jax import lax
from jax.experimental import pallas as pl
from jax.experimental.pallas import tpu as pltpu
from jax.sharding import PartitionSpec as P

D = 384
HEADS = 6
HEAD_DIM = 64
FF = 1536
SEQ = 197
PAD = 208
GROUP = 2
COLUMNS = 256
PARTS = 3
NS_STEPS = 5
STEP = 10
HALF = D // 2
SLOTS = 4
VEC = 4608
UNITS = FF // 2

norm_eps = 1e-06
ns_first = 3.4445
ns_second = -4.775
ns_third = 2.0315
momentum_decay = 0.95
matrix_rate = 1.0
adam_beta_one = 0.9
adam_beta_two = 0.999
adam_rate = 0.05
adam_decay = 0.05
adam_eps = 1e-08
f32 = jnp.float32
bf16 = jnp.bfloat16
VMEM_BYTES = 60 * 2**20
ONCE = pl.Buffered(1)


def split(value):
    high = value.astype(bf16)
    return high, (value - high.astype(f32)).astype(bf16)


def dot_one(left, right, left_dim, right_dim):
    return lax.dot_general(
        left, right, (((left_dim,), (right_dim,)), ((), ())), preferred_element_type=f32
    )


def dot(left, right, left_dim, right_dim):
    left_high, left_low = left if isinstance(left, tuple) else split(left)
    right_high, right_low = right if isinstance(right, tuple) else split(right)
    return dot_one(left_high, right_high, left_dim, right_dim) + (
        dot_one(left_high, right_low, left_dim, right_dim)
        + dot_one(left_low, right_high, left_dim, right_dim)
    )


def nn(left, right):
    return dot(left, right, 1, 0)


def nt(left, right):
    return dot(left, right, 1, 1)


def tn(left, right):
    return dot(left, right, 0, 0)


def levels(dp_size):
    bits = dp_size.bit_length() - 1
    out = []
    shift = 0
    while bits:
        width = min(2, bits)
        out.append((shift, 1 << width))
        shift += width
        bits -= width
    return out[::-1]


def padded_rows(dp_size):
    return -(-(D // dp_size) // 8) * 8


def swap_dp(value, mask, dp_size):
    return lax.ppermute(value, "dp", [(i, i ^ mask) for i in range(dp_size)])


def swap_tp(value):
    return lax.ppermute(value, "tp", [(0, 1), (1, 0)])


def tie(first, second):
    return lax.optimization_barrier((first, second))


def exchange(block, level, dp_size):
    shift, size = level
    return [swap_dp(block, s << shift, dp_size) for s in range(1, size)]


def gather(block, groups, dp_size):
    for level in groups:
        block = jnp.concatenate([block] + exchange(block, level, dp_size), axis=0)
    return block


def place_of(value, groups):
    place = 0
    stride = 1
    for shift, size in groups:
        place = place + ((value >> shift) & (size - 1)) * stride
        stride *= size
    return place


def scatter_sum(value, groups, dp_size):
    for shift, size in groups[::-1]:
        value = value.reshape((size, -1) + value.shape[1:])
        total = value[0]
        for part in [swap_dp(value[s], s << shift, dp_size) for s in range(1, size)]:
            total = total + part
        value = total
    return value


def normalize(rows):
    centre = jnp.sum(rows, axis=-1, keepdims=True) * (1.0 / D)
    offset = rows - centre
    spread = jnp.sum(offset * offset, axis=-1, keepdims=True) * (1.0 / D)
    rate = lax.rsqrt(spread + norm_eps)
    return offset * rate, rate


def normalize_back(grad, unit, rate, gain):
    scaled = grad * gain
    mean_one = jnp.sum(scaled, axis=-1, keepdims=True) * (1.0 / D)
    mean_two = jnp.sum(scaled * unit, axis=-1, keepdims=True) * (1.0 / D)
    return rate * (scaled - mean_one - unit * mean_two)


def row_sum(value):
    return jnp.sum(value, axis=0, keepdims=True)


def lanes(*parts):
    return jnp.concatenate(parts, axis=1)


def lines(*parts):
    return jnp.concatenate(parts, axis=0)


def left_three(value):
    high, low = split(value)
    return lanes(high, high, low)


def weights_three(value):
    high, low = split(value)
    return lines(high, low, high)


def rows_left(value):
    high, low = split(value)
    return lines(high, high, low)


def rows_right(value):
    high, low = split(value)
    return lines(high, low, high)


def nt_wide(left, weights):
    high, low = split(left)
    count = weights.shape[0] // 2
    both = dot_one(high, weights, 1, 1)
    return both[:, :count] + (both[:, count:] + dot_one(low, weights[:count], 1, 1))


def stack_pair(value):
    lane = lax.broadcasted_iota(jnp.int32, value.shape, 1)
    gap = jnp.zeros((COLUMNS - PAD, value.shape[1]), f32)
    return lines(
        jnp.where(lane < HEAD_DIM, value, 0.0), gap, jnp.where(lane < HEAD_DIM, 0.0, value), gap
    )


def pair_product(left_high, left_low, right):
    both = dot_one(left_high, lanes(*right), 1, 0)
    width = right[0].shape[1]
    return both[:, :width] + (both[:, width:] + dot_one(left_low, right[0], 1, 0))


def relative(vec, is_first):
    half = vec.shape[1] // 2
    return jnp.where(is_first, vec, jnp.concatenate([vec[:, half:], vec[:, :half]], axis=1))


def for_plane(dp_size, info, parts, place):
    every = levels(dp_size)
    count = every[-1][1]
    for low in range(count):

        @pl.when((info[1] & (count - 1)) == low)
        def _():
            for j in range(dp_size):
                at = place_of(info[1] ^ j, every[:-1])
                place(j, *[group[(j % count) ^ low][at] for group in parts])


def attention_forward(dp_size, info, images, *rest):
    count = levels(dp_size)[-1][1]
    own, other = rest[:count], rest[count : 2 * count]
    qkv_out, att_out, hid_out, wqkv_out, wo_out, vec_out, xs, plain_w, wqkv, wo, att, vec = rest[2 * count :]
    attention_forward_body(
        dp_size, info, images, own, other, qkv_out, att_out, hid_out, wqkv_out, wo_out, vec_out, xs, plain_w, wqkv, wo, att, vec
    )


def attention_forward_body(dp_size, info, images, own, other, qkv_out, att_out, hid_out, wqkv_out, wo_out, vec_out, xs, plain_w, wqkv, wo, att, vec):
    step = pl.program_id(0)
    rows = D // dp_size
    is_first = info[0] == 0

    @pl.when(step == 0)
    def _():
        xs[...] = jnp.zeros_like(xs)
        piece = VEC // (2 * dp_size)

        def place(j, mine, theirs):
            here = slice(j * rows, (j + 1) * rows)
            for kind in range(4):
                plain_w[here, kind * D : kind * D + HALF] = mine[:, kind * HALF : (kind + 1) * HALF]
                plain_w[here, kind * D + HALF : (kind + 1) * D] = theirs[:, kind * HALF : (kind + 1) * HALF]
            for line in range(-(-piece // 128)):
                size = min(128, piece - line * 128)
                one = mine[line : line + 1, 4 * HALF : 4 * HALF + size]
                two = theirs[line : line + 1, 4 * HALF : 4 * HALF + size]
                base = 2 * j * piece + line * 128
                vec[0:1, base : base + size] = jnp.where(is_first, one, two)
                vec[0:1, base + piece : base + piece + size] = jnp.where(is_first, two, one)

        for_plane(dp_size, info, (own, other), place)
        wqkv[...] = weights_three(plain_w[:, : 3 * D])
        wo[...] = weights_three(plain_w[:, 3 * D :])

    xs[:, :SEQ, :] = images[...]
    tokens = xs[...].reshape(GROUP * PAD, D)
    unit, _ = normalize(tokens)
    normed = unit * vec[0:1, :D] + vec[0:1, 2 * D : 3 * D]
    bias = lanes(
        relative(vec[0:1, 4 * D : 5 * D], is_first),
        jnp.zeros((1, D), f32),
        relative(vec[0:1, 5 * D : 6 * D], is_first),
    )
    qkv = dot_one(left_three(normed), wqkv[...], 1, 0) + bias
    qkv_out[...] = qkv.reshape(GROUP, PAD, 3 * D)
    column = lax.broadcasted_iota(jnp.int32, (PAD, 2 * COLUMNS), 1) & (COLUMNS - 1)
    lane = lax.broadcasted_iota(jnp.int32, (PAD, 2 * HEAD_DIM), 1)
    for image in range(GROUP):
        for pair in range(HEADS // 2):
            here = slice(pair * 128, (pair + 1) * 128)
            query_high, query_low = split(qkv_out[image, :, here] * 0.125)
            key_high, key_low = split(stack_pair(qkv_out[image, :, D + pair * 128 : D + (pair + 1) * 128]))
            value = split(stack_pair(qkv_out[image, :, 2 * D + pair * 128 : 2 * D + (pair + 1) * 128]))
            scores = dot_one(
                lanes(query_high, query_high, query_low), lanes(key_high, key_low, key_high), 1, 1
            )
            scores = jnp.where(column < SEQ, scores, -1e30)
            parts = []
            totals = []
            for half in (scores[:, :COLUMNS], scores[:, COLUMNS:]):
                part = jnp.exp(half - jnp.max(half, axis=-1, keepdims=True))
                parts.append(part)
                totals.append(1.0 / jnp.sum(part, axis=-1, keepdims=True))
            weights_high, weights_low = split(lanes(*parts))
            result = pair_product(weights_high, weights_low, value)
            att[image * PAD : (image + 1) * PAD, here] = result * jnp.where(
                lane < HEAD_DIM, totals[0], totals[1]
            )
    attended = att[...]
    att_out[...] = attended.reshape(GROUP, PAD, D)
    hidden = tokens + nt_wide(attended, wo[: 2 * D]) + vec[0:1, 6 * D : 7 * D]
    hid_out[...] = hidden.reshape(GROUP, PAD, D)

    @pl.when(step == pl.num_programs(0) - 1)
    def _():
        wqkv_out[...] = wqkv[...]
        wo_out[...] = wo[...]
        vec_out[...] = vec[...]


def mlp(dp_size, info, hid, att, cot, *rest):
    count = levels(dp_size)[-1][1]
    mlp_body(dp_size, info, hid, att, cot, rest[:count], rest[count : 2 * count], *rest[2 * count :])


def mlp_body(dp_size, info, hid, att, cot, own, other, wo, vec, block_out, dh_out, datt_out, keep, send, gout_out, sums, wup, wdown, cs, gup, gdown, gout, second_lanes, dy_lanes, second_rows, dy_rows, result, dsecond, bias):
    step = pl.program_id(0)
    rows = D // dp_size

    @pl.when(step == 0)
    def _():
        cs[...] = jnp.zeros_like(cs)

        def place(j, mine, theirs):
            here = slice(j * rows, (j + 1) * rows)
            gup[here, :UNITS] = mine[:, :UNITS]
            gup[here, UNITS:] = theirs[:, :UNITS]
            gdown[here, :UNITS] = mine[:, UNITS:]
            gdown[here, UNITS:] = theirs[:, UNITS:]

        for_plane(dp_size, info, (own, other), place)
        wup[...] = weights_three(gup[...])
        wdown[...] = weights_three(gdown[...])
        gup[...] = jnp.zeros_like(gup)
        gdown[...] = jnp.zeros_like(gdown)
        gout[...] = jnp.zeros_like(gout)
        sums[...] = jnp.zeros_like(sums)

    first = (info[0] * pl.num_programs(0) + step) * GROUP
    lives = [jnp.where(first + image < info[2], 1.0, 0.0).astype(f32) for image in range(GROUP)]
    for image in range(GROUP):
        cs[image, :SEQ, :] = cot[image] * lives[image]
    hidden = hid[...].reshape(GROUP * PAD, D)
    unit, rate = normalize(hidden)
    gain = vec[0:1, D : 2 * D]
    second = unit * gain + vec[0:1, 3 * D : 4 * D]
    dy = cs[...].reshape(GROUP * PAD, D)
    bias[...] = relative(vec[0:1, 8 * D :], info[0] == 0)
    second_lanes[...] = left_three(second)
    second_rows[...] = rows_left(second)
    dy_lanes[...] = left_three(dy)
    dy_rows[...] = rows_left(dy)
    result[...] = hidden + vec[0:1, 7 * D : 8 * D]
    dsecond[...] = jnp.zeros_like(dsecond)

    def units(part, carry):
        width = FF // PARTS
        here = pl.ds(pl.multiple_of(part * width, 128), width)
        pre = dot_one(second_lanes[...], wup[:, here], 1, 0) + bias[:, here]
        dact = dot_one(dy_lanes[...], wdown[:, here], 1, 0)
        phi = 0.5 * (1.0 + lax.erf(pre * math.sqrt(0.5)))
        slope = phi + pre * (jnp.exp(-0.5 * pre * pre) * (1.0 / math.sqrt(2.0 * math.pi)))
        act = pre * phi
        dpre = dact * slope
        result[...] += nt_wide(act, wdown[: 2 * D, here])
        gdown[:, here] += dot_one(dy_rows[...], rows_right(act), 0, 0)
        gup[:, here] += dot_one(second_rows[...], rows_right(dpre), 0, 0)
        dsecond[...] += nt_wide(dpre, wup[: 2 * D, here])
        sums[0:1, here] += row_sum(dpre)
        return carry

    lax.fori_loop(0, PARTS, units, 0)
    dsecond = dsecond[...]
    for image in range(GROUP):
        block_out[image] = result[image * PAD : image * PAD + SEQ] * lives[image]
    dh = dy + normalize_back(dsecond, unit, rate, gain)
    dh_out[...] = dh.reshape(GROUP, PAD, D)
    attended = att[...].reshape(GROUP * PAD, D)
    gout[...] += dot_one(rows_left(dh), rows_right(attended), 0, 0)
    datt_out[...] = dot_one(left_three(dh), wo[...], 1, 0).reshape(GROUP, PAD, D)
    sums[1:2, :D] += row_sum(dsecond * unit)
    sums[2:3, :D] += row_sum(dsecond)
    sums[3:4, :D] += row_sum(dh)
    sums[4:5, :D] += row_sum(dy)

    @pl.when(step == pl.num_programs(0) - 1)
    def _():
        gout_out[...] = gout[...]
        pitch = padded_rows(dp_size)
        if pitch != rows:
            keep[...] = jnp.zeros_like(keep)
            send[...] = jnp.zeros_like(send)
        upper = levels(dp_size)[:-1]
        low_count = levels(dp_size)[-1][1]
        low = info[1] & (low_count - 1)
        for j in range(dp_size):
            at = place_of(info[1] ^ j, upper)
            here = slice(j * rows, (j + 1) * rows)
            block = j % low_count
            there = slice(block * pitch, block * pitch + rows)
            for slot in range(SLOTS):
                grad = gup if slot < 2 else gdown
                base = (slot % 2) * D
                keep[low ^ slot, at, there, :] = grad[here, base : base + D]
                send[low ^ slot, at, there, :] = grad[here, UNITS + base : UNITS + base + D]


def attention_backward(dp_size, last, groups, first, info, images, qkv, datt, dh, wqkv, vec, *rest):
    if last:
        sums_a, gout, grads_in, sums_in, grad_in, keep, send, xs, dqkv, grads, sums, flat = rest
    else:
        grad_in, grads_out, sums_out, xs, dqkv, grads, sums = rest
    step = pl.program_id(0)
    rows = D // dp_size

    @pl.when(step == 0)
    def _():
        xs[...] = jnp.zeros_like(xs)
        if last:
            grads[...] = grads_in[...]
            sums[...] = sums_in[...]
        else:
            grads[...] = jnp.zeros_like(grads)
            sums[...] = jnp.zeros_like(sums)

    xs[:, :SEQ, :] = images[...]
    tokens = xs[...].reshape(GROUP * PAD, D)
    unit, rate = normalize(tokens)
    gain = vec[0:1, :D]
    normed = unit * gain + vec[0:1, 2 * D : 3 * D]
    line = lax.broadcasted_iota(jnp.int32, (PAD, 2 * COLUMNS), 0)
    for image in range(GROUP):
        part = slice(image * PAD, (image + 1) * PAD)
        for pair in range(HEADS // 2):
            here = slice(pair * 128, (pair + 1) * 128)
            key_at = slice(D + pair * 128, D + (pair + 1) * 128)
            value_at = slice(2 * D + pair * 128, 2 * D + (pair + 1) * 128)
            query = split(stack_pair(qkv[image, :, here] * 0.125))
            grad_o = split(stack_pair(datt[image, :, here]))
            key_high, key_low = split(qkv[image, :, key_at])
            value_high, value_low = split(qkv[image, :, value_at])
            scores = dot_one(
                lanes(key_high, key_high, key_low), lanes(query[0], query[1], query[0]), 1, 1
            )
            scores = jnp.where(line < SEQ, scores, -1e30)
            weights = jnp.exp(scores - jnp.max(scores, axis=0, keepdims=True))
            weights = weights * (1.0 / jnp.sum(weights, axis=0, keepdims=True))
            dweights = dot_one(
                lanes(value_high, value_high, value_low), lanes(grad_o[0], grad_o[1], grad_o[0]), 1, 1
            )
            delta = jnp.sum(weights * dweights, axis=0, keepdims=True)
            weights_high, weights_low = split(weights)
            ds_high, ds_low = split(weights * (dweights - delta))
            dqkv[part, value_at] = pair_product(weights_high, weights_low, grad_o)
            dqkv[part, key_at] = pair_product(ds_high, ds_low, query)
            both = dot_one(lanes(key_high, key_low), ds_high, 0, 0)
            turned = both[:128] + (both[128:] + dot_one(key_high, ds_low, 0, 0))
            turned = lines(turned[:HEAD_DIM, :COLUMNS], turned[HEAD_DIM:, COLUMNS:])
            dqkv[part, here] = turned.T[:PAD] * 0.125
    dall = dqkv[...]
    grads[...] += dot_one(rows_left(normed), rows_right(dall), 0, 0)
    dnormed = nt_wide(dall, wqkv[...])
    dx = dh[...].reshape(GROUP * PAD, D) + normalize_back(dnormed, unit, rate, gain)
    for image in range(GROUP):
        grad_in[image] = dx[image * PAD : image * PAD + SEQ]
    sums[0:1, :] += row_sum(dall)
    sums[1:2, :D] += row_sum(dnormed * unit)
    sums[2:3, :D] += row_sum(dnormed)

    @pl.when(step == pl.num_programs(0) - 1)
    def _():
        if not last:
            grads_out[...] = grads[...]
            sums_out[...] = sums[...]
            return
        is_first = info[0] == 0
        total = sums[0:1, :]
        query_sum = total[:, :D]
        value_sum = total[:, 2 * D :]
        flat[0:1, :D] = sums[1:2, :D]
        flat[0:1, D : 2 * D] = sums_a[1:2, :D]
        flat[0:1, 2 * D : 3 * D] = sums[2:3, :D]
        flat[0:1, 3 * D : 4 * D] = sums_a[2:3, :D]
        flat[0:1, 4 * D : 5 * D] = relative(query_sum, is_first)
        flat[0:1, 5 * D : 6 * D] = relative(value_sum, is_first)
        flat[0:1, 6 * D : 7 * D] = sums_a[3:4, :D]
        flat[0:1, 7 * D : 8 * D] = sums_a[4:5, :D]
        flat[0:1, 8 * D :] = relative(sums_a[0:1, :], is_first)
        pitch = padded_rows(dp_size)
        keep[...] = jnp.zeros_like(keep)
        send[...] = jnp.zeros_like(send)
        upper = levels(dp_size)[:-1]
        low_count = levels(dp_size)[-1][1]
        low = info[1] & (low_count - 1)
        piece = VEC // (2 * dp_size)
        for j in range(dp_size):
            at = place_of(info[1] ^ j, upper)
            here = slice(j * rows, (j + 1) * rows)
            block = j % low_count
            one = flat[0:1, 2 * j * piece : (2 * j + 1) * piece]
            two = flat[0:1, (2 * j + 1) * piece : (2 * j + 2) * piece]
            keep[low ^ block, at, 2 * pitch : 2 * pitch + 1, :piece] = jnp.where(is_first, one, two)
            send[low ^ block, at, 2 * pitch : 2 * pitch + 1, :piece] = jnp.where(is_first, two, one)
            for slot in range(SLOTS):
                place = block ^ slot
                there = slice((place % 2) * pitch, (place % 2) * pitch + rows)
                lanes = slice((place // 2) * HALF, (place // 2 + 1) * HALF)
                if slot < 3:
                    mine = grads[here, slot * D : slot * D + HALF]
                    theirs = grads[here, slot * D + HALF : (slot + 1) * D]
                else:
                    mine = gout[here, :HALF]
                    theirs = gout[here, HALF:]
                keep[low ^ slot, at, there, lanes] = mine
                send[low ^ slot, at, there, lanes] = theirs


def params():
    return pltpu.CompilerParams(vmem_limit_bytes=VMEM_BYTES, dimension_semantics=("arbitrary",))


def whole(shape):
    return pl.BlockSpec(shape, lambda g, info: (0,) * len(shape), pipeline_mode=ONCE)


def per_group(shape, first=0):
    return pl.BlockSpec((GROUP,) + shape, lambda g, info: (first + g,) + (0,) * len(shape))


def half_images(groups, first=0):
    return pl.BlockSpec((GROUP, SEQ, D), lambda g, info: (info[0] * groups + first + g, 0, 0))


def shaped(*shape):
    return jax.ShapeDtypeStruct(shape, f32)


def call(kernel, groups, in_specs, out_specs, out_shape, scratch, cost):
    return pl.pallas_call(
        kernel,
        grid_spec=pltpu.PrefetchScalarGridSpec(
            num_scalar_prefetch=1,
            grid=(groups,),
            in_specs=in_specs,
            out_specs=out_specs,
            scratch_shapes=[pltpu.VMEM(s, f32) if isinstance(s, tuple) else s for s in scratch],
        ),
        out_shape=out_shape,
        compiler_params=params(),
        cost_estimate=pl.CostEstimate(flops=cost, bytes_accessed=20 * 2**20, transcendentals=0),
    )


def polynomial(gram):
    pair = split(gram)
    return ns_second * gram + ns_third * nn(pair, pair)


def eye(size):
    line = lax.broadcasted_iota(jnp.int32, (size, size), 0)
    column = lax.broadcasted_iota(jnp.int32, (size, size), 1)
    return jnp.where(line == column, 1.0, 0.0).astype(f32)


def norm_scale(total):
    return 1.0 / (jnp.sqrt(jnp.full((1, 1), total, f32)) + 1e-07)


def gram_part(block, out):
    pair = split(block[...])
    out[...] = nt(pair, pair)


def product(left, right):
    return dot_one(left_three(left), weights_three(right), 1, 0)


def ns_wide(info, gram_ref, block, out):
    gram = gram_ref[...]
    ident = eye(gram.shape[0])
    scale = norm_scale(jnp.sum(gram * ident))
    gram = gram * (scale * scale)
    total = None
    for sweep in range(NS_STEPS):
        left, right = left_three(gram), weights_three(gram)
        mixing = ns_first * ident + ns_second * gram + ns_third * dot_one(left, right, 1, 0)
        mixing_right = weights_three(mixing)
        total = mixing if total is None else dot_one(left_three(total), mixing_right, 1, 0)
        if sweep < NS_STEPS - 1:
            gram = dot_one(left_three(dot_one(left, mixing_right, 1, 0)), mixing_right, 1, 0)
    factor = jnp.where(info[3] >= 2, -2.0, -1.0).astype(f32) * matrix_rate
    out[...] = product(total[: out.shape[0]], block[...]) * (scale * factor)


def ns_square(own, other, out):
    half = own.shape[0]
    matrix = lanes(
        lines(own[:, :HALF], own[:, HALF:]),
        lines(other[:, :HALF], other[:, HALF:]),
    )
    matrix = matrix * norm_scale(jnp.sum(matrix * matrix))
    for sweep in range(NS_STEPS):
        high, low = split(matrix)
        square = dot_one(lanes(high, high, low), lanes(high, low, high), 1, 1)
        mixing = ns_second * square + ns_third * product(square, square)
        matrix = ns_first * matrix + dot_one(left_three(mixing), lines(high, low, high), 1, 0)
    rows = out.shape[0]
    out[:, :HALF] = matrix[:rows, :HALF] * (-matrix_rate)
    out[:, HALF:] = matrix[half : half + rows, :HALF] * (-matrix_rate)


def plain(kernel, operands, out_shape, cost):
    return pl.pallas_call(
        kernel,
        in_specs=[
            pl.BlockSpec(memory_space=pltpu.SMEM if x.ndim == 1 else pltpu.VMEM) for x in operands
        ],
        out_specs=jax.tree.map(lambda _: pl.BlockSpec(memory_space=pltpu.VMEM), out_shape),
        out_shape=out_shape,
        compiler_params=pltpu.CompilerParams(vmem_limit_bytes=VMEM_BYTES // 2),
        cost_estimate=pl.CostEstimate(flops=cost, bytes_accessed=5 * 2**20, transcendentals=0),
    )(*operands)


def open_plane(count, keep, got, momenta, total):
    for s in range(SLOTS):
        total[s, :count] = (keep[s] + got[s]).reshape(count, D)
        total[s, count:] = momenta[s]


def close_plane(slots, above, pitch, info, own, *rest):
    parts = rest[: slots - 1]
    total, held_wide, held_small = rest[-3:]
    count = above * SLOTS * pitch
    low = info[3]
    blocks = [own.at[0]] + list(parts)
    value = blocks[0][:count]
    for block in blocks[1:]:
        value = value + block[:count]
    total[...] = value.reshape(total.shape)
    for s, block in enumerate(blocks):
        at = pl.multiple_of((low ^ s) * pitch, 8)
        held_wide[pl.ds(at, pitch), :] = block[count : count + pitch]
        there = slice((s % 2) * pitch, (s % 2 + 1) * pitch)
        held_small[there, (s // 2) * HALF : (s // 2 + 1) * HALF] = block[count + pitch :, :HALF]


def open_upper(size, slots, total, wide_part, held_wide, own, *rest):
    small_parts = rest[: slots - 1]
    grads, message = rest[-2:]
    value = total[0] + wide_part[...]
    grads[...] = value
    moment = momentum_decay * held_wide[...] + value
    wide = value.shape[0]
    small = own[0]
    for part in small_parts:
        small = small + part[...]
    small = small.reshape(size, -1, D)
    for s in range(size):
        message[s, :wide] = moment
        message[s, wide:] = small[s]


def close_upper(size, wide, own, *rest):
    parts = rest[: size - 1]
    held_small = rest[size - 1]
    moments, small, moment = rest[-3:]
    value = own[0, wide:]
    moments[:wide] = own[0, :wide]
    for s, part in enumerate(parts):
        moments[(s + 1) * wide : (s + 2) * wide] = part[:wide]
        value = value + part[wide:]
    small[...] = value
    rows = moment.shape[0]
    moment[...] = momentum_decay * held_small[...] + value[:rows]


def return_messages(rows, pitch, info, grads_a, steps_a, grads_b, steps_b, message):
    low = info[3]
    for s in range(SLOTS):
        at = pl.multiple_of((low ^ s) * pitch, 8)
        message[s, :, :D] = grads_a[pl.ds(at, pitch), :]
        message[s, :, D : 2 * D] = steps_a[pl.ds(at, pitch), :]
        here = slice((s % 2) * pitch, (s % 2 + 1) * pitch)
        lane = slice((s // 2) * HALF, (s // 2 + 1) * HALF)
        message[s, :, 2 * D : 2 * D + HALF] = grads_b[here, lane]
        message[s, :, 2 * D + HALF :] = steps_b[here, lane]


def finish(rows, info, own, *rest):
    parts, momenta, stack = rest[: SLOTS - 1], rest[SLOTS - 1 : SLOTS + 5], rest[-1]
    outs = rest[SLOTS + 5 : -1]
    low = info[3]
    stack[0] = own[0]
    for s, part in enumerate(parts):
        stack[s + 1] = part[...]
    for slot in range(SLOTS):
        block = stack[low ^ slot]
        grad, step, moment = outs[slot], outs[12 + slot], outs[6 + slot]
        value = block[:rows, 2 * D : 2 * D + HALF]
        grad[...] = value
        moment[...] = momentum_decay * momenta[slot][...] + value
        step[...] = block[:rows, 2 * D + HALF :]
        wide = 4 + slot // 2
        here = slice((slot % 2) * D, (slot % 2 + 1) * D)
        value = block[:rows, :D]
        outs[wide][:, here] = value
        outs[6 + wide][:, here] = momentum_decay * momenta[wide][:, here] + value
        outs[12 + wide][:, here] = block[:rows, D : 2 * D]


def gated(kernel, operands, out_shape, passes, scratch=(), cost=10**6):
    def run(*refs):
        count = len(operands) + len(passes)
        outs = refs[count : count + len(out_shape)]
        kernel(*refs[: len(operands)], *outs, *refs[count + len(out_shape) + len(passes) :])

    in_specs = []
    arrays = []
    for x in operands:
        if isinstance(x, tuple):
            x, index = x
            block = (1,) + x.shape[1:]
            in_specs.append(pl.BlockSpec(block, lambda g, n=x.ndim, i=index: (i,) + (0,) * (n - 1)))
        elif x.dtype == jnp.int32:
            in_specs.append(pl.BlockSpec(memory_space=pltpu.SMEM))
        else:
            in_specs.append(pl.BlockSpec(x.shape, lambda g, n=x.ndim: (0,) * n))
        arrays.append(x)
    anywhere = pl.BlockSpec(memory_space=pl.ANY)
    result = pl.pallas_call(
        run,
        grid=(1,),
        in_specs=in_specs + [anywhere] * len(passes),
        out_specs=[pl.BlockSpec(x.shape, lambda g, n=len(x.shape): (0,) * n) for x in out_shape]
        + [anywhere] * len(passes),
        out_shape=list(out_shape) + [shaped(*x.shape) for x in passes],
        scratch_shapes=list(scratch),
        input_output_aliases={
            len(operands) + i: len(out_shape) + i for i in range(len(passes))
        },
        compiler_params=pltpu.CompilerParams(vmem_limit_bytes=VMEM_BYTES // 2),
        cost_estimate=pl.CostEstimate(flops=cost, bytes_accessed=2**20, transcendentals=0),
    )(*arrays, *passes)
    return result


def pick(stack, index):
    return lax.dynamic_index_in_dim(stack, index, 0, keepdims=False)


def body(
    images,
    image_count,
    cotangent,
    w_query,
    w_key,
    w_value,
    w_out,
    w_up,
    w_down,
    vectors,
    mom_query,
    mom_key,
    mom_value,
    mom_out,
    mom_up,
    mom_down,
    adam_first,
    adam_second,
):
    tp_index = lax.axis_index("tp")
    dp_index = lax.axis_index("dp")
    dp_size = lax.axis_size("dp")
    rows = D // dp_size
    pitch = padded_rows(dp_size)
    piece = vectors.shape[0]
    groups = images.shape[0] // (2 * GROUP)
    slots = groups * GROUP
    is_first = tp_index == 0
    every = levels(dp_size)
    upper, plane = every[:-1], every[-1]
    above = dp_size // plane[1]
    low = dp_index & (plane[1] - 1)
    info = jnp.stack([tp_index, dp_index, image_count[0], low]).astype(jnp.int32)

    vec_tail = jnp.pad(vectors, (0, rows * 128 - piece)).reshape(rows, 128)
    shard_one = jnp.concatenate([w_query, w_key, w_value, w_out.T, vec_tail], axis=1)
    shard_two = jnp.concatenate([w_up, w_down.T], axis=1)
    mom_wide = jnp.concatenate([mom_up, mom_down.T], axis=1)
    mom_small = jnp.concatenate([mom_query, mom_key, mom_value, mom_out.T], axis=1)
    ahead = jnp.pad(mom_wide.reshape(rows, SLOTS, D), ((0, pitch - rows), (0, 0), (0, 0)))
    behind = jnp.pad(mom_small.reshape(rows, SLOTS, HALF), ((0, pitch - rows), (0, 0), (0, D - HALF)))
    mom_slots = jnp.concatenate([ahead, behind], axis=0).transpose(1, 0, 2)
    mom_slots = jnp.stack([pick(mom_slots, low ^ s) for s in range(SLOTS)])

    part_one = gather(shard_one[None], upper, dp_size)
    part_one, mom_slots = tie(part_one, mom_slots)
    got_one = exchange(part_one, plane, dp_size)
    upper_parts = [shard_two[None]]
    for level in upper[:-1]:
        upper_parts = [jnp.concatenate(upper_parts + exchange(upper_parts[0], level, dp_size), axis=0)]
    upper_parts = upper_parts + exchange(upper_parts[0], upper[-1], dp_size)
    got_one, upper_parts = tie(got_one, upper_parts)
    part_two = jnp.concatenate(upper_parts, axis=0)
    own_one = [part_one] + got_one
    other_one = [swap_tp(part) for part in own_one]
    got_two = exchange(part_two, plane, dp_size)
    near_two = swap_tp(part_two)

    qkv, att, hid, wqkv, wo, vec = call(
        functools.partial(attention_forward, dp_size),
        groups,
        [
            half_images(groups),
        ]
        + [whole((above, rows, 4 * HALF + 128))] * (2 * SLOTS),
        [
            per_group((PAD, 3 * D)),
            per_group((PAD, D)),
            per_group((PAD, D)),
            whole((3 * D, 3 * D)),
            whole((3 * D, D)),
            whole((1, VEC)),
        ],
        [
            shaped(slots, PAD, 3 * D),
            shaped(slots, PAD, D),
            shaped(slots, PAD, D),
            jax.ShapeDtypeStruct((3 * D, 3 * D), bf16),
            jax.ShapeDtypeStruct((3 * D, D), bf16),
            shaped(1, VEC),
        ],
        [
            (GROUP, PAD, D),
            (D, 4 * D),
            pltpu.VMEM((3 * D, 3 * D), bf16),
            pltpu.VMEM((3 * D, D), bf16),
            (GROUP * PAD, D),
            (1, VEC),
        ],
        16 * 10**9,
    )(info, images, *own_one, *other_one)

    got_two, hid = tie(got_two, hid)
    own_two = [part_two] + got_two
    other_two = [near_two] + [swap_tp(part) for part in got_two]

    block_own, dh, datt, keep_a, send_a, gout, sums_a = call(
        functools.partial(mlp, dp_size),
        groups,
        [
            per_group((PAD, D)),
            per_group((PAD, D)),
            half_images(groups),
        ]
        + [whole((above, rows, 2 * UNITS))] * (2 * SLOTS)
        + [
            whole((3 * D, D)),
            whole((1, VEC)),
        ],
        [
            per_group((SEQ, D)),
            per_group((PAD, D)),
            per_group((PAD, D)),
            whole((SLOTS, above, SLOTS * pitch, D)),
            whole((SLOTS, above, SLOTS * pitch, D)),
            whole((D, D)),
            whole((8, FF)),
        ],
        [
            shaped(slots, SEQ, D),
            shaped(slots, PAD, D),
            shaped(slots, PAD, D),
            shaped(SLOTS, above, SLOTS * pitch, D),
            shaped(SLOTS, above, SLOTS * pitch, D),
            shaped(D, D),
            shaped(8, FF),
        ],
        [
            pltpu.VMEM((3 * D, FF), bf16),
            pltpu.VMEM((3 * D, FF), bf16),
            (GROUP, PAD, D),
            (D, FF),
            (D, FF),
            (D, D),
            pltpu.VMEM((GROUP * PAD, 3 * D), bf16),
            pltpu.VMEM((GROUP * PAD, 3 * D), bf16),
            pltpu.VMEM((3 * GROUP * PAD, D), bf16),
            pltpu.VMEM((3 * GROUP * PAD, D), bf16),
            (GROUP * PAD, D),
            (GROUP * PAD, D),
            (1, FF),
        ],
        48 * 10**9,
    )(info, hid, att, cotangent, *own_two, *other_two, wo, vec)

    got_a = swap_tp(send_a)

    def backward(last, first, count, operands, extra_in, extra_out_specs, extra_out, extra_scratch):
        return call(
            functools.partial(attention_backward, dp_size, last, groups, first),
            count,
            [
                half_images(groups, first),
                per_group((PAD, 3 * D), first),
                per_group((PAD, D), first),
                per_group((PAD, D), first),
                whole((2 * D, 3 * D)),
                whole((1, VEC)),
            ]
            + [whole(x.shape) for x in extra_in],
            [per_group((SEQ, D))] + extra_out_specs,
            [shaped(count * GROUP, SEQ, D)] + extra_out,
            [(GROUP, PAD, D), (GROUP * PAD, 3 * D), (D, 3 * D), (8, 3 * D)] + extra_scratch,
            10 * 10**9 * count,
        )(*operands, *extra_in)

    grad_one, grads_one, sums_one = backward(
        False,
        0,
        1,
        (info, images, qkv, datt, dh, wqkv, vec),
        [],
        [whole((D, 3 * D)), whole((8, 3 * D))],
        [shaped(D, 3 * D), shaped(8, 3 * D)],
        [],
    )
    body_rows = above * SLOTS * pitch
    sum_a, sums_one = gated(
        functools.partial(open_plane, body_rows),
        [keep_a, got_a, mom_slots],
        [shaped(SLOTS, body_rows + 2 * pitch, D)],
        [sums_one],
    )
    plane_a = [swap_dp(sum_a[s], s, dp_size) for s in range(1, plane[1])]
    small = (SLOTS, above, 2 * pitch + 8, D)
    grad_two, keep_b, send_b = backward(
        True,
        1,
        groups - 1,
        (info, images, qkv, datt, dh, wqkv, vec),
        [sums_a, gout, grads_one, sums_one],
        [whole(small), whole(small)],
        [shaped(*small), shaped(*small)],
        [(1, VEC)],
    )
    total_a, held_wide, held_small, send_b, block_own = gated(
        functools.partial(close_plane, SLOTS, above, pitch),
        [info, (sum_a, 0)] + plane_a,
        [shaped(above, SLOTS * pitch, D), shaped(SLOTS * pitch, D), shaped(2 * pitch, D)],
        [send_b, block_own],
    )
    sum_b = (keep_b + swap_tp(send_b)).reshape((SLOTS, above) + small[2:])
    plane_b = [swap_dp(sum_b[s], s, dp_size) for s in range(1, plane[1])]
    total_a = scatter_sum(total_a, upper[1:], dp_size)
    shift, size = upper[0]
    total_a = total_a.reshape(size, SLOTS * pitch, D)
    while size > 2:
        half = size // 2
        total_a = total_a.reshape(half, 2, SLOTS * pitch, D)
        total_a = total_a[:, 0] + swap_dp(total_a[:, 1], 1 << shift, dp_size)
        shift, size = shift + 1, half
    upper_a = [swap_dp(total_a[1], 1 << shift, dp_size)]

    def both_halves(mine):
        theirs = swap_tp(mine)
        return jnp.concatenate(
            [jnp.where(is_first, mine, theirs), jnp.where(is_first, theirs, mine)], axis=0
        )

    block_out = both_halves(block_own)

    first_shift, first_size = upper[-1]
    count = above // first_size * (2 * pitch + 8)
    grads_a, message, grad_one, grad_two = gated(
        functools.partial(open_upper, first_size, SLOTS),
        [(total_a, 0)] + upper_a + [held_wide, (sum_b, 0)] + plane_b,
        [shaped(SLOTS * pitch, D), shaped(first_size, SLOTS * pitch + count, D)],
        [grad_one, grad_two],
    )
    got = [swap_dp(message[s], s << first_shift, dp_size) for s in range(1, first_size)]
    all_a, total_b, new_b, block_out = gated(
        functools.partial(close_upper, first_size, SLOTS * pitch),
        [(message, 0)] + got + [held_small],
        [shaped(first_size * SLOTS * pitch, D), shaped(count, D), shaped(2 * pitch, D)],
        [block_out],
    )
    input_grad = both_halves(jnp.concatenate([grad_one, grad_two], axis=0))
    if len(upper) > 1:
        all_a = gather(all_a[None], upper[:-1][::-1], dp_size).reshape(-1, D)
        total_b = scatter_sum(total_b.reshape(-1, 2 * pitch + 8, D), upper[:-1], dp_size)[0]
        new_b = momentum_decay * held_small + total_b[: 2 * pitch]
    grad_vectors = total_b[2 * pitch, :piece]
    grads_b = total_b[: 2 * pitch]

    all_b = gather(new_b[None], upper, dp_size).reshape(-1, D)
    (steps_b,) = gated(
        ns_square, [all_b, swap_tp(all_b)], [shaped(2 * pitch, D)], [], cost=12 * 10**9
    )
    size = all_a.shape[0]
    gram = plain(gram_part, (all_a,), shaped(size, size), 10**9)
    gram = gram + swap_tp(gram)
    gram_half = lax.dynamic_slice_in_dim(gram, tp_index * (size // 2), size // 2, 0)
    gram_far = swap_dp(gram_half, 1, dp_size)
    gram_half = gram_half + gram_far
    gram_other = swap_tp(gram_half)
    gram = jnp.concatenate(
        [jnp.where(is_first, gram_half, gram_other), jnp.where(is_first, gram_other, gram_half)]
    )
    steps_a, steps_b = gated(
        ns_wide, [info, gram, all_a], [shaped(SLOTS * pitch, D)], [steps_b], cost=12 * 10**9
    )

    message, input_grad = gated(
        functools.partial(return_messages, rows, pitch),
        [info, grads_a, steps_a, grads_b, steps_b],
        [shaped(SLOTS, pitch, 3 * D)],
        [input_grad],
    )
    got = [swap_dp(message[s], s, dp_size) for s in range(1, plane[1])]
    momenta = [mom_query, mom_key, mom_value, mom_out.T, mom_up, mom_down.T]
    kinds = [shaped(rows, HALF)] * 4 + [shaped(rows, UNITS)] * 2
    results = gated(
        functools.partial(finish, rows),
        [info, (message, 0)] + got + momenta,
        kinds * 3,
        [],
        [pltpu.VMEM((SLOTS, pitch, 3 * D), f32)],
    )

    def in_order(six):
        return (six[0], six[1], six[2], six[3].T, six[4], six[5].T)

    weight_grads = in_order(results[:6])
    new_momenta = in_order(results[6:12])
    steps = in_order(results[12:])

    first_new = adam_beta_one * adam_first + (1.0 - adam_beta_one) * grad_vectors
    second_new = adam_beta_two * adam_second + (1.0 - adam_beta_two) * grad_vectors * grad_vectors
    first_hat = first_new / (1.0 - adam_beta_one**STEP)
    second_hat = second_new / (1.0 - adam_beta_two**STEP)
    vector_update = -adam_rate * (
        first_hat / (jnp.sqrt(second_hat) + adam_eps) + adam_decay * vectors
    )
    return (
        (block_out, input_grad)
        + weight_grads
        + (grad_vectors,)
        + new_momenta
        + steps
        + (first_new, second_new, vector_update)
    )


def solution(mesh):
    image = P("dp", None, None)
    wide = P("dp", "tp")
    tall = P("tp", "dp")
    flat = P(("dp", "tp"))
    six = (wide, wide, wide, tall, wide, tall)
    in_specs = (image, P("dp"), image) + six + (flat,) + six + (flat, flat)
    out_specs = (image, image) + six + (flat,) + six + six + (flat, flat, flat)
    return jax.shard_map(body, mesh=mesh, in_specs=in_specs, out_specs=out_specs, check_vma=False)
```

```python
import functools
import math

import jax
import jax.numpy as jnp
import numpy as np
from jax import lax
from jax.experimental import pallas as pl
from jax.experimental.pallas import tpu as pltpu
from jax.sharding import PartitionSpec as P

D = 384
HEADS = 6
HEAD_DIM = 64
FF = 1536
SEQ = 197
PAD = 208
GROUP = 2
COLUMNS = 256
PARTS = 3
UNROLL = 3
NS_STEPS = 5
STEP = 10
HALF = D // 2
SLOTS = 4
VEC = 4608
UNITS = FF // 2

norm_eps = 1e-06
ns_first = 3.4445
ns_second = -4.775
ns_third = 2.0315
momentum_decay = 0.95
matrix_rate = 1.0
adam_beta_one = 0.9
adam_beta_two = 0.999
adam_rate = 0.05
adam_decay = 0.05
adam_eps = 1e-08
f32 = jnp.float32
bf16 = jnp.bfloat16
VMEM_BYTES = 60 * 2**20
ONCE = pl.Buffered(1)


def split(value):
    high = value.astype(bf16)
    return high, (value - high.astype(f32)).astype(bf16)


def dot_one(left, right, left_dim, right_dim):
    return lax.dot_general(
        left, right, (((left_dim,), (right_dim,)), ((), ())), preferred_element_type=f32
    )


def dot(left, right, left_dim, right_dim):
    left_high, left_low = left if isinstance(left, tuple) else split(left)
    right_high, right_low = right if isinstance(right, tuple) else split(right)
    return dot_one(left_high, right_high, left_dim, right_dim) + (
        dot_one(left_high, right_low, left_dim, right_dim)
        + dot_one(left_low, right_high, left_dim, right_dim)
    )


def nn(left, right):
    return dot(left, right, 1, 0)


def nt(left, right):
    return dot(left, right, 1, 1)


def tn(left, right):
    return dot(left, right, 0, 0)


def levels(dp_size):
    bits = dp_size.bit_length() - 1
    out = []
    shift = 0
    while bits:
        width = min(2, bits)
        out.append((shift, 1 << width))
        shift += width
        bits -= width
    return out[::-1]


def padded_rows(dp_size):
    return -(-(D // dp_size) // 8) * 8


def swap_dp(value, mask, dp_size):
    return lax.ppermute(value, "dp", [(i, i ^ mask) for i in range(dp_size)])


def swap_tp(value):
    return lax.ppermute(value, "tp", [(0, 1), (1, 0)])


def tie(first, second):
    return lax.optimization_barrier((first, second))


def exchange(block, level, dp_size):
    shift, size = level
    return [swap_dp(block, s << shift, dp_size) for s in range(1, size)]


def gather(block, groups, dp_size):
    for level in groups:
        block = jnp.concatenate([block] + exchange(block, level, dp_size), axis=0)
    return block


def place_of(value, groups):
    place = 0
    stride = 1
    for shift, size in groups:
        place = place + ((value >> shift) & (size - 1)) * stride
        stride *= size
    return place


def scatter_sum(value, groups, dp_size):
    for shift, size in groups[::-1]:
        value = value.reshape((size, -1) + value.shape[1:])
        total = value[0]
        for part in [swap_dp(value[s], s << shift, dp_size) for s in range(1, size)]:
            total = total + part
        value = total
    return value


def normalize(rows):
    centre = jnp.sum(rows, axis=-1, keepdims=True) * (1.0 / D)
    offset = rows - centre
    spread = jnp.sum(offset * offset, axis=-1, keepdims=True) * (1.0 / D)
    rate = lax.rsqrt(spread + norm_eps)
    return offset * rate, rate


def normalize_back(grad, unit, rate, gain):
    scaled = grad * gain
    mean_one = jnp.sum(scaled, axis=-1, keepdims=True) * (1.0 / D)
    mean_two = jnp.sum(scaled * unit, axis=-1, keepdims=True) * (1.0 / D)
    return rate * (scaled - mean_one - unit * mean_two)


def row_sum(value):
    return jnp.sum(value, axis=0, keepdims=True)


def lanes(*parts):
    return jnp.concatenate(parts, axis=1)


def lines(*parts):
    return jnp.concatenate(parts, axis=0)


def left_three(value):
    high, low = split(value)
    return lanes(high, high, low)


def weights_three(value):
    high, low = split(value)
    return lines(high, low, high)


def rows_left(value):
    high, low = split(value)
    return lines(high, high, low)


def rows_right(value):
    high, low = split(value)
    return lines(high, low, high)


def nt_wide(left, weights):
    high, low = split(left)
    count = weights.shape[0] // 2
    both = dot_one(high, weights, 1, 1)
    return both[:, :count] + (both[:, count:] + dot_one(low, weights[:count], 1, 1))


def stack_pair(value):
    lane = lax.broadcasted_iota(jnp.int32, value.shape, 1)
    gap = jnp.zeros((COLUMNS - PAD, value.shape[1]), f32)
    return lines(
        jnp.where(lane < HEAD_DIM, value, 0.0), gap, jnp.where(lane < HEAD_DIM, 0.0, value), gap
    )


def pair_product(left_high, left_low, right):
    both = dot_one(left_high, lanes(*right), 1, 0)
    width = right[0].shape[1]
    return both[:, :width] + (both[:, width:] + dot_one(left_low, right[0], 1, 0))


def relative(vec, is_first):
    half = vec.shape[1] // 2
    return jnp.where(is_first, vec, jnp.concatenate([vec[:, half:], vec[:, :half]], axis=1))


def for_plane(dp_size, info, parts, place):
    every = levels(dp_size)
    count = every[-1][1]
    for low in range(count):

        @pl.when((info[1] & (count - 1)) == low)
        def _():
            for j in range(dp_size):
                at = place_of(info[1] ^ j, every[:-1])
                place(j, *[group[(j % count) ^ low][at] for group in parts])


def attention_forward(dp_size, info, images, *rest):
    count = levels(dp_size)[-1][1]
    own, other = rest[:count], rest[count : 2 * count]
    qkv_out, att_out, hid_out, wqkv_out, wo_out, vec_out, xs, plain_w, wqkv, wo, att, vec = rest[2 * count :]
    attention_forward_body(
        dp_size, info, images, own, other, qkv_out, att_out, hid_out, wqkv_out, wo_out, vec_out, xs, plain_w, wqkv, wo, att, vec
    )


def attention_forward_body(dp_size, info, images, own, other, qkv_out, att_out, hid_out, wqkv_out, wo_out, vec_out, xs, plain_w, wqkv, wo, att, vec):
    step = pl.program_id(0)
    rows = D // dp_size
    is_first = info[0] == 0

    @pl.when(step == 0)
    def _():
        xs[...] = jnp.zeros_like(xs)
        piece = VEC // (2 * dp_size)

        def place(j, mine, theirs):
            here = slice(j * rows, (j + 1) * rows)
            for kind in range(4):
                plain_w[here, kind * D : kind * D + HALF] = mine[:, kind * HALF : (kind + 1) * HALF]
                plain_w[here, kind * D + HALF : (kind + 1) * D] = theirs[:, kind * HALF : (kind + 1) * HALF]
            for line in range(-(-piece // 128)):
                size = min(128, piece - line * 128)
                one = mine[line : line + 1, 4 * HALF : 4 * HALF + size]
                two = theirs[line : line + 1, 4 * HALF : 4 * HALF + size]
                base = 2 * j * piece + line * 128
                vec[0:1, base : base + size] = jnp.where(is_first, one, two)
                vec[0:1, base + piece : base + piece + size] = jnp.where(is_first, two, one)

        for_plane(dp_size, info, (own, other), place)
        wqkv[...] = weights_three(plain_w[:, : 3 * D])
        wo[...] = weights_three(plain_w[:, 3 * D :])

    xs[:, :SEQ, :] = images[...]
    tokens = xs[...].reshape(GROUP * PAD, D)
    unit, _ = normalize(tokens)
    normed = unit * vec[0:1, :D] + vec[0:1, 2 * D : 3 * D]
    bias = lanes(
        relative(vec[0:1, 4 * D : 5 * D], is_first),
        jnp.zeros((1, D), f32),
        relative(vec[0:1, 5 * D : 6 * D], is_first),
    )
    qkv = dot_one(left_three(normed), wqkv[...], 1, 0) + bias
    qkv_out[...] = qkv.reshape(GROUP, PAD, 3 * D)
    column = lax.broadcasted_iota(jnp.int32, (PAD, 2 * COLUMNS), 1) & (COLUMNS - 1)
    lane = lax.broadcasted_iota(jnp.int32, (PAD, 2 * HEAD_DIM), 1)

    def head_pair(index, carry):
        image = index // (HEADS // 2)
        pair = index % (HEADS // 2)

        def at(base):
            return pl.ds(pl.multiple_of(base + pair * 128, 128), 128)

        query_high, query_low = split(qkv_out[image, :, at(0)] * 0.125)
        key_high, key_low = split(stack_pair(qkv_out[image, :, at(D)]))
        value = split(stack_pair(qkv_out[image, :, at(2 * D)]))
        scores = dot_one(
            lanes(query_high, query_high, query_low), lanes(key_high, key_low, key_high), 1, 1
        )
        scores = jnp.where(column < SEQ, scores, -1e30)
        parts = []
        totals = []
        for half in (scores[:, :COLUMNS], scores[:, COLUMNS:]):
            part = jnp.exp(half - jnp.max(half, axis=-1, keepdims=True))
            parts.append(part)
            totals.append(1.0 / jnp.sum(part, axis=-1, keepdims=True))
        weights_high, weights_low = split(lanes(*parts))
        result = pair_product(weights_high, weights_low, value)
        att[pl.ds(pl.multiple_of(image * PAD, 16), PAD), at(0)] = result * jnp.where(
            lane < HEAD_DIM, totals[0], totals[1]
        )
        return carry

    lax.fori_loop(0, GROUP * HEADS // 2, head_pair, 0, unroll=UNROLL)
    attended = att[...]
    att_out[...] = attended.reshape(GROUP, PAD, D)
    hidden = tokens + nt_wide(attended, wo[: 2 * D]) + vec[0:1, 6 * D : 7 * D]
    hid_out[...] = hidden.reshape(GROUP, PAD, D)

    @pl.when(step == pl.num_programs(0) - 1)
    def _():
        wqkv_out[...] = wqkv[...]
        wo_out[...] = wo[...]
        vec_out[...] = vec[...]


def mlp(dp_size, info, hid, att, cot, *rest):
    count = levels(dp_size)[-1][1]
    own, other, (wo, vec) = rest[:count], rest[count : 2 * count], rest[2 * count : 2 * count + 2]
    block_out, dh_out, datt_out, *more = rest[2 * count + 2 :]
    keeps, sends, more = more[:SLOTS], more[SLOTS : 2 * SLOTS], more[2 * SLOTS :]
    mlp_body(
        dp_size, info, hid, att, cot, own, other, wo, vec, block_out, dh_out, datt_out, keeps, sends, *more
    )


def mlp_body(dp_size, info, hid, att, cot, own, other, wo, vec, block_out, dh_out, datt_out, keeps, sends, gout_out, sums, wup, wdown, cs, gup, gdown, gout, second_lanes, dy_lanes, second_rows, dy_rows, result, dsecond, bias):
    step = pl.program_id(0)
    rows = D // dp_size

    @pl.when(step == 0)
    def _():
        cs[...] = jnp.zeros_like(cs)

        def place(j, mine, theirs):
            here = slice(j * rows, (j + 1) * rows)
            gup[here, :UNITS] = mine[:, :UNITS]
            gup[here, UNITS:] = theirs[:, :UNITS]
            gdown[here, :UNITS] = mine[:, UNITS:]
            gdown[here, UNITS:] = theirs[:, UNITS:]

        for_plane(dp_size, info, (own, other), place)
        wup[...] = weights_three(gup[...])
        wdown[...] = weights_three(gdown[...])
        gup[...] = jnp.zeros_like(gup)
        gdown[...] = jnp.zeros_like(gdown)
        gout[...] = jnp.zeros_like(gout)
        sums[...] = jnp.zeros_like(sums)

    first = (info[0] * pl.num_programs(0) + step) * GROUP
    lives = [jnp.where(first + image < info[2], 1.0, 0.0).astype(f32) for image in range(GROUP)]
    for image in range(GROUP):
        cs[image, :SEQ, :] = cot[image] * lives[image]
    hidden = hid[...].reshape(GROUP * PAD, D)
    unit, rate = normalize(hidden)
    gain = vec[0:1, D : 2 * D]
    second = unit * gain + vec[0:1, 3 * D : 4 * D]
    dy = cs[...].reshape(GROUP * PAD, D)
    bias[...] = relative(vec[0:1, 8 * D :], info[0] == 0)
    second_lanes[...] = left_three(second)
    second_rows[...] = rows_left(second)
    dy_lanes[...] = left_three(dy)
    dy_rows[...] = rows_left(dy)
    result[...] = hidden + vec[0:1, 7 * D : 8 * D]
    dsecond[...] = jnp.zeros_like(dsecond)

    def units(part, carry):
        width = FF // PARTS
        here = pl.ds(pl.multiple_of(part * width, 128), width)
        pre = dot_one(second_lanes[...], wup[:, here], 1, 0) + bias[:, here]
        dact = dot_one(dy_lanes[...], wdown[:, here], 1, 0)
        phi = 0.5 * (1.0 + lax.erf(pre * math.sqrt(0.5)))
        slope = phi + pre * (jnp.exp(-0.5 * pre * pre) * (1.0 / math.sqrt(2.0 * math.pi)))
        act = pre * phi
        dpre = dact * slope
        result[...] += nt_wide(act, wdown[: 2 * D, here])
        gdown[:, here] += dot_one(dy_rows[...], rows_right(act), 0, 0)
        gup[:, here] += dot_one(second_rows[...], rows_right(dpre), 0, 0)
        dsecond[...] += nt_wide(dpre, wup[: 2 * D, here])
        sums[0:1, here] += row_sum(dpre)
        return carry

    lax.fori_loop(0, PARTS, units, 0)
    dsecond = dsecond[...]
    for image in range(GROUP):
        block_out[image] = result[image * PAD : image * PAD + SEQ] * lives[image]
    dh = dy + normalize_back(dsecond, unit, rate, gain)
    dh_out[...] = dh.reshape(GROUP, PAD, D)
    attended = att[...].reshape(GROUP * PAD, D)
    gout[...] += dot_one(rows_left(dh), rows_right(attended), 0, 0)
    datt_out[...] = dot_one(left_three(dh), wo[...], 1, 0).reshape(GROUP, PAD, D)
    sums[1:2, :D] += row_sum(dsecond * unit)
    sums[2:3, :D] += row_sum(dsecond)
    sums[3:4, :D] += row_sum(dh)
    sums[4:5, :D] += row_sum(dy)

    @pl.when(step == pl.num_programs(0) - 1)
    def _():
        gout_out[...] = gout[...]
        pitch = padded_rows(dp_size)
        if pitch != rows:
            for ref in list(keeps) + list(sends):
                ref[...] = jnp.zeros_like(ref)
        upper = levels(dp_size)[:-1]
        low_count = levels(dp_size)[-1][1]
        for low in range(low_count):

            @pl.when((info[1] & (low_count - 1)) == low)
            def _():
                for j in range(dp_size):
                    at = place_of(info[1] ^ j, upper)
                    here = slice(j * rows, (j + 1) * rows)
                    block = j % low_count
                    there = slice(block * pitch, block * pitch + rows)
                    for slot in range(SLOTS):
                        grad = gup if slot < 2 else gdown
                        base = (slot % 2) * D
                        keeps[low ^ slot][at, there, :] = grad[here, base : base + D]
                        sends[low ^ slot][at, there, :] = grad[here, UNITS + base : UNITS + base + D]


def attention_backward(dp_size, last, groups, first, info, images, qkv, datt, dh, wqkv, vec, *rest):
    if last:
        sums_a, gout, grad_in, keep, send, xs, dqkv, grads, sums, flat = rest
    else:
        grad_in, grads_out, sums_out, xs, dqkv, grads, sums = rest
    step = pl.program_id(0)
    rows = D // dp_size

    @pl.when(step == 0)
    def _():
        xs[...] = jnp.zeros_like(xs)
        grads[...] = jnp.zeros_like(grads)
        sums[...] = jnp.zeros_like(sums)

    xs[:, :SEQ, :] = images[...]
    tokens = xs[...].reshape(GROUP * PAD, D)
    unit, rate = normalize(tokens)
    gain = vec[0:1, :D]
    normed = unit * gain + vec[0:1, 2 * D : 3 * D]
    line = lax.broadcasted_iota(jnp.int32, (PAD, 2 * COLUMNS), 0)

    def head_pair(index, carry):
        image = index // (HEADS // 2)
        pair = index % (HEADS // 2)
        part = pl.ds(pl.multiple_of(image * PAD, 16), PAD)

        def at(base):
            return pl.ds(pl.multiple_of(base + pair * 128, 128), 128)

        query = split(stack_pair(qkv[image, :, at(0)] * 0.125))
        grad_o = split(stack_pair(datt[image, :, at(0)]))
        key_high, key_low = split(qkv[image, :, at(D)])
        value_high, value_low = split(qkv[image, :, at(2 * D)])
        scores = dot_one(
            lanes(key_high, key_high, key_low), lanes(query[0], query[1], query[0]), 1, 1
        )
        scores = jnp.where(line < SEQ, scores, -1e30)
        weights = jnp.exp(scores - jnp.max(scores, axis=0, keepdims=True))
        weights = weights * (1.0 / jnp.sum(weights, axis=0, keepdims=True))
        dweights = dot_one(
            lanes(value_high, value_high, value_low), lanes(grad_o[0], grad_o[1], grad_o[0]), 1, 1
        )
        delta = jnp.sum(weights * dweights, axis=0, keepdims=True)
        weights_high, weights_low = split(weights)
        ds_high, ds_low = split(weights * (dweights - delta))
        dqkv[part, at(2 * D)] = pair_product(weights_high, weights_low, grad_o)
        dqkv[part, at(D)] = pair_product(ds_high, ds_low, query)
        both = dot_one(lanes(key_high, key_low), ds_high, 0, 0)
        turned = both[:128] + (both[128:] + dot_one(key_high, ds_low, 0, 0))
        turned = lines(turned[:HEAD_DIM, :COLUMNS], turned[HEAD_DIM:, COLUMNS:])
        dqkv[part, at(0)] = turned.T[:PAD] * 0.125
        return carry

    lax.fori_loop(0, GROUP * HEADS // 2, head_pair, 0, unroll=UNROLL)
    dall = dqkv[...]
    grads[...] += dot_one(rows_left(normed), rows_right(dall), 0, 0)
    dnormed = nt_wide(dall, wqkv[...])
    dx = dh[...].reshape(GROUP * PAD, D) + normalize_back(dnormed, unit, rate, gain)
    for image in range(GROUP):
        grad_in[image] = dx[image * PAD : image * PAD + SEQ]
    sums[0:1, :] += row_sum(dall)
    sums[1:2, :D] += row_sum(dnormed * unit)
    sums[2:3, :D] += row_sum(dnormed)

    @pl.when(step == pl.num_programs(0) - 1)
    def _():
        if not last:
            grads_out[...] = grads[...]
            sums_out[...] = sums[...]
            return
        is_first = info[0] == 0
        total = sums[0:1, :]
        query_sum = total[:, :D]
        value_sum = total[:, 2 * D :]
        flat[0:1, :D] = sums[1:2, :D]
        flat[0:1, D : 2 * D] = sums_a[1:2, :D]
        flat[0:1, 2 * D : 3 * D] = sums[2:3, :D]
        flat[0:1, 3 * D : 4 * D] = sums_a[2:3, :D]
        flat[0:1, 4 * D : 5 * D] = relative(query_sum, is_first)
        flat[0:1, 5 * D : 6 * D] = relative(value_sum, is_first)
        flat[0:1, 6 * D : 7 * D] = sums_a[3:4, :D]
        flat[0:1, 7 * D : 8 * D] = sums_a[4:5, :D]
        flat[0:1, 8 * D :] = relative(sums_a[0:1, :], is_first)
        pitch = padded_rows(dp_size)
        clear = 0 if pitch != rows else 2 * pitch
        blank = jnp.zeros(keep.shape[:2] + (keep.shape[2] - clear, D), f32)
        keep[:, :, clear:, :] = blank
        send[:, :, clear:, :] = blank
        upper = levels(dp_size)[:-1]
        low_count = levels(dp_size)[-1][1]
        low = info[1] & (low_count - 1)
        piece = VEC // (2 * dp_size)
        for j in range(dp_size):
            at = place_of(info[1] ^ j, upper)
            here = slice(j * rows, (j + 1) * rows)
            block = j % low_count
            one = flat[0:1, 2 * j * piece : (2 * j + 1) * piece]
            two = flat[0:1, (2 * j + 1) * piece : (2 * j + 2) * piece]
            keep[low ^ block, at, 2 * pitch : 2 * pitch + 1, :piece] = jnp.where(is_first, one, two)
            send[low ^ block, at, 2 * pitch : 2 * pitch + 1, :piece] = jnp.where(is_first, two, one)
            for slot in range(SLOTS):
                place = block ^ slot
                there = slice((place % 2) * pitch, (place % 2) * pitch + rows)
                lanes = slice((place // 2) * HALF, (place // 2 + 1) * HALF)
                if slot < 3:
                    mine = grads[here, slot * D : slot * D + HALF]
                    theirs = grads[here, slot * D + HALF : (slot + 1) * D]
                else:
                    mine = gout[here, :HALF]
                    theirs = gout[here, HALF:]
                keep[low ^ slot, at, there, lanes] = mine
                send[low ^ slot, at, there, lanes] = theirs


def params():
    return pltpu.CompilerParams(vmem_limit_bytes=VMEM_BYTES, dimension_semantics=("arbitrary",))


def whole(shape):
    return pl.BlockSpec(shape, lambda g, info: (0,) * len(shape), pipeline_mode=ONCE)


def per_group(shape, first=0):
    return pl.BlockSpec((GROUP,) + shape, lambda g, info: (first + g,) + (0,) * len(shape))


def half_images(groups, first=0):
    return pl.BlockSpec((GROUP, SEQ, D), lambda g, info: (info[0] * groups + first + g, 0, 0))


def shaped(*shape):
    return jax.ShapeDtypeStruct(shape, f32)


def call(kernel, groups, in_specs, out_specs, out_shape, scratch, cost, aliases=None):
    return pl.pallas_call(
        kernel,
        grid_spec=pltpu.PrefetchScalarGridSpec(
            num_scalar_prefetch=1,
            grid=(groups,),
            in_specs=in_specs,
            out_specs=out_specs,
            scratch_shapes=[pltpu.VMEM(s, f32) if isinstance(s, tuple) else s for s in scratch],
        ),
        out_shape=out_shape,
        input_output_aliases=aliases or {},
        compiler_params=params(),
        cost_estimate=pl.CostEstimate(flops=cost, bytes_accessed=20 * 2**20, transcendentals=0),
    )


def polynomial(gram):
    pair = split(gram)
    return ns_second * gram + ns_third * nn(pair, pair)


def eye(size):
    line = lax.broadcasted_iota(jnp.int32, (size, size), 0)
    column = lax.broadcasted_iota(jnp.int32, (size, size), 1)
    return jnp.where(line == column, 1.0, 0.0).astype(f32)


def norm_scale(total):
    return 1.0 / (jnp.sqrt(jnp.full((1, 1), total, f32)) + 1e-07)


def gram_part(block, out):
    pair = split(block[...])
    out[...] = nt(pair, pair)


def product(left, right):
    return dot_one(left_three(left), weights_three(right), 1, 0)


def newton(info, gram_ref, own, other, out):
    half = own.shape[0]
    rows = (out.shape[0]) // 2

    @pl.when(info[0] == 0)
    def _():
        gram = gram_ref[...]
        ident = eye(gram.shape[0])
        scale = norm_scale(jnp.sum(gram * ident))
        gram = gram * (scale * scale)
        total = None
        for sweep in range(NS_STEPS):
            left, right = left_three(gram), weights_three(gram)
            mixing = ns_first * ident + ns_second * gram + ns_third * dot_one(left, right, 1, 0)
            mixing_right = weights_three(mixing)
            total = mixing if total is None else dot_one(left_three(total), mixing_right, 1, 0)
            if sweep < NS_STEPS - 1:
                gram = dot_one(left_three(dot_one(left, mixing_right, 1, 0)), mixing_right, 1, 0)
        factor = jnp.where(info[3] >= 2, -2.0, -1.0).astype(f32) * matrix_rate
        out[...] = total[: out.shape[0]] * (scale * factor)

    @pl.when(info[0] != 0)
    def _():
        matrix = lanes(
            lines(own[:, :HALF], own[:, HALF:]),
            lines(other[:, :HALF], other[:, HALF:]),
        )
        matrix = matrix * norm_scale(jnp.sum(matrix * matrix))
        for sweep in range(NS_STEPS):
            high, low = split(matrix)
            square = dot_one(lanes(high, high, low), lanes(high, low, high), 1, 1)
            mixing = ns_second * square + ns_third * product(square, square)
            matrix = ns_first * matrix + dot_one(left_three(mixing), lines(high, low, high), 1, 0)
        matrix = matrix * (-matrix_rate)
        for column in range(2):
            lane = slice(column * HALF, (column + 1) * HALF)
            there = slice(column * rows, (column + 1) * rows)
            if out.shape[1] > D:
                out[there, D:] = jnp.zeros((rows, out.shape[1] - D), f32)
            out[there, :HALF] = matrix[:rows, lane]
            out[there, HALF:D] = matrix[half : half + rows, lane]


def plain(kernel, operands, out_shape, cost):
    return pl.pallas_call(
        kernel,
        in_specs=[
            pl.BlockSpec(memory_space=pltpu.SMEM if x.ndim == 1 else pltpu.VMEM) for x in operands
        ],
        out_specs=jax.tree.map(lambda _: pl.BlockSpec(memory_space=pltpu.VMEM), out_shape),
        out_shape=out_shape,
        compiler_params=pltpu.CompilerParams(vmem_limit_bytes=VMEM_BYTES // 2),
        cost_estimate=pl.CostEstimate(flops=cost, bytes_accessed=5 * 2**20, transcendentals=0),
    )(*operands)


def pass_on():
    pass


def open_plane(count, keep, got, momenta, total):
    total[:count] = (keep[...] + got[...]).reshape(count, D)
    total[count:] = momenta[...]


def close_plane(slots, above, pitch, info, own, *rest):
    parts = rest[: slots - 1]
    total, held_wide, held_small = rest[-3:]
    count = above * SLOTS * pitch
    low = info[3]
    blocks = [own] + list(parts)
    value = blocks[0][:count]
    for block in blocks[1:]:
        value = value + block[:count]
    total[...] = value.reshape(total.shape)
    for s, block in enumerate(blocks):
        at = pl.multiple_of((low ^ s) * pitch, 8)
        held_wide[pl.ds(at, pitch), :] = block[count : count + pitch]
        there = slice((s % 2) * pitch, (s % 2 + 1) * pitch)
        held_small[there, (s // 2) * HALF : (s // 2 + 1) * HALF] = block[count + pitch :, :HALF]


def open_upper(size, slots, count, total, *rest):
    wide_parts = rest[: count - 1]
    held_wide, own = rest[count - 1 : count + 1]
    small_parts = rest[count + 1 : count + slots]
    grads, message = rest[-2:]
    value = total[0]
    for part in wide_parts:
        value = value + part[...]
    grads[...] = value
    moment = momentum_decay * held_wide[...] + value
    wide = value.shape[0]
    small = own[0]
    for part in small_parts:
        small = small + part[...]
    small = small.reshape(size, -1, D)
    for s in range(size):
        message[s, :wide] = moment
        message[s, wide:] = small[s]


def close_upper(size, wide, own, *rest):
    parts = rest[: size - 1]
    held_small = rest[size - 1]
    moments, small, moment = rest[-3:]
    value = own[0, wide:]
    moments[:wide] = own[0, :wide]
    for s, part in enumerate(parts):
        moments[(s + 1) * wide : (s + 2) * wide] = part[:wide]
        value = value + part[wide:]
    small[...] = value
    rows = moment.shape[0]
    moment[...] = momentum_decay * held_small[...] + value[:rows]


def join_small(gram, gram_far, own, *rest):
    parts, (gram_sum, joined) = rest[:-2], rest[-2:]
    gram_sum[...] = gram[...] + gram_far[...]
    rows = own.shape[0]
    joined[:rows] = own[...]
    for s, part in enumerate(parts):
        joined[(s + 1) * rows : (s + 2) * rows] = part[...]


def return_messages(rows, pitch, info, result, result_far, block, grads_a, grads_b, message, steps_a):
    low = info[3]
    is_first = info[0] == 0
    steps_a[...] = product(jnp.where(is_first, result[...], result_far[...]), block[...])
    steps_b = jnp.where(is_first, result_far[2 * pitch :, :D], result[: 2 * pitch, :D])
    for s in range(SLOTS):
        at = pl.multiple_of((low ^ s) * pitch, 8)
        message[s, :, :D] = grads_a[pl.ds(at, pitch), :]
        message[s, :, D : 2 * D] = steps_a[pl.ds(at, pitch), :]
        here = slice((s % 2) * pitch, (s % 2 + 1) * pitch)
        lane = slice((s // 2) * HALF, (s // 2 + 1) * HALF)
        message[s, :, 2 * D : 2 * D + HALF] = grads_b[here, lane]
        message[s, :, 2 * D + HALF :] = steps_b[here, lane]


def finish(rows, info, own, *rest):
    parts, momenta, stack = rest[: SLOTS - 1], rest[SLOTS - 1 : SLOTS + 5], rest[-1]
    outs = rest[SLOTS + 5 : -1]
    low = info[3]
    stack[0] = own[0]
    for s, part in enumerate(parts):
        stack[s + 1] = part[...]
    for slot in range(SLOTS):
        block = stack[low ^ slot]
        grad, step, moment = outs[slot], outs[12 + slot], outs[6 + slot]
        value = block[:rows, 2 * D : 2 * D + HALF]
        grad[...] = value
        moment[...] = momentum_decay * momenta[slot][...] + value
        step[...] = block[:rows, 2 * D + HALF :]
        wide = 4 + slot // 2
        here = slice((slot % 2) * D, (slot % 2 + 1) * D)
        value = block[:rows, :D]
        outs[wide][:, here] = value
        outs[6 + wide][:, here] = momentum_decay * momenta[wide][:, here] + value
        outs[12 + wide][:, here] = block[:rows, D : 2 * D]


def gated(kernel, operands, out_shape, passes, scratch=(), cost=10**6, vmem=VMEM_BYTES // 2, after=()):
    def run(*refs):
        count = len(operands) + len(passes) + len(after)
        outs = refs[count : count + len(out_shape)]
        kernel(*refs[: len(operands)], *outs, *refs[count + len(out_shape) + len(passes) :])

    in_specs = []
    arrays = []
    for x in operands:
        if isinstance(x, tuple):
            x, index = x
            block = (1,) + x.shape[1:]
            in_specs.append(pl.BlockSpec(block, lambda g, n=x.ndim, i=index: (i,) + (0,) * (n - 1)))
        elif x.dtype == jnp.int32:
            in_specs.append(pl.BlockSpec(memory_space=pltpu.SMEM))
        else:
            in_specs.append(pl.BlockSpec(x.shape, lambda g, n=x.ndim: (0,) * n))
        arrays.append(x)
    anywhere = pl.BlockSpec(memory_space=pl.ANY)
    result = pl.pallas_call(
        run,
        grid=(1,),
        in_specs=in_specs + [anywhere] * (len(passes) + len(after)),
        out_specs=[pl.BlockSpec(x.shape, lambda g, n=len(x.shape): (0,) * n) for x in out_shape]
        + [anywhere] * len(passes),
        out_shape=list(out_shape) + [shaped(*x.shape) for x in passes],
        scratch_shapes=list(scratch),
        input_output_aliases={
            len(operands) + i: len(out_shape) + i for i in range(len(passes))
        },
        compiler_params=pltpu.CompilerParams(vmem_limit_bytes=vmem),
        cost_estimate=pl.CostEstimate(flops=cost, bytes_accessed=2**20, transcendentals=0),
    )(*arrays, *passes, *after)
    return result


def pick(stack, index):
    return lax.dynamic_index_in_dim(stack, index, 0, keepdims=False)


def body(
    images,
    image_count,
    cotangent,
    w_query,
    w_key,
    w_value,
    w_out,
    w_up,
    w_down,
    vectors,
    mom_query,
    mom_key,
    mom_value,
    mom_out,
    mom_up,
    mom_down,
    adam_first,
    adam_second,
):
    tp_index = lax.axis_index("tp")
    dp_index = lax.axis_index("dp")
    dp_size = lax.axis_size("dp")
    rows = D // dp_size
    pitch = padded_rows(dp_size)
    piece = vectors.shape[0]
    groups = images.shape[0] // (2 * GROUP)
    slots = groups * GROUP
    is_first = tp_index == 0
    every = levels(dp_size)
    upper, plane = every[:-1], every[-1]
    above = dp_size // plane[1]
    low = dp_index & (plane[1] - 1)
    info = jnp.stack([tp_index, dp_index, image_count[0], low]).astype(jnp.int32)

    vec_tail = jnp.pad(vectors, (0, rows * 128 - piece)).reshape(rows, 128)
    shard_one = jnp.concatenate([w_query, w_key, w_value, w_out.T, vec_tail], axis=1)
    shard_two = jnp.concatenate([w_up, w_down.T], axis=1)
    mom_wide = jnp.concatenate([mom_up, mom_down.T], axis=1)
    mom_small = jnp.concatenate([mom_query, mom_key, mom_value, mom_out.T], axis=1)
    ahead = jnp.pad(mom_wide.reshape(rows, SLOTS, D), ((0, pitch - rows), (0, 0), (0, 0)))
    behind = jnp.pad(mom_small.reshape(rows, SLOTS, HALF), ((0, pitch - rows), (0, 0), (0, D - HALF)))
    mom_slots = jnp.concatenate([ahead, behind], axis=0).transpose(1, 0, 2)
    mom_slots = [pick(mom_slots, low ^ s) for s in range(SLOTS)]

    part_one = gather(shard_one[None], upper, dp_size)
    part_one, mom_slots = tie(part_one, mom_slots)
    got_one = exchange(part_one, plane, dp_size)
    upper_parts = [shard_two[None]]
    for level in upper[:-1]:
        upper_parts = [jnp.concatenate(upper_parts + exchange(upper_parts[0], level, dp_size), axis=0)]
    upper_parts = upper_parts + exchange(upper_parts[0], upper[-1], dp_size)
    got_one, upper_parts = tie(got_one, upper_parts)
    part_two = jnp.concatenate(upper_parts, axis=0)
    own_one = [part_one] + got_one
    other_one = [swap_tp(part) for part in own_one]
    got_two = exchange(part_two, plane, dp_size)
    near_two = swap_tp(part_two)

    qkv, att, hid, wqkv, wo, vec = call(
        functools.partial(attention_forward, dp_size),
        groups,
        [
            half_images(groups),
        ]
        + [whole((above, rows, 4 * HALF + 128))] * (2 * SLOTS),
        [
            per_group((PAD, 3 * D)),
            per_group((PAD, D)),
            per_group((PAD, D)),
            whole((3 * D, 3 * D)),
            whole((3 * D, D)),
            whole((1, VEC)),
        ],
        [
            shaped(slots, PAD, 3 * D),
            shaped(slots, PAD, D),
            shaped(slots, PAD, D),
            jax.ShapeDtypeStruct((3 * D, 3 * D), bf16),
            jax.ShapeDtypeStruct((3 * D, D), bf16),
            shaped(1, VEC),
        ],
        [
            (GROUP, PAD, D),
            (D, 4 * D),
            pltpu.VMEM((3 * D, 3 * D), bf16),
            pltpu.VMEM((3 * D, D), bf16),
            (GROUP * PAD, D),
            (1, VEC),
        ],
        16 * 10**9,
    )(info, images, *own_one, *other_one)

    got_two, hid = tie(got_two, hid)
    own_two = [part_two] + got_two
    other_two = [near_two] + [swap_tp(part) for part in got_two]

    block_own, dh, datt, *slots_a = call(
        functools.partial(mlp, dp_size),
        groups,
        [
            per_group((PAD, D)),
            per_group((PAD, D)),
            half_images(groups),
        ]
        + [whole((above, rows, 2 * UNITS))] * (2 * SLOTS)
        + [
            whole((3 * D, D)),
            whole((1, VEC)),
        ],
        [
            per_group((SEQ, D)),
            per_group((PAD, D)),
            per_group((PAD, D)),
        ]
        + [whole((above, SLOTS * pitch, D))] * (2 * SLOTS)
        + [whole((D, D)), whole((8, FF))],
        [
            shaped(slots, SEQ, D),
            shaped(slots, PAD, D),
            shaped(slots, PAD, D),
        ]
        + [shaped(above, SLOTS * pitch, D)] * (2 * SLOTS)
        + [shaped(D, D), shaped(8, FF)],
        [
            pltpu.VMEM((3 * D, FF), bf16),
            pltpu.VMEM((3 * D, FF), bf16),
            (GROUP, PAD, D),
            (D, FF),
            (D, FF),
            (D, D),
            pltpu.VMEM((GROUP * PAD, 3 * D), bf16),
            pltpu.VMEM((GROUP * PAD, 3 * D), bf16),
            pltpu.VMEM((3 * GROUP * PAD, D), bf16),
            pltpu.VMEM((3 * GROUP * PAD, D), bf16),
            (GROUP * PAD, D),
            (GROUP * PAD, D),
            (1, FF),
        ],
        48 * 10**9,
    )(info, hid, att, cotangent, *own_two, *other_two, wo, vec)

    keep_a, send_a, (gout, sums_a) = slots_a[:SLOTS], slots_a[SLOTS : 2 * SLOTS], slots_a[2 * SLOTS :]
    body_rows = above * SLOTS * pitch
    got_a = [swap_tp(send_a[s]) for s in range(SLOTS)]
    sum_a = [
        gated(
            functools.partial(open_plane, body_rows),
            [keep_a[s], got_a[s], mom_slots[s]],
            [shaped(body_rows + 2 * pitch, D)],
            [],
        )[0]
        for s in range(SLOTS)
    ]
    plane_a = [swap_dp(sum_a[s], s, dp_size) for s in range(1, plane[1])]
    (sums_a,) = gated(pass_on, [], [], [sums_a], after=sum_a)

    def backward(last, first, count, operands, extra_in, before, extra_out_specs, extra_out, extra_scratch):
        return call(
            functools.partial(attention_backward, dp_size, last, groups, first),
            count,
            [
                half_images(groups, first),
                per_group((PAD, 3 * D), first),
                per_group((PAD, D), first),
                per_group((PAD, D), first),
                whole((2 * D, 3 * D)),
                whole((1, VEC)),
            ]
            + [whole(x.shape) for x in extra_in]
            + [pl.BlockSpec(memory_space=pl.ANY)] * len(before),
            [per_group((SEQ, D), first)] + extra_out_specs,
            [shaped(slots, SEQ, D)] + extra_out,
            [(GROUP, PAD, D), (GROUP * PAD, 3 * D), (D, 3 * D), (8, 3 * D)] + extra_scratch,
            10 * 10**9 * count,
            {len(operands) + len(extra_in): 0} if before else {},
        )(*operands, *extra_in, *before)

    small = (SLOTS, above, 2 * pitch + 8, D)
    grad_own, keep_b, send_b = backward(
        True,
        0,
        groups,
        (info, images, qkv, datt, dh, wqkv, vec),
        [sums_a, gout],
        [],
        [whole(small), whole(small)],
        [shaped(*small), shaped(*small)],
        [(1, VEC)],
    )
    total_a, held_wide, held_small, send_b = gated(
        functools.partial(close_plane, SLOTS, above, pitch),
        [info, sum_a[0]] + plane_a,
        [shaped(above, SLOTS * pitch, D), shaped(SLOTS * pitch, D), shaped(2 * pitch, D)],
        [send_b],
    )
    sum_b = (keep_b + swap_tp(send_b)).reshape((SLOTS, above) + small[2:])
    plane_b = [swap_dp(sum_b[s], s, dp_size) for s in range(1, plane[1])]
    total_a = scatter_sum(total_a, upper[1:], dp_size)
    shift, size = upper[0]
    total_a = total_a.reshape(size, SLOTS * pitch, D)
    upper_a = [swap_dp(total_a[s], s << shift, dp_size) for s in range(1, size)]

    def both_halves(mine):
        theirs = swap_tp(mine)
        return jnp.concatenate(
            [jnp.where(is_first, mine, theirs), jnp.where(is_first, theirs, mine)], axis=0
        )

    first_shift, first_size = upper[-1]
    count = above // first_size * (2 * pitch + 8)
    grads_a, message, block_own, grad_own = gated(
        functools.partial(open_upper, first_size, SLOTS, size),
        [(total_a, 0)] + upper_a + [held_wide, (sum_b, 0)] + plane_b,
        [shaped(SLOTS * pitch, D), shaped(first_size, SLOTS * pitch + count, D)],
        [block_own, grad_own],
    )
    block_out = both_halves(block_own)
    input_grad = both_halves(grad_own)
    got = [swap_dp(message[s], s << first_shift, dp_size) for s in range(1, first_size)]
    all_a, total_b, new_b, block_out, input_grad = gated(
        functools.partial(close_upper, first_size, SLOTS * pitch),
        [(message, 0)] + got + [held_small],
        [shaped(first_size * SLOTS * pitch, D), shaped(count, D), shaped(2 * pitch, D)],
        [block_out, input_grad],
    )
    if len(upper) > 1:
        all_a = gather(all_a[None], upper[:-1][::-1], dp_size).reshape(-1, D)
        total_b = scatter_sum(total_b.reshape(-1, 2 * pitch + 8, D), upper[:-1], dp_size)[0]
        new_b = momentum_decay * held_small + total_b[: 2 * pitch]
    grad_vectors = total_b[2 * pitch, :piece]
    grads_b = total_b[: 2 * pitch]

    part_b = gather(new_b[None], upper[:-1], dp_size).reshape(-1, D)
    parts_b = exchange(part_b, upper[-1], dp_size)
    size = all_a.shape[0]
    gram = plain(gram_part, (all_a,), shaped(size, size), 10**9)
    gram = gram + swap_tp(gram)
    gram_half = lax.dynamic_slice_in_dim(gram, tp_index * (size // 2), size // 2, 0)
    gram_half, all_b = gated(
        join_small,
        [gram_half, swap_dp(gram_half, 1, dp_size), part_b] + parts_b,
        [shaped(size // 2, size), shaped(part_b.shape[0] * (len(parts_b) + 1), D)],
        [],
    )
    gram_other = swap_tp(gram_half)
    gram = jnp.concatenate(
        [jnp.where(is_first, gram_half, gram_other), jnp.where(is_first, gram_other, gram_half)]
    )
    (result,) = gated(
        newton,
        [info, gram, all_b, swap_tp(all_b)],
        [shaped(SLOTS * pitch, size)],
        [],
        cost=12 * 10**9,
    )
    result_far = swap_tp(result)

    (message,) = gated(
        functools.partial(return_messages, rows, pitch),
        [info, result, result_far, all_a, grads_a, grads_b],
        [shaped(SLOTS, pitch, 3 * D)],
        [],
        [pltpu.VMEM((SLOTS * pitch, D), f32)],
    )
    got = [swap_dp(message[s], s, dp_size) for s in range(1, plane[1])]
    momenta = [mom_query, mom_key, mom_value, mom_out.T, mom_up, mom_down.T]
    kinds = [shaped(rows, HALF)] * 4 + [shaped(rows, UNITS)] * 2
    results = gated(
        functools.partial(finish, rows),
        [info, (message, 0)] + got + momenta,
        kinds * 3,
        [],
        [pltpu.VMEM((SLOTS, pitch, 3 * D), f32)],
    )

    def in_order(six):
        return (six[0], six[1], six[2], six[3].T, six[4], six[5].T)

    weight_grads = in_order(results[:6])
    new_momenta = in_order(results[6:12])
    steps = in_order(results[12:])

    first_new = adam_beta_one * adam_first + (1.0 - adam_beta_one) * grad_vectors
    second_new = adam_beta_two * adam_second + (1.0 - adam_beta_two) * grad_vectors * grad_vectors
    first_hat = first_new / (1.0 - adam_beta_one**STEP)
    second_hat = second_new / (1.0 - adam_beta_two**STEP)
    vector_update = -adam_rate * (
        first_hat / (jnp.sqrt(second_hat) + adam_eps) + adam_decay * vectors
    )
    return (
        (block_out, input_grad)
        + weight_grads
        + (grad_vectors,)
        + new_momenta
        + steps
        + (first_new, second_new, vector_update)
    )


def solution(mesh):
    image = P("dp", None, None)
    wide = P("dp", "tp")
    tall = P("tp", "dp")
    flat = P(("dp", "tp"))
    six = (wide, wide, wide, tall, wide, tall)
    in_specs = (image, P("dp"), image) + six + (flat,) + six + (flat, flat)
    out_specs = (image, image) + six + (flat,) + six + six + (flat, flat, flat)
    return jax.shard_map(body, mesh=mesh, in_specs=in_specs, out_specs=out_specs, check_vma=False)
```

```python
import functools
import math

import jax
import jax.numpy as jnp
import numpy as np
from jax import lax
from jax.experimental import pallas as pl
from jax.experimental.pallas import tpu as pltpu
from jax.sharding import PartitionSpec as P

D = 384
HEADS = 6
HEAD_DIM = 64
FF = 1536
SEQ = 197
PAD = 208
GROUP = 2
COLUMNS = 256
PARTS = 3
UNROLL = 3
NS_STEPS = 5
STEP = 10
HALF = D // 2
SLOTS = 4
VEC = 4608
UNITS = FF // 2

norm_eps = 1e-06
ns_first = 3.4445
ns_second = -4.775
ns_third = 2.0315
momentum_decay = 0.95
matrix_rate = 1.0
adam_beta_one = 0.9
adam_beta_two = 0.999
adam_rate = 0.05
adam_decay = 0.05
adam_eps = 1e-08
f32 = jnp.float32
bf16 = jnp.bfloat16
VMEM_BYTES = 60 * 2**20
ONCE = pl.Buffered(1)


def split(value):
    high = value.astype(bf16)
    return high, (value - high.astype(f32)).astype(bf16)


def dot_one(left, right, left_dim, right_dim):
    return lax.dot_general(
        left, right, (((left_dim,), (right_dim,)), ((), ())), preferred_element_type=f32
    )


def dot(left, right, left_dim, right_dim):
    left_high, left_low = left if isinstance(left, tuple) else split(left)
    right_high, right_low = right if isinstance(right, tuple) else split(right)
    return dot_one(left_high, right_high, left_dim, right_dim) + (
        dot_one(left_high, right_low, left_dim, right_dim)
        + dot_one(left_low, right_high, left_dim, right_dim)
    )


def nn(left, right):
    return dot(left, right, 1, 0)


def nt(left, right):
    return dot(left, right, 1, 1)


def tn(left, right):
    return dot(left, right, 0, 0)


def levels(dp_size):
    bits = dp_size.bit_length() - 1
    out = []
    shift = 0
    while bits:
        width = min(2, bits)
        out.append((shift, 1 << width))
        shift += width
        bits -= width
    return out[::-1]


def padded_rows(dp_size):
    return -(-(D // dp_size) // 8) * 8


def swap_dp(value, mask, dp_size):
    return lax.ppermute(value, "dp", [(i, i ^ mask) for i in range(dp_size)])


def swap_tp(value):
    return lax.ppermute(value, "tp", [(0, 1), (1, 0)])


def tie(first, second):
    return lax.optimization_barrier((first, second))


def exchange(block, level, dp_size):
    shift, size = level
    return [swap_dp(block, s << shift, dp_size) for s in range(1, size)]


def gather(block, groups, dp_size):
    for level in groups:
        block = jnp.concatenate([block] + exchange(block, level, dp_size), axis=0)
    return block


def place_of(value, groups):
    place = 0
    stride = 1
    for shift, size in groups:
        place = place + ((value >> shift) & (size - 1)) * stride
        stride *= size
    return place


def scatter_sum(value, groups, dp_size):
    for shift, size in groups[::-1]:
        value = value.reshape((size, -1) + value.shape[1:])
        total = value[0]
        for part in [swap_dp(value[s], s << shift, dp_size) for s in range(1, size)]:
            total = total + part
        value = total
    return value


def normalize(rows):
    centre = jnp.sum(rows, axis=-1, keepdims=True) * (1.0 / D)
    offset = rows - centre
    spread = jnp.sum(offset * offset, axis=-1, keepdims=True) * (1.0 / D)
    rate = lax.rsqrt(spread + norm_eps)
    return offset * rate, rate


def normalize_back(grad, unit, rate, gain):
    scaled = grad * gain
    mean_one = jnp.sum(scaled, axis=-1, keepdims=True) * (1.0 / D)
    mean_two = jnp.sum(scaled * unit, axis=-1, keepdims=True) * (1.0 / D)
    return rate * (scaled - mean_one - unit * mean_two)


def row_sum(value):
    return jnp.sum(value, axis=0, keepdims=True)


def lanes(*parts):
    return jnp.concatenate(parts, axis=1)


def lines(*parts):
    return jnp.concatenate(parts, axis=0)


def left_three(value):
    high, low = split(value)
    return lanes(high, high, low)


def weights_three(value):
    high, low = split(value)
    return lines(high, low, high)


def rows_left(value):
    high, low = split(value)
    return lines(high, high, low)


def rows_right(value):
    high, low = split(value)
    return lines(high, low, high)


def nt_wide(left, weights):
    high, low = split(left)
    count = weights.shape[0] // 2
    both = dot_one(high, weights, 1, 1)
    return both[:, :count] + (both[:, count:] + dot_one(low, weights[:count], 1, 1))


def stack_pair(value):
    lane = lax.broadcasted_iota(jnp.int32, value.shape, 1)
    gap = jnp.zeros((COLUMNS - PAD, value.shape[1]), f32)
    return lines(
        jnp.where(lane < HEAD_DIM, value, 0.0), gap, jnp.where(lane < HEAD_DIM, 0.0, value), gap
    )


def pair_product(left_high, left_low, right):
    both = dot_one(left_high, lanes(*right), 1, 0)
    width = right[0].shape[1]
    return both[:, :width] + (both[:, width:] + dot_one(left_low, right[0], 1, 0))


def relative(vec, is_first):
    half = vec.shape[1] // 2
    return jnp.where(is_first, vec, jnp.concatenate([vec[:, half:], vec[:, :half]], axis=1))


def for_plane(dp_size, info, parts, place):
    every = levels(dp_size)
    count = every[-1][1]
    for low in range(count):

        @pl.when((info[1] & (count - 1)) == low)
        def _():
            for j in range(dp_size):
                at = place_of(info[1] ^ j, every[:-1])
                place(j, *[group[(j % count) ^ low][at] for group in parts])


def attention_forward(dp_size, info, images, *rest):
    count = levels(dp_size)[-1][1]
    own, other = rest[:count], rest[count : 2 * count]
    qkv_out, att_out, hid_out, wqkv_out, wo_out, vec_out, xs, plain_w, wqkv, wo, att, vec = rest[2 * count :]
    attention_forward_body(
        dp_size, info, images, own, other, qkv_out, att_out, hid_out, wqkv_out, wo_out, vec_out, xs, plain_w, wqkv, wo, att, vec
    )


def attention_forward_body(dp_size, info, images, own, other, qkv_out, att_out, hid_out, wqkv_out, wo_out, vec_out, xs, plain_w, wqkv, wo, att, vec):
    step = pl.program_id(0)
    rows = D // dp_size
    is_first = info[0] == 0

    @pl.when(step == 0)
    def _():
        xs[...] = jnp.zeros_like(xs)
        piece = VEC // (2 * dp_size)

        def place(j, mine, theirs):
            here = slice(j * rows, (j + 1) * rows)
            for kind in range(4):
                plain_w[here, kind * D : kind * D + HALF] = mine[:, kind * HALF : (kind + 1) * HALF]
                plain_w[here, kind * D + HALF : (kind + 1) * D] = theirs[:, kind * HALF : (kind + 1) * HALF]
            for line in range(-(-piece // 128)):
                size = min(128, piece - line * 128)
                one = mine[line : line + 1, 4 * HALF : 4 * HALF + size]
                two = theirs[line : line + 1, 4 * HALF : 4 * HALF + size]
                base = 2 * j * piece + line * 128
                vec[0:1, base : base + size] = jnp.where(is_first, one, two)
                vec[0:1, base + piece : base + piece + size] = jnp.where(is_first, two, one)

        for_plane(dp_size, info, (own, other), place)
        wqkv[...] = weights_three(plain_w[:, : 3 * D])
        wo[...] = weights_three(plain_w[:, 3 * D :])

    xs[:, :SEQ, :] = images[...]
    tokens = xs[...].reshape(GROUP * PAD, D)
    unit, _ = normalize(tokens)
    normed = unit * vec[0:1, :D] + vec[0:1, 2 * D : 3 * D]
    bias = lanes(
        relative(vec[0:1, 4 * D : 5 * D], is_first),
        jnp.zeros((1, D), f32),
        relative(vec[0:1, 5 * D : 6 * D], is_first),
    )
    qkv = dot_one(left_three(normed), wqkv[...], 1, 0) + bias
    qkv_out[...] = qkv.reshape(GROUP, PAD, 3 * D)
    column = lax.broadcasted_iota(jnp.int32, (PAD, 2 * COLUMNS), 1) & (COLUMNS - 1)
    lane = lax.broadcasted_iota(jnp.int32, (PAD, 2 * HEAD_DIM), 1)

    def head_pair(index, carry):
        image = index // (HEADS // 2)
        pair = index % (HEADS // 2)

        def at(base):
            return pl.ds(pl.multiple_of(base + pair * 128, 128), 128)

        query_high, query_low = split(qkv_out[image, :, at(0)] * 0.125)
        key_high, key_low = split(stack_pair(qkv_out[image, :, at(D)]))
        value = split(stack_pair(qkv_out[image, :, at(2 * D)]))
        scores = dot_one(
            lanes(query_high, query_high, query_low), lanes(key_high, key_low, key_high), 1, 1
        )
        scores = jnp.where(column < SEQ, scores, -1e30)
        parts = []
        totals = []
        for half in (scores[:, :COLUMNS], scores[:, COLUMNS:]):
            part = jnp.exp(half - jnp.max(half, axis=-1, keepdims=True))
            parts.append(part)
            totals.append(1.0 / jnp.sum(part, axis=-1, keepdims=True))
        weights_high, weights_low = split(lanes(*parts))
        result = pair_product(weights_high, weights_low, value)
        att[pl.ds(pl.multiple_of(image * PAD, 16), PAD), at(0)] = result * jnp.where(
            lane < HEAD_DIM, totals[0], totals[1]
        )
        return carry

    lax.fori_loop(0, GROUP * HEADS // 2, head_pair, 0, unroll=True)
    attended = att[...]
    att_out[...] = attended.reshape(GROUP, PAD, D)
    hidden = tokens + nt_wide(attended, wo[: 2 * D]) + vec[0:1, 6 * D : 7 * D]
    hid_out[...] = hidden.reshape(GROUP, PAD, D)

    @pl.when(step == pl.num_programs(0) - 1)
    def _():
        wqkv_out[...] = wqkv[...]
        wo_out[...] = wo[...]
        vec_out[...] = vec[...]


def mlp(dp_size, info, hid, att, cot, *rest):
    count = levels(dp_size)[-1][1]
    own, other, (wo, vec) = rest[:count], rest[count : 2 * count], rest[2 * count : 2 * count + 2]
    block_out, dh_out, datt_out, *more = rest[2 * count + 2 :]
    keeps, sends, more = more[:SLOTS], more[SLOTS : 2 * SLOTS], more[2 * SLOTS :]
    mlp_body(
        dp_size, info, hid, att, cot, own, other, wo, vec, block_out, dh_out, datt_out, keeps, sends, *more
    )


def mlp_body(dp_size, info, hid, att, cot, own, other, wo, vec, block_out, dh_out, datt_out, keeps, sends, gout_out, sums, wup, wdown, cs, gup, gdown, gout, second_lanes, dy_lanes, second_rows, dy_rows, result, dsecond, bias):
    step = pl.program_id(0)
    rows = D // dp_size

    @pl.when(step == 0)
    def _():
        cs[...] = jnp.zeros_like(cs)

        def place(j, mine, theirs):
            here = slice(j * rows, (j + 1) * rows)
            gup[here, :UNITS] = mine[:, :UNITS]
            gup[here, UNITS:] = theirs[:, :UNITS]
            gdown[here, :UNITS] = mine[:, UNITS:]
            gdown[here, UNITS:] = theirs[:, UNITS:]

        for_plane(dp_size, info, (own, other), place)
        wup[...] = weights_three(gup[...])
        wdown[...] = weights_three(gdown[...])
        gup[...] = jnp.zeros_like(gup)
        gdown[...] = jnp.zeros_like(gdown)
        gout[...] = jnp.zeros_like(gout)
        sums[...] = jnp.zeros_like(sums)

    first = (info[0] * pl.num_programs(0) + step) * GROUP
    lives = [jnp.where(first + image < info[2], 1.0, 0.0).astype(f32) for image in range(GROUP)]
    for image in range(GROUP):
        cs[image, :SEQ, :] = cot[image] * lives[image]
    hidden = hid[...].reshape(GROUP * PAD, D)
    unit, rate = normalize(hidden)
    gain = vec[0:1, D : 2 * D]
    second = unit * gain + vec[0:1, 3 * D : 4 * D]
    dy = cs[...].reshape(GROUP * PAD, D)
    bias[...] = relative(vec[0:1, 8 * D :], info[0] == 0)
    second_lanes[...] = left_three(second)
    second_rows[...] = rows_left(second)
    dy_lanes[...] = left_three(dy)
    dy_rows[...] = rows_left(dy)
    result[...] = hidden + vec[0:1, 7 * D : 8 * D]
    dsecond[...] = jnp.zeros_like(dsecond)

    def units(part, carry):
        width = FF // PARTS
        here = pl.ds(pl.multiple_of(part * width, 128), width)
        pre = dot_one(second_lanes[...], wup[:, here], 1, 0) + bias[:, here]
        dact = dot_one(dy_lanes[...], wdown[:, here], 1, 0)
        phi = 0.5 * (1.0 + lax.erf(pre * math.sqrt(0.5)))
        slope = phi + pre * (jnp.exp(-0.5 * pre * pre) * (1.0 / math.sqrt(2.0 * math.pi)))
        act = pre * phi
        dpre = dact * slope
        result[...] += nt_wide(act, wdown[: 2 * D, here])
        gdown[:, here] += dot_one(dy_rows[...], rows_right(act), 0, 0)
        gup[:, here] += dot_one(second_rows[...], rows_right(dpre), 0, 0)
        dsecond[...] += nt_wide(dpre, wup[: 2 * D, here])
        sums[0:1, here] += row_sum(dpre)
        return carry

    lax.fori_loop(0, PARTS, units, 0)
    dsecond = dsecond[...]
    for image in range(GROUP):
        block_out[image] = result[image * PAD : image * PAD + SEQ] * lives[image]
    dh = dy + normalize_back(dsecond, unit, rate, gain)
    dh_out[...] = dh.reshape(GROUP, PAD, D)
    attended = att[...].reshape(GROUP * PAD, D)
    gout[...] += dot_one(rows_left(dh), rows_right(attended), 0, 0)
    datt_out[...] = dot_one(left_three(dh), wo[...], 1, 0).reshape(GROUP, PAD, D)
    sums[1:2, :D] += row_sum(dsecond * unit)
    sums[2:3, :D] += row_sum(dsecond)
    sums[3:4, :D] += row_sum(dh)
    sums[4:5, :D] += row_sum(dy)

    @pl.when(step == pl.num_programs(0) - 1)
    def _():
        gout_out[...] = gout[...]
        pitch = padded_rows(dp_size)
        if pitch != rows:
            for ref in list(keeps) + list(sends):
                ref[...] = jnp.zeros_like(ref)
        upper = levels(dp_size)[:-1]
        low_count = levels(dp_size)[-1][1]
        for low in range(low_count):

            @pl.when((info[1] & (low_count - 1)) == low)
            def _():
                for j in range(dp_size):
                    at = place_of(info[1] ^ j, upper)
                    here = slice(j * rows, (j + 1) * rows)
                    block = j % low_count
                    there = slice(block * pitch, block * pitch + rows)
                    for slot in range(SLOTS):
                        grad = gup if slot < 2 else gdown
                        base = (slot % 2) * D
                        keeps[low ^ slot][at, there, :] = grad[here, base : base + D]
                        sends[low ^ slot][at, there, :] = grad[here, UNITS + base : UNITS + base + D]


def attention_backward(dp_size, last, groups, first, info, images, qkv, datt, dh, wqkv, vec, *rest):
    if last:
        sums_a, gout, grad_in, keep, send, xs, dqkv, grads, sums, flat = rest
    else:
        grad_in, grads_out, sums_out, xs, dqkv, grads, sums = rest
    step = pl.program_id(0)
    rows = D // dp_size

    @pl.when(step == 0)
    def _():
        xs[...] = jnp.zeros_like(xs)
        grads[...] = jnp.zeros_like(grads)
        sums[...] = jnp.zeros_like(sums)

    xs[:, :SEQ, :] = images[...]
    tokens = xs[...].reshape(GROUP * PAD, D)
    unit, rate = normalize(tokens)
    gain = vec[0:1, :D]
    normed = unit * gain + vec[0:1, 2 * D : 3 * D]
    line = lax.broadcasted_iota(jnp.int32, (PAD, 2 * COLUMNS), 0)

    def head_pair(index, carry):
        image = index // (HEADS // 2)
        pair = index % (HEADS // 2)
        part = pl.ds(pl.multiple_of(image * PAD, 16), PAD)

        def at(base):
            return pl.ds(pl.multiple_of(base + pair * 128, 128), 128)

        query = split(stack_pair(qkv[image, :, at(0)] * 0.125))
        grad_o = split(stack_pair(datt[image, :, at(0)]))
        key_high, key_low = split(qkv[image, :, at(D)])
        value_high, value_low = split(qkv[image, :, at(2 * D)])
        scores = dot_one(
            lanes(key_high, key_high, key_low), lanes(query[0], query[1], query[0]), 1, 1
        )
        scores = jnp.where(line < SEQ, scores, -1e30)
        weights = jnp.exp(scores - jnp.max(scores, axis=0, keepdims=True))
        weights = weights * (1.0 / jnp.sum(weights, axis=0, keepdims=True))
        dweights = dot_one(
            lanes(value_high, value_high, value_low), lanes(grad_o[0], grad_o[1], grad_o[0]), 1, 1
        )
        delta = jnp.sum(weights * dweights, axis=0, keepdims=True)
        weights_high, weights_low = split(weights)
        ds_high, ds_low = split(weights * (dweights - delta))
        dqkv[part, at(2 * D)] = pair_product(weights_high, weights_low, grad_o)
        dqkv[part, at(D)] = pair_product(ds_high, ds_low, query)
        both = dot_one(lanes(key_high, key_low), ds_high, 0, 0)
        turned = both[:128] + (both[128:] + dot_one(key_high, ds_low, 0, 0))
        turned = lines(turned[:HEAD_DIM, :COLUMNS], turned[HEAD_DIM:, COLUMNS:])
        dqkv[part, at(0)] = turned.T[:PAD] * 0.125
        return carry

    lax.fori_loop(0, GROUP * HEADS // 2, head_pair, 0, unroll=True)
    dall = dqkv[...]
    grads[...] += dot_one(rows_left(normed), rows_right(dall), 0, 0)
    dnormed = nt_wide(dall, wqkv[...])
    dx = dh[...].reshape(GROUP * PAD, D) + normalize_back(dnormed, unit, rate, gain)
    for image in range(GROUP):
        grad_in[image] = dx[image * PAD : image * PAD + SEQ]
    sums[0:1, :] += row_sum(dall)
    sums[1:2, :D] += row_sum(dnormed * unit)
    sums[2:3, :D] += row_sum(dnormed)

    @pl.when(step == pl.num_programs(0) - 1)
    def _():
        if not last:
            grads_out[...] = grads[...]
            sums_out[...] = sums[...]
            return
        is_first = info[0] == 0
        total = sums[0:1, :]
        query_sum = total[:, :D]
        value_sum = total[:, 2 * D :]
        flat[0:1, :D] = sums[1:2, :D]
        flat[0:1, D : 2 * D] = sums_a[1:2, :D]
        flat[0:1, 2 * D : 3 * D] = sums[2:3, :D]
        flat[0:1, 3 * D : 4 * D] = sums_a[2:3, :D]
        flat[0:1, 4 * D : 5 * D] = relative(query_sum, is_first)
        flat[0:1, 5 * D : 6 * D] = relative(value_sum, is_first)
        flat[0:1, 6 * D : 7 * D] = sums_a[3:4, :D]
        flat[0:1, 7 * D : 8 * D] = sums_a[4:5, :D]
        flat[0:1, 8 * D :] = relative(sums_a[0:1, :], is_first)
        pitch = padded_rows(dp_size)
        clear = 0 if pitch != rows else 2 * pitch
        blank = jnp.zeros(keep.shape[:2] + (keep.shape[2] - clear, D), f32)
        keep[:, :, clear:, :] = blank
        send[:, :, clear:, :] = blank
        upper = levels(dp_size)[:-1]
        low_count = levels(dp_size)[-1][1]
        low = info[1] & (low_count - 1)
        piece = VEC // (2 * dp_size)
        for j in range(dp_size):
            at = place_of(info[1] ^ j, upper)
            here = slice(j * rows, (j + 1) * rows)
            block = j % low_count
            one = flat[0:1, 2 * j * piece : (2 * j + 1) * piece]
            two = flat[0:1, (2 * j + 1) * piece : (2 * j + 2) * piece]
            keep[low ^ block, at, 2 * pitch : 2 * pitch + 1, :piece] = jnp.where(is_first, one, two)
            send[low ^ block, at, 2 * pitch : 2 * pitch + 1, :piece] = jnp.where(is_first, two, one)
            for slot in range(SLOTS):
                place = block ^ slot
                there = slice((place % 2) * pitch, (place % 2) * pitch + rows)
                lanes = slice((place // 2) * HALF, (place // 2 + 1) * HALF)
                if slot < 3:
                    mine = grads[here, slot * D : slot * D + HALF]
                    theirs = grads[here, slot * D + HALF : (slot + 1) * D]
                else:
                    mine = gout[here, :HALF]
                    theirs = gout[here, HALF:]
                keep[low ^ slot, at, there, lanes] = mine
                send[low ^ slot, at, there, lanes] = theirs


def params():
    return pltpu.CompilerParams(vmem_limit_bytes=VMEM_BYTES, dimension_semantics=("arbitrary",))


def whole(shape):
    return pl.BlockSpec(shape, lambda g, info: (0,) * len(shape), pipeline_mode=ONCE)


def per_group(shape, first=0):
    return pl.BlockSpec((GROUP,) + shape, lambda g, info: (first + g,) + (0,) * len(shape))


def half_images(groups, first=0):
    return pl.BlockSpec((GROUP, SEQ, D), lambda g, info: (info[0] * groups + first + g, 0, 0))


def shaped(*shape):
    return jax.ShapeDtypeStruct(shape, f32)


def call(kernel, groups, in_specs, out_specs, out_shape, scratch, cost, aliases=None):
    return pl.pallas_call(
        kernel,
        grid_spec=pltpu.PrefetchScalarGridSpec(
            num_scalar_prefetch=1,
            grid=(groups,),
            in_specs=in_specs,
            out_specs=out_specs,
            scratch_shapes=[pltpu.VMEM(s, f32) if isinstance(s, tuple) else s for s in scratch],
        ),
        out_shape=out_shape,
        input_output_aliases=aliases or {},
        compiler_params=params(),
        cost_estimate=pl.CostEstimate(flops=cost, bytes_accessed=20 * 2**20, transcendentals=0),
    )


def polynomial(gram):
    pair = split(gram)
    return ns_second * gram + ns_third * nn(pair, pair)


def eye(size):
    line = lax.broadcasted_iota(jnp.int32, (size, size), 0)
    column = lax.broadcasted_iota(jnp.int32, (size, size), 1)
    return jnp.where(line == column, 1.0, 0.0).astype(f32)


def norm_scale(total):
    return 1.0 / (jnp.sqrt(jnp.full((1, 1), total, f32)) + 1e-07)


def gram_part(block, out):
    pair = split(block[...])
    out[...] = nt(pair, pair)


def product(left, right):
    return dot_one(left_three(left), weights_three(right), 1, 0)


def newton(info, gram_ref, own, other, out):
    half = own.shape[0]
    rows = (out.shape[0]) // 2

    @pl.when(info[0] == 0)
    def _():
        gram = gram_ref[...]
        ident = eye(gram.shape[0])
        scale = norm_scale(jnp.sum(gram * ident))
        gram = gram * (scale * scale)
        total = None
        for sweep in range(NS_STEPS):
            left, right = left_three(gram), weights_three(gram)
            mixing = ns_first * ident + ns_second * gram + ns_third * dot_one(left, right, 1, 0)
            mixing_right = weights_three(mixing)
            if total is None:
                total = mixing
                inner = dot_one(left, mixing_right, 1, 0)
            elif sweep < NS_STEPS - 1:
                both = dot_one(lines(left, left_three(total)), mixing_right, 1, 0)
                inner, total = both[: gram.shape[0]], both[gram.shape[0] :]
            else:
                total = dot_one(left_three(total[: out.shape[0]]), mixing_right, 1, 0)
            if sweep < NS_STEPS - 1:
                gram = dot_one(left_three(inner), mixing_right, 1, 0)
        factor = jnp.where(info[3] >= 2, -2.0, -1.0).astype(f32) * matrix_rate
        out[...] = total * (scale * factor)

    @pl.when(info[0] != 0)
    def _():
        matrix = lanes(
            lines(own[:, :HALF], own[:, HALF:]),
            lines(other[:, :HALF], other[:, HALF:]),
        )
        matrix = matrix * norm_scale(jnp.sum(matrix * matrix))
        for sweep in range(NS_STEPS):
            high, low = split(matrix)
            square = dot_one(lanes(high, high, low), lanes(high, low, high), 1, 1)
            mixing = ns_second * square + ns_third * product(square, square)
            matrix = ns_first * matrix + dot_one(left_three(mixing), lines(high, low, high), 1, 0)
        matrix = matrix * (-matrix_rate)
        for column in range(2):
            lane = slice(column * HALF, (column + 1) * HALF)
            there = slice(column * rows, (column + 1) * rows)
            if out.shape[1] > D:
                out[there, D:] = jnp.zeros((rows, out.shape[1] - D), f32)
            out[there, :HALF] = matrix[:rows, lane]
            out[there, HALF:D] = matrix[half : half + rows, lane]


def plain(kernel, operands, out_shape, cost):
    return pl.pallas_call(
        kernel,
        in_specs=[
            pl.BlockSpec(memory_space=pltpu.SMEM if x.ndim == 1 else pltpu.VMEM) for x in operands
        ],
        out_specs=jax.tree.map(lambda _: pl.BlockSpec(memory_space=pltpu.VMEM), out_shape),
        out_shape=out_shape,
        compiler_params=pltpu.CompilerParams(vmem_limit_bytes=VMEM_BYTES // 2),
        cost_estimate=pl.CostEstimate(flops=cost, bytes_accessed=5 * 2**20, transcendentals=0),
    )(*operands)


def pass_on():
    pass


def open_plane(count, keep, got, momenta, total):
    total[:count] = (keep[...] + got[...]).reshape(count, D)
    total[count:] = momenta[...]


def close_plane(slots, above, pitch, info, own, *rest):
    parts = rest[: slots - 1]
    total, held_wide, held_small = rest[-3:]
    count = above * SLOTS * pitch
    low = info[3]
    blocks = [own] + list(parts)
    value = blocks[0][:count]
    for block in blocks[1:]:
        value = value + block[:count]
    total[...] = value.reshape(total.shape)
    for s, block in enumerate(blocks):
        at = pl.multiple_of((low ^ s) * pitch, 8)
        held_wide[pl.ds(at, pitch), :] = block[count : count + pitch]
        there = slice((s % 2) * pitch, (s % 2 + 1) * pitch)
        held_small[there, (s // 2) * HALF : (s // 2 + 1) * HALF] = block[count + pitch :, :HALF]


def open_upper(size, slots, count, total, *rest):
    wide_parts = rest[: count - 1]
    held_wide, own = rest[count - 1 : count + 1]
    small_parts = rest[count + 1 : count + slots]
    grads, message = rest[-2:]
    value = total[0]
    for part in wide_parts:
        value = value + part[...]
    grads[...] = value
    moment = momentum_decay * held_wide[...] + value
    wide = value.shape[0]
    small = own[0]
    for part in small_parts:
        small = small + part[...]
    small = small.reshape(size, -1, D)
    for s in range(size):
        message[s, :wide] = moment
        message[s, wide:] = small[s]


def close_upper(size, wide, own, *rest):
    parts = rest[: size - 1]
    held_small = rest[size - 1]
    moments, small, moment = rest[-3:]
    value = own[0, wide:]
    moments[:wide] = own[0, :wide]
    for s, part in enumerate(parts):
        moments[(s + 1) * wide : (s + 2) * wide] = part[:wide]
        value = value + part[wide:]
    small[...] = value
    rows = moment.shape[0]
    moment[...] = momentum_decay * held_small[...] + value[:rows]


def join_small(gram, gram_far, own, *rest):
    parts, (gram_sum, joined) = rest[:-2], rest[-2:]
    gram_sum[...] = gram[...] + gram_far[...]
    rows = own.shape[0]
    joined[:rows] = own[...]
    for s, part in enumerate(parts):
        joined[(s + 1) * rows : (s + 2) * rows] = part[...]


def return_messages(rows, pitch, info, result, result_far, block, grads_a, grads_b, message, steps_a):
    low = info[3]
    is_first = info[0] == 0
    steps_a[...] = product(jnp.where(is_first, result[...], result_far[...]), block[...])
    steps_b = jnp.where(is_first, result_far[2 * pitch :, :D], result[: 2 * pitch, :D])
    for s in range(SLOTS):
        at = pl.multiple_of((low ^ s) * pitch, 8)
        message[s, :, :D] = grads_a[pl.ds(at, pitch), :]
        message[s, :, D : 2 * D] = steps_a[pl.ds(at, pitch), :]
        here = slice((s % 2) * pitch, (s % 2 + 1) * pitch)
        lane = slice((s // 2) * HALF, (s // 2 + 1) * HALF)
        message[s, :, 2 * D : 2 * D + HALF] = grads_b[here, lane]
        message[s, :, 2 * D + HALF :] = steps_b[here, lane]


def finish(rows, info, own, *rest):
    parts, momenta, stack = rest[: SLOTS - 1], rest[SLOTS - 1 : SLOTS + 5], rest[-1]
    outs = rest[SLOTS + 5 : -1]
    low = info[3]
    stack[0] = own[0]
    for s, part in enumerate(parts):
        stack[s + 1] = part[...]
    for slot in range(SLOTS):
        block = stack[low ^ slot]
        grad, step, moment = outs[slot], outs[12 + slot], outs[6 + slot]
        value = block[:rows, 2 * D : 2 * D + HALF]
        grad[...] = value
        moment[...] = momentum_decay * momenta[slot][...] + value
        step[...] = block[:rows, 2 * D + HALF :]
        wide = 4 + slot // 2
        here = slice((slot % 2) * D, (slot % 2 + 1) * D)
        value = block[:rows, :D]
        outs[wide][:, here] = value
        outs[6 + wide][:, here] = momentum_decay * momenta[wide][:, here] + value
        outs[12 + wide][:, here] = block[:rows, D : 2 * D]


def gated(kernel, operands, out_shape, passes, scratch=(), cost=10**6, vmem=VMEM_BYTES // 2, after=()):
    def run(*refs):
        count = len(operands) + len(passes) + len(after)
        outs = refs[count : count + len(out_shape)]
        kernel(*refs[: len(operands)], *outs, *refs[count + len(out_shape) + len(passes) :])

    in_specs = []
    arrays = []
    for x in operands:
        if isinstance(x, tuple):
            x, index = x
            block = (1,) + x.shape[1:]
            in_specs.append(pl.BlockSpec(block, lambda g, n=x.ndim, i=index: (i,) + (0,) * (n - 1)))
        elif x.dtype == jnp.int32:
            in_specs.append(pl.BlockSpec(memory_space=pltpu.SMEM))
        else:
            in_specs.append(pl.BlockSpec(x.shape, lambda g, n=x.ndim: (0,) * n))
        arrays.append(x)
    anywhere = pl.BlockSpec(memory_space=pl.ANY)
    result = pl.pallas_call(
        run,
        grid=(1,),
        in_specs=in_specs + [anywhere] * (len(passes) + len(after)),
        out_specs=[pl.BlockSpec(x.shape, lambda g, n=len(x.shape): (0,) * n) for x in out_shape]
        + [anywhere] * len(passes),
        out_shape=list(out_shape) + [shaped(*x.shape) for x in passes],
        scratch_shapes=list(scratch),
        input_output_aliases={
            len(operands) + i: len(out_shape) + i for i in range(len(passes))
        },
        compiler_params=pltpu.CompilerParams(vmem_limit_bytes=vmem),
        cost_estimate=pl.CostEstimate(flops=cost, bytes_accessed=2**20, transcendentals=0),
    )(*arrays, *passes, *after)
    return result


def pick(stack, index):
    return lax.dynamic_index_in_dim(stack, index, 0, keepdims=False)


def body(
    images,
    image_count,
    cotangent,
    w_query,
    w_key,
    w_value,
    w_out,
    w_up,
    w_down,
    vectors,
    mom_query,
    mom_key,
    mom_value,
    mom_out,
    mom_up,
    mom_down,
    adam_first,
    adam_second,
):
    tp_index = lax.axis_index("tp")
    dp_index = lax.axis_index("dp")
    dp_size = lax.axis_size("dp")
    rows = D // dp_size
    pitch = padded_rows(dp_size)
    piece = vectors.shape[0]
    groups = images.shape[0] // (2 * GROUP)
    slots = groups * GROUP
    is_first = tp_index == 0
    every = levels(dp_size)
    upper, plane = every[:-1], every[-1]
    above = dp_size // plane[1]
    low = dp_index & (plane[1] - 1)
    info = jnp.stack([tp_index, dp_index, image_count[0], low]).astype(jnp.int32)

    vec_tail = jnp.pad(vectors, (0, rows * 128 - piece)).reshape(rows, 128)
    shard_one = jnp.concatenate([w_query, w_key, w_value, w_out.T, vec_tail], axis=1)
    shard_two = jnp.concatenate([w_up, w_down.T], axis=1)
    mom_wide = jnp.concatenate([mom_up, mom_down.T], axis=1)
    mom_small = jnp.concatenate([mom_query, mom_key, mom_value, mom_out.T], axis=1)
    ahead = jnp.pad(mom_wide.reshape(rows, SLOTS, D), ((0, pitch - rows), (0, 0), (0, 0)))
    behind = jnp.pad(mom_small.reshape(rows, SLOTS, HALF), ((0, pitch - rows), (0, 0), (0, D - HALF)))
    mom_slots = jnp.concatenate([ahead, behind], axis=0).transpose(1, 0, 2)
    mom_slots = [pick(mom_slots, low ^ s) for s in range(SLOTS)]

    part_one = gather(shard_one[None], upper, dp_size)
    part_one, mom_slots = tie(part_one, mom_slots)
    got_one = exchange(part_one, plane, dp_size)
    upper_parts = [shard_two[None]]
    for level in upper[:-1]:
        upper_parts = [jnp.concatenate(upper_parts + exchange(upper_parts[0], level, dp_size), axis=0)]
    upper_parts = upper_parts + exchange(upper_parts[0], upper[-1], dp_size)
    got_one, upper_parts = tie(got_one, upper_parts)
    part_two = jnp.concatenate(upper_parts, axis=0)
    own_one = [part_one] + got_one
    other_one = [swap_tp(part) for part in own_one]
    got_two = exchange(part_two, plane, dp_size)
    near_two = swap_tp(part_two)

    qkv, att, hid, wqkv, wo, vec = call(
        functools.partial(attention_forward, dp_size),
        groups,
        [
            half_images(groups),
        ]
        + [whole((above, rows, 4 * HALF + 128))] * (2 * SLOTS),
        [
            per_group((PAD, 3 * D)),
            per_group((PAD, D)),
            per_group((PAD, D)),
            whole((3 * D, 3 * D)),
            whole((3 * D, D)),
            whole((1, VEC)),
        ],
        [
            shaped(slots, PAD, 3 * D),
            shaped(slots, PAD, D),
            shaped(slots, PAD, D),
            jax.ShapeDtypeStruct((3 * D, 3 * D), bf16),
            jax.ShapeDtypeStruct((3 * D, D), bf16),
            shaped(1, VEC),
        ],
        [
            (GROUP, PAD, D),
            (D, 4 * D),
            pltpu.VMEM((3 * D, 3 * D), bf16),
            pltpu.VMEM((3 * D, D), bf16),
            (GROUP * PAD, D),
            (1, VEC),
        ],
        16 * 10**9,
    )(info, images, *own_one, *other_one)

    got_two, hid = tie(got_two, hid)
    own_two = [part_two] + got_two
    other_two = [near_two] + [swap_tp(part) for part in got_two]

    block_own, dh, datt, *slots_a = call(
        functools.partial(mlp, dp_size),
        groups,
        [
            per_group((PAD, D)),
            per_group((PAD, D)),
            half_images(groups),
        ]
        + [whole((above, rows, 2 * UNITS))] * (2 * SLOTS)
        + [
            whole((3 * D, D)),
            whole((1, VEC)),
        ],
        [
            per_group((SEQ, D)),
            per_group((PAD, D)),
            per_group((PAD, D)),
        ]
        + [whole((above, SLOTS * pitch, D))] * (2 * SLOTS)
        + [whole((D, D)), whole((8, FF))],
        [
            shaped(slots, SEQ, D),
            shaped(slots, PAD, D),
            shaped(slots, PAD, D),
        ]
        + [shaped(above, SLOTS * pitch, D)] * (2 * SLOTS)
        + [shaped(D, D), shaped(8, FF)],
        [
            pltpu.VMEM((3 * D, FF), bf16),
            pltpu.VMEM((3 * D, FF), bf16),
            (GROUP, PAD, D),
            (D, FF),
            (D, FF),
            (D, D),
            pltpu.VMEM((GROUP * PAD, 3 * D), bf16),
            pltpu.VMEM((GROUP * PAD, 3 * D), bf16),
            pltpu.VMEM((3 * GROUP * PAD, D), bf16),
            pltpu.VMEM((3 * GROUP * PAD, D), bf16),
            (GROUP * PAD, D),
            (GROUP * PAD, D),
            (1, FF),
        ],
        48 * 10**9,
    )(info, hid, att, cotangent, *own_two, *other_two, wo, vec)

    keep_a, send_a, (gout, sums_a) = slots_a[:SLOTS], slots_a[SLOTS : 2 * SLOTS], slots_a[2 * SLOTS :]
    body_rows = above * SLOTS * pitch
    got_a = [swap_tp(send_a[s]) for s in range(SLOTS)]
    sum_a = [
        gated(
            functools.partial(open_plane, body_rows),
            [keep_a[s], got_a[s], mom_slots[s]],
            [shaped(body_rows + 2 * pitch, D)],
            [],
        )[0]
        for s in range(SLOTS)
    ]
    plane_a = [swap_dp(sum_a[s], s, dp_size) for s in range(1, plane[1])]
    (sums_a,) = gated(pass_on, [], [], [sums_a], after=sum_a)

    def backward(last, first, count, operands, extra_in, before, extra_out_specs, extra_out, extra_scratch):
        return call(
            functools.partial(attention_backward, dp_size, last, groups, first),
            count,
            [
                half_images(groups, first),
                per_group((PAD, 3 * D), first),
                per_group((PAD, D), first),
                per_group((PAD, D), first),
                whole((2 * D, 3 * D)),
                whole((1, VEC)),
            ]
            + [whole(x.shape) for x in extra_in]
            + [pl.BlockSpec(memory_space=pl.ANY)] * len(before),
            [per_group((SEQ, D), first)] + extra_out_specs,
            [shaped(slots, SEQ, D)] + extra_out,
            [(GROUP, PAD, D), (GROUP * PAD, 3 * D), (D, 3 * D), (8, 3 * D)] + extra_scratch,
            10 * 10**9 * count,
            {len(operands) + len(extra_in): 0} if before else {},
        )(*operands, *extra_in, *before)

    small = (SLOTS, above, 2 * pitch + 8, D)
    grad_own, keep_b, send_b = backward(
        True,
        0,
        groups,
        (info, images, qkv, datt, dh, wqkv, vec),
        [sums_a, gout],
        [],
        [whole(small), whole(small)],
        [shaped(*small), shaped(*small)],
        [(1, VEC)],
    )
    (send_b,) = gated(pass_on, [], [], [send_b], after=plane_a)
    total_a, held_wide, held_small = gated(
        functools.partial(close_plane, SLOTS, above, pitch),
        [info, sum_a[0]] + plane_a,
        [shaped(above, SLOTS * pitch, D), shaped(SLOTS * pitch, D), shaped(2 * pitch, D)],
        [],
    )
    sum_b = (keep_b + swap_tp(send_b)).reshape((SLOTS, above) + small[2:])
    plane_b = [swap_dp(sum_b[s], s, dp_size) for s in range(1, plane[1])]
    total_a = scatter_sum(total_a, upper[1:], dp_size)
    shift, size = upper[0]
    total_a = total_a.reshape(size, SLOTS * pitch, D)
    upper_a = [swap_dp(total_a[s], s << shift, dp_size) for s in range(1, size)]

    def both_halves(mine):
        theirs = swap_tp(mine)
        return jnp.concatenate(
            [jnp.where(is_first, mine, theirs), jnp.where(is_first, theirs, mine)], axis=0
        )

    first_shift, first_size = upper[-1]
    count = above // first_size * (2 * pitch + 8)
    grads_a, message, block_own, grad_own = gated(
        functools.partial(open_upper, first_size, SLOTS, size),
        [(total_a, 0)] + upper_a + [held_wide, (sum_b, 0)] + plane_b,
        [shaped(SLOTS * pitch, D), shaped(first_size, SLOTS * pitch + count, D)],
        [block_own, grad_own],
    )
    block_out = both_halves(block_own)
    input_grad = both_halves(grad_own)
    got = [swap_dp(message[s], s << first_shift, dp_size) for s in range(1, first_size)]
    all_a, total_b, new_b, block_out, input_grad = gated(
        functools.partial(close_upper, first_size, SLOTS * pitch),
        [(message, 0)] + got + [held_small],
        [shaped(first_size * SLOTS * pitch, D), shaped(count, D), shaped(2 * pitch, D)],
        [block_out, input_grad],
    )
    if len(upper) > 1:
        all_a = gather(all_a[None], upper[:-1][::-1], dp_size).reshape(-1, D)
        total_b = scatter_sum(total_b.reshape(-1, 2 * pitch + 8, D), upper[:-1], dp_size)[0]
        new_b = momentum_decay * held_small + total_b[: 2 * pitch]
    grad_vectors = total_b[2 * pitch, :piece]
    grads_b = total_b[: 2 * pitch]

    part_b = gather(new_b[None], upper[:-1], dp_size).reshape(-1, D)
    parts_b = exchange(part_b, upper[-1], dp_size)
    size = all_a.shape[0]
    gram = plain(gram_part, (all_a,), shaped(size, size), 10**9)
    gram = gram + swap_tp(gram)
    gram_half = lax.dynamic_slice_in_dim(gram, tp_index * (size // 2), size // 2, 0)
    gram_half, all_b = gated(
        join_small,
        [gram_half, swap_dp(gram_half, 1, dp_size), part_b] + parts_b,
        [shaped(size // 2, size), shaped(part_b.shape[0] * (len(parts_b) + 1), D)],
        [],
    )
    gram_other = swap_tp(gram_half)
    gram = jnp.concatenate(
        [jnp.where(is_first, gram_half, gram_other), jnp.where(is_first, gram_other, gram_half)]
    )
    (result,) = gated(
        newton,
        [info, gram, all_b, swap_tp(all_b)],
        [shaped(SLOTS * pitch, size)],
        [],
        cost=12 * 10**9,
    )
    result_far = swap_tp(result)

    (message,) = gated(
        functools.partial(return_messages, rows, pitch),
        [info, result, result_far, all_a, grads_a, grads_b],
        [shaped(SLOTS, pitch, 3 * D)],
        [],
        [pltpu.VMEM((SLOTS * pitch, D), f32)],
    )
    got = [swap_dp(message[s], s, dp_size) for s in range(1, plane[1])]
    momenta = [mom_query, mom_key, mom_value, mom_out.T, mom_up, mom_down.T]
    kinds = [shaped(rows, HALF)] * 4 + [shaped(rows, UNITS)] * 2
    results = gated(
        functools.partial(finish, rows),
        [info, (message, 0)] + got + momenta,
        kinds * 3,
        [],
        [pltpu.VMEM((SLOTS, pitch, 3 * D), f32)],
    )

    def in_order(six):
        return (six[0], six[1], six[2], six[3].T, six[4], six[5].T)

    weight_grads = in_order(results[:6])
    new_momenta = in_order(results[6:12])
    steps = in_order(results[12:])

    first_new = adam_beta_one * adam_first + (1.0 - adam_beta_one) * grad_vectors
    second_new = adam_beta_two * adam_second + (1.0 - adam_beta_two) * grad_vectors * grad_vectors
    first_hat = first_new / (1.0 - adam_beta_one**STEP)
    second_hat = second_new / (1.0 - adam_beta_two**STEP)
    vector_update = -adam_rate * (
        first_hat / (jnp.sqrt(second_hat) + adam_eps) + adam_decay * vectors
    )
    return (
        (block_out, input_grad)
        + weight_grads
        + (grad_vectors,)
        + new_momenta
        + steps
        + (first_new, second_new, vector_update)
    )


def solution(mesh):
    image = P("dp", None, None)
    wide = P("dp", "tp")
    tall = P("tp", "dp")
    flat = P(("dp", "tp"))
    six = (wide, wide, wide, tall, wide, tall)
    in_specs = (image, P("dp"), image) + six + (flat,) + six + (flat, flat)
    out_specs = (image, image) + six + (flat,) + six + six + (flat, flat, flat)
    return jax.shard_map(body, mesh=mesh, in_specs=in_specs, out_specs=out_specs, check_vma=False)
```

```python
import functools
import math

import jax
import jax.numpy as jnp
import numpy as np
from jax import lax
from jax.experimental import pallas as pl
from jax.experimental.pallas import tpu as pltpu
from jax.sharding import PartitionSpec as P

D = 384
HEADS = 6
HEAD_DIM = 64
FF = 1536
SEQ = 197
PAD = 208
GROUP = 2
COLUMNS = 256
PARTS = 2
UNROLL = 3
NS_STEPS = 5
STEP = 10
HALF = D // 2
SLOTS = 4
VEC = 4608
UNITS = FF // 2

norm_eps = 1e-06
ns_first = 3.4445
ns_second = -4.775
ns_third = 2.0315
momentum_decay = 0.95
matrix_rate = 1.0
adam_beta_one = 0.9
adam_beta_two = 0.999
adam_rate = 0.05
adam_decay = 0.05
adam_eps = 1e-08
f32 = jnp.float32
bf16 = jnp.bfloat16
VMEM_BYTES = 60 * 2**20
ONCE = pl.Buffered(1)


def split(value):
    high = value.astype(bf16)
    return high, (value - high.astype(f32)).astype(bf16)


def dot_one(left, right, left_dim, right_dim):
    return lax.dot_general(
        left, right, (((left_dim,), (right_dim,)), ((), ())), preferred_element_type=f32
    )


def dot(left, right, left_dim, right_dim):
    left_high, left_low = left if isinstance(left, tuple) else split(left)
    right_high, right_low = right if isinstance(right, tuple) else split(right)
    return dot_one(left_high, right_high, left_dim, right_dim) + (
        dot_one(left_high, right_low, left_dim, right_dim)
        + dot_one(left_low, right_high, left_dim, right_dim)
    )


def nn(left, right):
    return dot(left, right, 1, 0)


def nt(left, right):
    return dot(left, right, 1, 1)


def tn(left, right):
    return dot(left, right, 0, 0)


def levels(dp_size):
    bits = dp_size.bit_length() - 1
    out = []
    shift = 0
    while bits:
        width = min(2, bits)
        out.append((shift, 1 << width))
        shift += width
        bits -= width
    return out[::-1]


def padded_rows(dp_size):
    return -(-(D // dp_size) // 8) * 8


def swap_dp(value, mask, dp_size):
    return lax.ppermute(value, "dp", [(i, i ^ mask) for i in range(dp_size)])


def swap_tp(value):
    return lax.ppermute(value, "tp", [(0, 1), (1, 0)])


def tie(first, second):
    return lax.optimization_barrier((first, second))


def exchange(block, level, dp_size):
    shift, size = level
    return [swap_dp(block, s << shift, dp_size) for s in range(1, size)]


def gather(block, groups, dp_size):
    for level in groups:
        block = jnp.concatenate([block] + exchange(block, level, dp_size), axis=0)
    return block


def place_of(value, groups):
    place = 0
    stride = 1
    for shift, size in groups:
        place = place + ((value >> shift) & (size - 1)) * stride
        stride *= size
    return place


def scatter_sum(value, groups, dp_size):
    for shift, size in groups[::-1]:
        value = value.reshape((size, -1) + value.shape[1:])
        total = value[0]
        for part in [swap_dp(value[s], s << shift, dp_size) for s in range(1, size)]:
            total = total + part
        value = total
    return value


def normalize(rows):
    centre = jnp.sum(rows, axis=-1, keepdims=True) * (1.0 / D)
    offset = rows - centre
    spread = jnp.sum(offset * offset, axis=-1, keepdims=True) * (1.0 / D)
    rate = lax.rsqrt(spread + norm_eps)
    return offset * rate, rate


def normalize_back(grad, unit, rate, gain):
    scaled = grad * gain
    mean_one = jnp.sum(scaled, axis=-1, keepdims=True) * (1.0 / D)
    mean_two = jnp.sum(scaled * unit, axis=-1, keepdims=True) * (1.0 / D)
    return rate * (scaled - mean_one - unit * mean_two)


def row_sum(value):
    return jnp.sum(value, axis=0, keepdims=True)


def lanes(*parts):
    return jnp.concatenate(parts, axis=1)


def lines(*parts):
    return jnp.concatenate(parts, axis=0)


def left_three(value):
    high, low = split(value)
    return lanes(high, high, low)


def weights_three(value):
    high, low = split(value)
    return lines(high, low, high)


def rows_left(value):
    high, low = split(value)
    return lines(high, high, low)


def rows_right(value):
    high, low = split(value)
    return lines(high, low, high)


def nt_wide(left, weights):
    high, low = split(left)
    count = weights.shape[0] // 2
    both = dot_one(high, weights, 1, 1)
    return both[:, :count] + (both[:, count:] + dot_one(low, weights[:count], 1, 1))


def stack_pair(value):
    lane = lax.broadcasted_iota(jnp.int32, value.shape, 1)
    gap = jnp.zeros((COLUMNS - PAD, value.shape[1]), f32)
    return lines(
        jnp.where(lane < HEAD_DIM, value, 0.0), gap, jnp.where(lane < HEAD_DIM, 0.0, value), gap
    )


def pair_product(left_high, left_low, right):
    both = dot_one(left_high, lanes(*right), 1, 0)
    width = right[0].shape[1]
    return both[:, :width] + (both[:, width:] + dot_one(left_low, right[0], 1, 0))


def relative(vec, is_first):
    half = vec.shape[1] // 2
    return jnp.where(is_first, vec, jnp.concatenate([vec[:, half:], vec[:, :half]], axis=1))


def for_plane(dp_size, info, parts, place):
    every = levels(dp_size)
    count = every[-1][1]
    for low in range(count):

        @pl.when((info[1] & (count - 1)) == low)
        def _():
            for j in range(dp_size):
                at = place_of(info[1] ^ j, every[:-1])
                place(j, *[group[(j % count) ^ low][at] for group in parts])


def attention_forward(dp_size, info, images, *rest):
    count = levels(dp_size)[-1][1]
    own, other = rest[:count], rest[count : 2 * count]
    qkv_out, att_out, hid_out, wqkv_out, wo_out, vec_out, xs, plain_w, wqkv, wo, att, vec = rest[2 * count :]
    attention_forward_body(
        dp_size, info, images, own, other, qkv_out, att_out, hid_out, wqkv_out, wo_out, vec_out, xs, plain_w, wqkv, wo, att, vec
    )


def attention_forward_body(dp_size, info, images, own, other, qkv_out, att_out, hid_out, wqkv_out, wo_out, vec_out, xs, plain_w, wqkv, wo, att, vec):
    step = pl.program_id(0)
    rows = D // dp_size
    is_first = info[0] == 0

    @pl.when(step == 0)
    def _():
        xs[...] = jnp.zeros_like(xs)
        piece = VEC // (2 * dp_size)

        def place(j, mine, theirs):
            here = slice(j * rows, (j + 1) * rows)
            for kind in range(4):
                plain_w[here, kind * D : kind * D + HALF] = mine[:, kind * HALF : (kind + 1) * HALF]
                plain_w[here, kind * D + HALF : (kind + 1) * D] = theirs[:, kind * HALF : (kind + 1) * HALF]
            for line in range(-(-piece // 128)):
                size = min(128, piece - line * 128)
                one = mine[line : line + 1, 4 * HALF : 4 * HALF + size]
                two = theirs[line : line + 1, 4 * HALF : 4 * HALF + size]
                base = 2 * j * piece + line * 128
                vec[0:1, base : base + size] = jnp.where(is_first, one, two)
                vec[0:1, base + piece : base + piece + size] = jnp.where(is_first, two, one)

        for_plane(dp_size, info, (own, other), place)
        wqkv[...] = weights_three(plain_w[:, : 3 * D])
        wo[...] = weights_three(plain_w[:, 3 * D :])

    xs[:, :SEQ, :] = images[...]
    tokens = xs[...].reshape(GROUP * PAD, D)
    unit, _ = normalize(tokens)
    normed = unit * vec[0:1, :D] + vec[0:1, 2 * D : 3 * D]
    bias = lanes(
        relative(vec[0:1, 4 * D : 5 * D], is_first),
        jnp.zeros((1, D), f32),
        relative(vec[0:1, 5 * D : 6 * D], is_first),
    )
    qkv = dot_one(left_three(normed), wqkv[...], 1, 0) + bias
    qkv_out[...] = qkv.reshape(GROUP, PAD, 3 * D)
    column = lax.broadcasted_iota(jnp.int32, (PAD, 2 * COLUMNS), 1) & (COLUMNS - 1)
    lane = lax.broadcasted_iota(jnp.int32, (PAD, 2 * HEAD_DIM), 1)

    def head_pair(index, carry):
        image = index // (HEADS // 2)
        pair = index % (HEADS // 2)

        def at(base):
            return pl.ds(pl.multiple_of(base + pair * 128, 128), 128)

        query_high, query_low = split(qkv_out[image, :, at(0)] * 0.125)
        key_high, key_low = split(stack_pair(qkv_out[image, :, at(D)]))
        value = split(stack_pair(qkv_out[image, :, at(2 * D)]))
        scores = dot_one(
            lanes(query_high, query_high, query_low), lanes(key_high, key_low, key_high), 1, 1
        )
        scores = jnp.where(column < SEQ, scores, -1e30)
        parts = []
        totals = []
        for half in (scores[:, :COLUMNS], scores[:, COLUMNS:]):
            part = jnp.exp(half - jnp.max(half, axis=-1, keepdims=True))
            parts.append(part)
            totals.append(1.0 / jnp.sum(part, axis=-1, keepdims=True))
        weights_high, weights_low = split(lanes(*parts))
        result = pair_product(weights_high, weights_low, value)
        att[pl.ds(pl.multiple_of(image * PAD, 16), PAD), at(0)] = result * jnp.where(
            lane < HEAD_DIM, totals[0], totals[1]
        )
        return carry

    lax.fori_loop(0, GROUP * HEADS // 2, head_pair, 0, unroll=True)
    attended = att[...]
    att_out[...] = attended.reshape(GROUP, PAD, D)
    hidden = tokens + nt_wide(attended, wo[: 2 * D]) + vec[0:1, 6 * D : 7 * D]
    hid_out[...] = hidden.reshape(GROUP, PAD, D)

    @pl.when(step == pl.num_programs(0) - 1)
    def _():
        wqkv_out[...] = wqkv[...]
        wo_out[...] = wo[...]
        vec_out[...] = vec[...]


def mlp(dp_size, info, hid, att, cot, *rest):
    count = levels(dp_size)[-1][1]
    own, other, (wo, vec) = rest[:count], rest[count : 2 * count], rest[2 * count : 2 * count + 2]
    block_out, dh_out, datt_out, *more = rest[2 * count + 2 :]
    keeps, sends, more = more[:SLOTS], more[SLOTS : 2 * SLOTS], more[2 * SLOTS :]
    mlp_body(
        dp_size, info, hid, att, cot, own, other, wo, vec, block_out, dh_out, datt_out, keeps, sends, *more
    )


def mlp_body(dp_size, info, hid, att, cot, own, other, wo, vec, block_out, dh_out, datt_out, keeps, sends, gout_out, sums, wup, wdown, cs, gup, gdown, gout, second_lanes, dy_lanes, second_rows, dy_rows, result, dsecond, bias):
    step = pl.program_id(0)
    rows = D // dp_size

    @pl.when(step == 0)
    def _():
        cs[...] = jnp.zeros_like(cs)

        def place(j, mine, theirs):
            here = slice(j * rows, (j + 1) * rows)
            gup[here, :UNITS] = mine[:, :UNITS]
            gup[here, UNITS:] = theirs[:, :UNITS]
            gdown[here, :UNITS] = mine[:, UNITS:]
            gdown[here, UNITS:] = theirs[:, UNITS:]

        for_plane(dp_size, info, (own, other), place)
        wup[...] = weights_three(gup[...])
        wdown[...] = weights_three(gdown[...])
        gup[...] = jnp.zeros_like(gup)
        gdown[...] = jnp.zeros_like(gdown)
        gout[...] = jnp.zeros_like(gout)
        sums[...] = jnp.zeros_like(sums)

    first = (info[0] * pl.num_programs(0) + step) * GROUP
    lives = [jnp.where(first + image < info[2], 1.0, 0.0).astype(f32) for image in range(GROUP)]
    for image in range(GROUP):
        cs[image, :SEQ, :] = cot[image] * lives[image]
    hidden = hid[...].reshape(GROUP * PAD, D)
    unit, rate = normalize(hidden)
    gain = vec[0:1, D : 2 * D]
    second = unit * gain + vec[0:1, 3 * D : 4 * D]
    dy = cs[...].reshape(GROUP * PAD, D)
    bias[...] = relative(vec[0:1, 8 * D :], info[0] == 0)
    second_lanes[...] = left_three(second)
    second_rows[...] = rows_left(second)
    dy_lanes[...] = left_three(dy)
    dy_rows[...] = rows_left(dy)
    result[...] = hidden + vec[0:1, 7 * D : 8 * D]
    dsecond[...] = jnp.zeros_like(dsecond)

    def units(part, carry):
        width = FF // PARTS
        here = pl.ds(pl.multiple_of(part * width, 128), width)
        pre = dot_one(second_lanes[...], wup[:, here], 1, 0) + bias[:, here]
        dact = dot_one(dy_lanes[...], wdown[:, here], 1, 0)
        phi = 0.5 * (1.0 + lax.erf(pre * math.sqrt(0.5)))
        slope = phi + pre * (jnp.exp(-0.5 * pre * pre) * (1.0 / math.sqrt(2.0 * math.pi)))
        act = pre * phi
        dpre = dact * slope
        result[...] += nt_wide(act, wdown[: 2 * D, here])
        gdown[:, here] += dot_one(dy_rows[...], rows_right(act), 0, 0)
        gup[:, here] += dot_one(second_rows[...], rows_right(dpre), 0, 0)
        dsecond[...] += nt_wide(dpre, wup[: 2 * D, here])
        sums[0:1, here] += row_sum(dpre)
        return carry

    lax.fori_loop(0, PARTS, units, 0, unroll=True)
    dsecond = dsecond[...]
    for image in range(GROUP):
        block_out[image] = result[image * PAD : image * PAD + SEQ] * lives[image]
    dh = dy + normalize_back(dsecond, unit, rate, gain)
    dh_out[...] = dh.reshape(GROUP, PAD, D)
    attended = att[...].reshape(GROUP * PAD, D)
    gout[...] += dot_one(rows_left(dh), rows_right(attended), 0, 0)
    datt_out[...] = dot_one(left_three(dh), wo[...], 1, 0).reshape(GROUP, PAD, D)
    sums[1:2, :D] += row_sum(dsecond * unit)
    sums[2:3, :D] += row_sum(dsecond)
    sums[3:4, :D] += row_sum(dh)
    sums[4:5, :D] += row_sum(dy)

    @pl.when(step == pl.num_programs(0) - 1)
    def _():
        gout_out[...] = gout[...]
        pitch = padded_rows(dp_size)
        if pitch != rows:
            for ref in list(keeps) + list(sends):
                ref[...] = jnp.zeros_like(ref)
        upper = levels(dp_size)[:-1]
        low_count = levels(dp_size)[-1][1]
        for low in range(low_count):

            @pl.when((info[1] & (low_count - 1)) == low)
            def _():
                for j in range(dp_size):
                    at = place_of(info[1] ^ j, upper)
                    here = slice(j * rows, (j + 1) * rows)
                    block = j % low_count
                    there = slice(block * pitch, block * pitch + rows)
                    for slot in range(SLOTS):
                        grad = gup if slot < 2 else gdown
                        base = (slot % 2) * D
                        keeps[low ^ slot][at, there, :] = grad[here, base : base + D]
                        sends[low ^ slot][at, there, :] = grad[here, UNITS + base : UNITS + base + D]


def attention_backward(dp_size, last, groups, first, info, images, qkv, datt, dh, wqkv, vec, *rest):
    if last:
        sums_a, gout, grad_in, keep, send, xs, dqkv, grads, sums, flat = rest
    else:
        grad_in, grads_out, sums_out, xs, dqkv, grads, sums = rest
    step = pl.program_id(0)
    rows = D // dp_size

    @pl.when(step == 0)
    def _():
        xs[...] = jnp.zeros_like(xs)
        grads[...] = jnp.zeros_like(grads)
        sums[...] = jnp.zeros_like(sums)

    xs[:, :SEQ, :] = images[...]
    tokens = xs[...].reshape(GROUP * PAD, D)
    unit, rate = normalize(tokens)
    gain = vec[0:1, :D]
    normed = unit * gain + vec[0:1, 2 * D : 3 * D]
    line = lax.broadcasted_iota(jnp.int32, (PAD, 2 * COLUMNS), 0)

    def head_pair(index, carry):
        image = index // (HEADS // 2)
        pair = index % (HEADS // 2)
        part = pl.ds(pl.multiple_of(image * PAD, 16), PAD)

        def at(base):
            return pl.ds(pl.multiple_of(base + pair * 128, 128), 128)

        query = split(stack_pair(qkv[image, :, at(0)] * 0.125))
        grad_o = split(stack_pair(datt[image, :, at(0)]))
        key_high, key_low = split(qkv[image, :, at(D)])
        value_high, value_low = split(qkv[image, :, at(2 * D)])
        scores = dot_one(
            lanes(key_high, key_high, key_low), lanes(query[0], query[1], query[0]), 1, 1
        )
        scores = jnp.where(line < SEQ, scores, -1e30)
        weights = jnp.exp(scores - jnp.max(scores, axis=0, keepdims=True))
        weights = weights * (1.0 / jnp.sum(weights, axis=0, keepdims=True))
        dweights = dot_one(
            lanes(value_high, value_high, value_low), lanes(grad_o[0], grad_o[1], grad_o[0]), 1, 1
        )
        delta = jnp.sum(weights * dweights, axis=0, keepdims=True)
        weights_high, weights_low = split(weights)
        ds_high, ds_low = split(weights * (dweights - delta))
        dqkv[part, at(2 * D)] = pair_product(weights_high, weights_low, grad_o)
        dqkv[part, at(D)] = pair_product(ds_high, ds_low, query)
        both = dot_one(lanes(key_high, key_low), ds_high, 0, 0)
        turned = both[:128] + (both[128:] + dot_one(key_high, ds_low, 0, 0))
        turned = lines(turned[:HEAD_DIM, :COLUMNS], turned[HEAD_DIM:, COLUMNS:])
        dqkv[part, at(0)] = turned.T[:PAD] * 0.125
        return carry

    lax.fori_loop(0, GROUP * HEADS // 2, head_pair, 0, unroll=True)
    dall = dqkv[...]
    grads[...] += dot_one(rows_left(normed), rows_right(dall), 0, 0)
    dnormed = nt_wide(dall, wqkv[...])
    dx = dh[...].reshape(GROUP * PAD, D) + normalize_back(dnormed, unit, rate, gain)
    for image in range(GROUP):
        grad_in[image] = dx[image * PAD : image * PAD + SEQ]
    sums[0:1, :] += row_sum(dall)
    sums[1:2, :D] += row_sum(dnormed * unit)
    sums[2:3, :D] += row_sum(dnormed)

    @pl.when(step == pl.num_programs(0) - 1)
    def _():
        if not last:
            grads_out[...] = grads[...]
            sums_out[...] = sums[...]
            return
        is_first = info[0] == 0
        total = sums[0:1, :]
        query_sum = total[:, :D]
        value_sum = total[:, 2 * D :]
        flat[0:1, :D] = sums[1:2, :D]
        flat[0:1, D : 2 * D] = sums_a[1:2, :D]
        flat[0:1, 2 * D : 3 * D] = sums[2:3, :D]
        flat[0:1, 3 * D : 4 * D] = sums_a[2:3, :D]
        flat[0:1, 4 * D : 5 * D] = relative(query_sum, is_first)
        flat[0:1, 5 * D : 6 * D] = relative(value_sum, is_first)
        flat[0:1, 6 * D : 7 * D] = sums_a[3:4, :D]
        flat[0:1, 7 * D : 8 * D] = sums_a[4:5, :D]
        flat[0:1, 8 * D :] = relative(sums_a[0:1, :], is_first)
        pitch = padded_rows(dp_size)
        clear = 0 if pitch != rows else 2 * pitch
        blank = jnp.zeros(keep.shape[:2] + (keep.shape[2] - clear, D), f32)
        keep[:, :, clear:, :] = blank
        send[:, :, clear:, :] = blank
        upper = levels(dp_size)[:-1]
        low_count = levels(dp_size)[-1][1]
        low = info[1] & (low_count - 1)
        piece = VEC // (2 * dp_size)
        for j in range(dp_size):
            at = place_of(info[1] ^ j, upper)
            here = slice(j * rows, (j + 1) * rows)
            block = j % low_count
            one = flat[0:1, 2 * j * piece : (2 * j + 1) * piece]
            two = flat[0:1, (2 * j + 1) * piece : (2 * j + 2) * piece]
            keep[low ^ block, at, 2 * pitch : 2 * pitch + 1, :piece] = jnp.where(is_first, one, two)
            send[low ^ block, at, 2 * pitch : 2 * pitch + 1, :piece] = jnp.where(is_first, two, one)
            for slot in range(SLOTS):
                place = block ^ slot
                there = slice((place % 2) * pitch, (place % 2) * pitch + rows)
                lanes = slice((place // 2) * HALF, (place // 2 + 1) * HALF)
                if slot < 3:
                    mine = grads[here, slot * D : slot * D + HALF]
                    theirs = grads[here, slot * D + HALF : (slot + 1) * D]
                else:
                    mine = gout[here, :HALF]
                    theirs = gout[here, HALF:]
                keep[low ^ slot, at, there, lanes] = mine
                send[low ^ slot, at, there, lanes] = theirs


def params():
    return pltpu.CompilerParams(vmem_limit_bytes=VMEM_BYTES, dimension_semantics=("arbitrary",))


def whole(shape):
    return pl.BlockSpec(shape, lambda g, info: (0,) * len(shape), pipeline_mode=ONCE)


def per_group(shape, first=0):
    return pl.BlockSpec((GROUP,) + shape, lambda g, info: (first + g,) + (0,) * len(shape))


def half_images(groups, first=0):
    return pl.BlockSpec((GROUP, SEQ, D), lambda g, info: (info[0] * groups + first + g, 0, 0))


def shaped(*shape):
    return jax.ShapeDtypeStruct(shape, f32)


def call(kernel, groups, in_specs, out_specs, out_shape, scratch, cost, aliases=None):
    return pl.pallas_call(
        kernel,
        grid_spec=pltpu.PrefetchScalarGridSpec(
            num_scalar_prefetch=1,
            grid=(groups,),
            in_specs=in_specs,
            out_specs=out_specs,
            scratch_shapes=[pltpu.VMEM(s, f32) if isinstance(s, tuple) else s for s in scratch],
        ),
        out_shape=out_shape,
        input_output_aliases=aliases or {},
        compiler_params=params(),
        cost_estimate=pl.CostEstimate(flops=cost, bytes_accessed=20 * 2**20, transcendentals=0),
    )


def polynomial(gram):
    pair = split(gram)
    return ns_second * gram + ns_third * nn(pair, pair)


def eye(size):
    line = lax.broadcasted_iota(jnp.int32, (size, size), 0)
    column = lax.broadcasted_iota(jnp.int32, (size, size), 1)
    return jnp.where(line == column, 1.0, 0.0).astype(f32)


def norm_scale(total):
    return 1.0 / (jnp.sqrt(jnp.full((1, 1), total, f32)) + 1e-07)


def gram_part(block, out):
    pair = split(block[...])
    out[...] = nt(pair, pair)


def product(left, right):
    return dot_one(left_three(left), weights_three(right), 1, 0)


def newton(info, gram_ref, own, other, out):
    half = own.shape[0]
    rows = (out.shape[0]) // 2

    @pl.when(info[0] == 0)
    def _():
        gram = gram_ref[...]
        ident = eye(gram.shape[0])
        scale = norm_scale(jnp.sum(gram * ident))
        gram = gram * (scale * scale)
        total = None
        for sweep in range(NS_STEPS):
            left, right = left_three(gram), weights_three(gram)
            mixing = ns_first * ident + ns_second * gram + ns_third * dot_one(left, right, 1, 0)
            mixing_right = weights_three(mixing)
            if total is None:
                total = mixing
                inner = dot_one(left, mixing_right, 1, 0)
            elif sweep < NS_STEPS - 1:
                both = dot_one(lines(left, left_three(total)), mixing_right, 1, 0)
                inner, total = both[: gram.shape[0]], both[gram.shape[0] :]
            else:
                total = dot_one(left_three(total[: out.shape[0]]), mixing_right, 1, 0)
            if sweep < NS_STEPS - 1:
                gram = dot_one(left_three(inner), mixing_right, 1, 0)
        factor = jnp.where(info[3] >= 2, -2.0, -1.0).astype(f32) * matrix_rate
        out[...] = total * (scale * factor)

    @pl.when(info[0] != 0)
    def _():
        matrix = lanes(
            lines(own[:, :HALF], own[:, HALF:]),
            lines(other[:, :HALF], other[:, HALF:]),
        )
        matrix = matrix * norm_scale(jnp.sum(matrix * matrix))
        for sweep in range(NS_STEPS):
            high, low = split(matrix)
            square = dot_one(lanes(high, high, low), lanes(high, low, high), 1, 1)
            mixing = ns_second * square + ns_third * product(square, square)
            matrix = ns_first * matrix + dot_one(left_three(mixing), lines(high, low, high), 1, 0)
        matrix = matrix * (-matrix_rate)
        for column in range(2):
            lane = slice(column * HALF, (column + 1) * HALF)
            there = slice(column * rows, (column + 1) * rows)
            if out.shape[1] > D:
                out[there, D:] = jnp.zeros((rows, out.shape[1] - D), f32)
            out[there, :HALF] = matrix[:rows, lane]
            out[there, HALF:D] = matrix[half : half + rows, lane]


def plain(kernel, operands, out_shape, cost):
    return pl.pallas_call(
        kernel,
        in_specs=[
            pl.BlockSpec(memory_space=pltpu.SMEM if x.ndim == 1 else pltpu.VMEM) for x in operands
        ],
        out_specs=jax.tree.map(lambda _: pl.BlockSpec(memory_space=pltpu.VMEM), out_shape),
        out_shape=out_shape,
        compiler_params=pltpu.CompilerParams(vmem_limit_bytes=VMEM_BYTES // 2),
        cost_estimate=pl.CostEstimate(flops=cost, bytes_accessed=5 * 2**20, transcendentals=0),
    )(*operands)


def pass_on():
    pass


def open_plane(count, keep, got, momenta, total):
    total[:count] = (keep[...] + got[...]).reshape(count, D)
    total[count:] = momenta[...]


def close_plane(slots, above, pitch, info, own, *rest):
    parts = rest[: slots - 1]
    total, held_wide, held_small = rest[-3:]
    count = above * SLOTS * pitch
    low = info[3]
    blocks = [own] + list(parts)
    value = blocks[0][:count]
    for block in blocks[1:]:
        value = value + block[:count]
    total[...] = value.reshape(total.shape)
    for s, block in enumerate(blocks):
        at = pl.multiple_of((low ^ s) * pitch, 8)
        held_wide[pl.ds(at, pitch), :] = block[count : count + pitch]
        there = slice((s % 2) * pitch, (s % 2 + 1) * pitch)
        held_small[there, (s // 2) * HALF : (s // 2 + 1) * HALF] = block[count + pitch :, :HALF]


def open_upper(size, slots, count, total, *rest):
    wide_parts = rest[: count - 1]
    held_wide, own = rest[count - 1 : count + 1]
    small_parts = rest[count + 1 : count + slots]
    grads, message = rest[-2:]
    value = total[0]
    for part in wide_parts:
        value = value + part[...]
    grads[...] = value
    moment = momentum_decay * held_wide[...] + value
    wide = value.shape[0]
    small = own[0]
    for part in small_parts:
        small = small + part[...]
    small = small.reshape(size, -1, D)
    for s in range(size):
        message[s, :wide] = moment
        message[s, wide:] = small[s]


def close_upper(size, wide, own, *rest):
    parts = rest[: size - 1]
    held_small = rest[size - 1]
    moments, small, moment = rest[-3:]
    value = own[0, wide:]
    moments[:wide] = own[0, :wide]
    for s, part in enumerate(parts):
        moments[(s + 1) * wide : (s + 2) * wide] = part[:wide]
        value = value + part[wide:]
    small[...] = value
    rows = moment.shape[0]
    moment[...] = momentum_decay * held_small[...] + value[:rows]


def join_small(gram, gram_far, own, *rest):
    parts, (gram_sum, joined) = rest[:-2], rest[-2:]
    gram_sum[...] = gram[...] + gram_far[...]
    rows = own.shape[0]
    joined[:rows] = own[...]
    for s, part in enumerate(parts):
        joined[(s + 1) * rows : (s + 2) * rows] = part[...]


def return_messages(rows, pitch, info, result, result_far, block, grads_a, grads_b, message, steps_a):
    low = info[3]
    is_first = info[0] == 0
    steps_a[...] = product(jnp.where(is_first, result[...], result_far[...]), block[...])
    steps_b = jnp.where(is_first, result_far[2 * pitch :, :D], result[: 2 * pitch, :D])
    for s in range(SLOTS):
        at = pl.multiple_of((low ^ s) * pitch, 8)
        message[s, :, :D] = grads_a[pl.ds(at, pitch), :]
        message[s, :, D : 2 * D] = steps_a[pl.ds(at, pitch), :]
        here = slice((s % 2) * pitch, (s % 2 + 1) * pitch)
        lane = slice((s // 2) * HALF, (s // 2 + 1) * HALF)
        message[s, :, 2 * D : 2 * D + HALF] = grads_b[here, lane]
        message[s, :, 2 * D + HALF :] = steps_b[here, lane]


def finish(rows, info, own, *rest):
    parts, momenta, stack = rest[: SLOTS - 1], rest[SLOTS - 1 : SLOTS + 5], rest[-1]
    outs = rest[SLOTS + 5 : -1]
    low = info[3]
    stack[0] = own[0]
    for s, part in enumerate(parts):
        stack[s + 1] = part[...]
    for slot in range(SLOTS):
        block = stack[low ^ slot]
        grad, step, moment = outs[slot], outs[12 + slot], outs[6 + slot]
        value = block[:rows, 2 * D : 2 * D + HALF]
        grad[...] = value
        moment[...] = momentum_decay * momenta[slot][...] + value
        step[...] = block[:rows, 2 * D + HALF :]
        wide = 4 + slot // 2
        here = slice((slot % 2) * D, (slot % 2 + 1) * D)
        value = block[:rows, :D]
        outs[wide][:, here] = value
        outs[6 + wide][:, here] = momentum_decay * momenta[wide][:, here] + value
        outs[12 + wide][:, here] = block[:rows, D : 2 * D]


def gated(kernel, operands, out_shape, passes, scratch=(), cost=10**6, vmem=VMEM_BYTES // 2, after=()):
    def run(*refs):
        count = len(operands) + len(passes) + len(after)
        outs = refs[count : count + len(out_shape)]
        kernel(*refs[: len(operands)], *outs, *refs[count + len(out_shape) + len(passes) :])

    in_specs = []
    arrays = []
    for x in operands:
        if isinstance(x, tuple):
            x, index = x
            block = (1,) + x.shape[1:]
            in_specs.append(pl.BlockSpec(block, lambda g, n=x.ndim, i=index: (i,) + (0,) * (n - 1)))
        elif x.dtype == jnp.int32:
            in_specs.append(pl.BlockSpec(memory_space=pltpu.SMEM))
        else:
            in_specs.append(pl.BlockSpec(x.shape, lambda g, n=x.ndim: (0,) * n))
        arrays.append(x)
    anywhere = pl.BlockSpec(memory_space=pl.ANY)
    result = pl.pallas_call(
        run,
        grid=(1,),
        in_specs=in_specs + [anywhere] * (len(passes) + len(after)),
        out_specs=[pl.BlockSpec(x.shape, lambda g, n=len(x.shape): (0,) * n) for x in out_shape]
        + [anywhere] * len(passes),
        out_shape=list(out_shape) + [shaped(*x.shape) for x in passes],
        scratch_shapes=list(scratch),
        input_output_aliases={
            len(operands) + i: len(out_shape) + i for i in range(len(passes))
        },
        compiler_params=pltpu.CompilerParams(vmem_limit_bytes=vmem),
        cost_estimate=pl.CostEstimate(flops=cost, bytes_accessed=2**20, transcendentals=0),
    )(*arrays, *passes, *after)
    return result


def pick(stack, index):
    return lax.dynamic_index_in_dim(stack, index, 0, keepdims=False)


def body(
    images,
    image_count,
    cotangent,
    w_query,
    w_key,
    w_value,
    w_out,
    w_up,
    w_down,
    vectors,
    mom_query,
    mom_key,
    mom_value,
    mom_out,
    mom_up,
    mom_down,
    adam_first,
    adam_second,
):
    tp_index = lax.axis_index("tp")
    dp_index = lax.axis_index("dp")
    dp_size = lax.axis_size("dp")
    rows = D // dp_size
    pitch = padded_rows(dp_size)
    piece = vectors.shape[0]
    groups = images.shape[0] // (2 * GROUP)
    slots = groups * GROUP
    is_first = tp_index == 0
    every = levels(dp_size)
    upper, plane = every[:-1], every[-1]
    above = dp_size // plane[1]
    low = dp_index & (plane[1] - 1)
    info = jnp.stack([tp_index, dp_index, image_count[0], low]).astype(jnp.int32)

    vec_tail = jnp.pad(vectors, (0, rows * 128 - piece)).reshape(rows, 128)
    shard_one = jnp.concatenate([w_query, w_key, w_value, w_out.T, vec_tail], axis=1)
    shard_two = jnp.concatenate([w_up, w_down.T], axis=1)
    mom_wide = jnp.concatenate([mom_up, mom_down.T], axis=1)
    mom_small = jnp.concatenate([mom_query, mom_key, mom_value, mom_out.T], axis=1)
    ahead = jnp.pad(mom_wide.reshape(rows, SLOTS, D), ((0, pitch - rows), (0, 0), (0, 0)))
    behind = jnp.pad(mom_small.reshape(rows, SLOTS, HALF), ((0, pitch - rows), (0, 0), (0, D - HALF)))
    mom_slots = jnp.concatenate([ahead, behind], axis=0).transpose(1, 0, 2)
    mom_slots = [pick(mom_slots, low ^ s) for s in range(SLOTS)]

    part_one = gather(shard_one[None], upper, dp_size)
    part_one, mom_slots = tie(part_one, mom_slots)
    got_one = exchange(part_one, plane, dp_size)
    upper_parts = [shard_two[None]]
    for level in upper[:-1]:
        upper_parts = [jnp.concatenate(upper_parts + exchange(upper_parts[0], level, dp_size), axis=0)]
    upper_parts = upper_parts + exchange(upper_parts[0], upper[-1], dp_size)
    got_one, upper_parts = tie(got_one, upper_parts)
    part_two = jnp.concatenate(upper_parts, axis=0)
    own_one = [part_one] + got_one
    other_one = [swap_tp(part) for part in own_one]
    got_two = exchange(part_two, plane, dp_size)
    near_two = swap_tp(part_two)

    qkv, att, hid, wqkv, wo, vec = call(
        functools.partial(attention_forward, dp_size),
        groups,
        [
            half_images(groups),
        ]
        + [whole((above, rows, 4 * HALF + 128))] * (2 * SLOTS),
        [
            per_group((PAD, 3 * D)),
            per_group((PAD, D)),
            per_group((PAD, D)),
            whole((3 * D, 3 * D)),
            whole((3 * D, D)),
            whole((1, VEC)),
        ],
        [
            shaped(slots, PAD, 3 * D),
            shaped(slots, PAD, D),
            shaped(slots, PAD, D),
            jax.ShapeDtypeStruct((3 * D, 3 * D), bf16),
            jax.ShapeDtypeStruct((3 * D, D), bf16),
            shaped(1, VEC),
        ],
        [
            (GROUP, PAD, D),
            (D, 4 * D),
            pltpu.VMEM((3 * D, 3 * D), bf16),
            pltpu.VMEM((3 * D, D), bf16),
            (GROUP * PAD, D),
            (1, VEC),
        ],
        16 * 10**9,
    )(info, images, *own_one, *other_one)

    got_two, hid = tie(got_two, hid)
    own_two = [part_two] + got_two
    other_two = [near_two] + [swap_tp(part) for part in got_two]

    block_own, dh, datt, *slots_a = call(
        functools.partial(mlp, dp_size),
        groups,
        [
            per_group((PAD, D)),
            per_group((PAD, D)),
            half_images(groups),
        ]
        + [whole((above, rows, 2 * UNITS))] * (2 * SLOTS)
        + [
            whole((3 * D, D)),
            whole((1, VEC)),
        ],
        [
            per_group((SEQ, D)),
            per_group((PAD, D)),
            per_group((PAD, D)),
        ]
        + [whole((above, SLOTS * pitch, D))] * (2 * SLOTS)
        + [whole((D, D)), whole((8, FF))],
        [
            shaped(slots, SEQ, D),
            shaped(slots, PAD, D),
            shaped(slots, PAD, D),
        ]
        + [shaped(above, SLOTS * pitch, D)] * (2 * SLOTS)
        + [shaped(D, D), shaped(8, FF)],
        [
            pltpu.VMEM((3 * D, FF), bf16),
            pltpu.VMEM((3 * D, FF), bf16),
            (GROUP, PAD, D),
            (D, FF),
            (D, FF),
            (D, D),
            pltpu.VMEM((GROUP * PAD, 3 * D), bf16),
            pltpu.VMEM((GROUP * PAD, 3 * D), bf16),
            pltpu.VMEM((3 * GROUP * PAD, D), bf16),
            pltpu.VMEM((3 * GROUP * PAD, D), bf16),
            (GROUP * PAD, D),
            (GROUP * PAD, D),
            (1, FF),
        ],
        48 * 10**9,
    )(info, hid, att, cotangent, *own_two, *other_two, wo, vec)

    keep_a, send_a, (gout, sums_a) = slots_a[:SLOTS], slots_a[SLOTS : 2 * SLOTS], slots_a[2 * SLOTS :]
    body_rows = above * SLOTS * pitch
    got_a = [swap_tp(send_a[s]) for s in range(SLOTS)]
    sum_a = [
        gated(
            functools.partial(open_plane, body_rows),
            [keep_a[s], got_a[s], mom_slots[s]],
            [shaped(body_rows + 2 * pitch, D)],
            [],
        )[0]
        for s in range(SLOTS)
    ]
    plane_a = [swap_dp(sum_a[s], s, dp_size) for s in range(1, plane[1])]
    (sums_a,) = gated(pass_on, [], [], [sums_a], after=sum_a)

    def backward(last, first, count, operands, extra_in, before, extra_out_specs, extra_out, extra_scratch):
        return call(
            functools.partial(attention_backward, dp_size, last, groups, first),
            count,
            [
                half_images(groups, first),
                per_group((PAD, 3 * D), first),
                per_group((PAD, D), first),
                per_group((PAD, D), first),
                whole((2 * D, 3 * D)),
                whole((1, VEC)),
            ]
            + [whole(x.shape) for x in extra_in]
            + [pl.BlockSpec(memory_space=pl.ANY)] * len(before),
            [per_group((SEQ, D), first)] + extra_out_specs,
            [shaped(slots, SEQ, D)] + extra_out,
            [(GROUP, PAD, D), (GROUP * PAD, 3 * D), (D, 3 * D), (8, 3 * D)] + extra_scratch,
            10 * 10**9 * count,
            {len(operands) + len(extra_in): 0} if before else {},
        )(*operands, *extra_in, *before)

    small = (SLOTS, above, 2 * pitch + 8, D)
    grad_own, keep_b, send_b = backward(
        True,
        0,
        groups,
        (info, images, qkv, datt, dh, wqkv, vec),
        [sums_a, gout],
        [],
        [whole(small), whole(small)],
        [shaped(*small), shaped(*small)],
        [(1, VEC)],
    )
    (send_b,) = gated(pass_on, [], [], [send_b], after=plane_a)
    total_a, held_wide, held_small = gated(
        functools.partial(close_plane, SLOTS, above, pitch),
        [info, sum_a[0]] + plane_a,
        [shaped(above, SLOTS * pitch, D), shaped(SLOTS * pitch, D), shaped(2 * pitch, D)],
        [],
    )
    sum_b = (keep_b + swap_tp(send_b)).reshape((SLOTS, above) + small[2:])
    plane_b = [swap_dp(sum_b[s], s, dp_size) for s in range(1, plane[1])]
    total_a = scatter_sum(total_a, upper[1:], dp_size)
    shift, size = upper[0]
    total_a = total_a.reshape(size, SLOTS * pitch, D)
    upper_a = [swap_dp(total_a[s], s << shift, dp_size) for s in range(1, size)]

    def both_halves(mine):
        theirs = swap_tp(mine)
        return jnp.concatenate(
            [jnp.where(is_first, mine, theirs), jnp.where(is_first, theirs, mine)], axis=0
        )

    first_shift, first_size = upper[-1]
    count = above // first_size * (2 * pitch + 8)
    grads_a, message, block_own, grad_own = gated(
        functools.partial(open_upper, first_size, SLOTS, size),
        [(total_a, 0)] + upper_a + [held_wide, (sum_b, 0)] + plane_b,
        [shaped(SLOTS * pitch, D), shaped(first_size, SLOTS * pitch + count, D)],
        [block_own, grad_own],
    )
    block_out = both_halves(block_own)
    input_grad = both_halves(grad_own)
    got = [swap_dp(message[s], s << first_shift, dp_size) for s in range(1, first_size)]
    all_a, total_b, new_b, block_out, input_grad = gated(
        functools.partial(close_upper, first_size, SLOTS * pitch),
        [(message, 0)] + got + [held_small],
        [shaped(first_size * SLOTS * pitch, D), shaped(count, D), shaped(2 * pitch, D)],
        [block_out, input_grad],
    )
    if len(upper) > 1:
        all_a = gather(all_a[None], upper[:-1][::-1], dp_size).reshape(-1, D)
        total_b = scatter_sum(total_b.reshape(-1, 2 * pitch + 8, D), upper[:-1], dp_size)[0]
        new_b = momentum_decay * held_small + total_b[: 2 * pitch]
    grad_vectors = total_b[2 * pitch, :piece]
    grads_b = total_b[: 2 * pitch]

    part_b = gather(new_b[None], upper[:-1], dp_size).reshape(-1, D)
    parts_b = exchange(part_b, upper[-1], dp_size)
    size = all_a.shape[0]
    gram = plain(gram_part, (all_a,), shaped(size, size), 10**9)
    gram = gram + swap_tp(gram)
    gram_half = lax.dynamic_slice_in_dim(gram, tp_index * (size // 2), size // 2, 0)
    gram_half, all_b = gated(
        join_small,
        [gram_half, swap_dp(gram_half, 1, dp_size), part_b] + parts_b,
        [shaped(size // 2, size), shaped(part_b.shape[0] * (len(parts_b) + 1), D)],
        [],
    )
    gram_other = swap_tp(gram_half)
    gram = jnp.concatenate(
        [jnp.where(is_first, gram_half, gram_other), jnp.where(is_first, gram_other, gram_half)]
    )
    (result,) = gated(
        newton,
        [info, gram, all_b, swap_tp(all_b)],
        [shaped(SLOTS * pitch, size)],
        [],
        cost=12 * 10**9,
    )
    result_far = swap_tp(result)

    (message,) = gated(
        functools.partial(return_messages, rows, pitch),
        [info, result, result_far, all_a, grads_a, grads_b],
        [shaped(SLOTS, pitch, 3 * D)],
        [],
        [pltpu.VMEM((SLOTS * pitch, D), f32)],
    )
    got = [swap_dp(message[s], s, dp_size) for s in range(1, plane[1])]
    momenta = [mom_query, mom_key, mom_value, mom_out.T, mom_up, mom_down.T]
    kinds = [shaped(rows, HALF)] * 4 + [shaped(rows, UNITS)] * 2
    results = gated(
        functools.partial(finish, rows),
        [info, (message, 0)] + got + momenta,
        kinds * 3,
        [],
        [pltpu.VMEM((SLOTS, pitch, 3 * D), f32)],
    )

    def in_order(six):
        return (six[0], six[1], six[2], six[3].T, six[4], six[5].T)

    weight_grads = in_order(results[:6])
    new_momenta = in_order(results[6:12])
    steps = in_order(results[12:])

    first_new = adam_beta_one * adam_first + (1.0 - adam_beta_one) * grad_vectors
    second_new = adam_beta_two * adam_second + (1.0 - adam_beta_two) * grad_vectors * grad_vectors
    first_hat = first_new / (1.0 - adam_beta_one**STEP)
    second_hat = second_new / (1.0 - adam_beta_two**STEP)
    vector_update = -adam_rate * (
        first_hat / (jnp.sqrt(second_hat) + adam_eps) + adam_decay * vectors
    )
    return (
        (block_out, input_grad)
        + weight_grads
        + (grad_vectors,)
        + new_momenta
        + steps
        + (first_new, second_new, vector_update)
    )


def solution(mesh):
    image = P("dp", None, None)
    wide = P("dp", "tp")
    tall = P("tp", "dp")
    flat = P(("dp", "tp"))
    six = (wide, wide, wide, tall, wide, tall)
    in_specs = (image, P("dp"), image) + six + (flat,) + six + (flat, flat)
    out_specs = (image, image) + six + (flat,) + six + six + (flat, flat, flat)
    return jax.shard_map(body, mesh=mesh, in_specs=in_specs, out_specs=out_specs, check_vma=False)
```
